32 devices in a mesh: group: 2 (over y), expert: 4 (over z), tensor: 4 (over x, core).
Axes of the slice: x: 2, y: 2, z: 4, core: 2. Of those that a mesh axis runs over, the one named last changes fastest.
Arguments:
- tokens: bfloat16 [768, 3584], P(('group', 'expert'), 'tensor'), parts along dimension 0, may hold values from -6 to 6
- expert_ids: int32 [768, 2], P(('group', 'expert')), parts along dimension 0, may hold values from 0 to 3, all different within a row
- weight_codes: int32 [768, 2], P(('group', 'expert')), parts along dimension 0, may hold values from 1 to 8
- up_weight: bfloat16 [4, 3584, 2432], P('expert', None, 'tensor'), may hold values from -0.09375 to 0.09375
- down_weight: bfloat16 [4, 2432, 3584], P('expert', 'tensor'), may hold values from -0.125 to 0.125
Outputs:
- mixed: bfloat16 [768, 3584], P(('group', 'expert'), 'tensor'), parts along dimension 0
The draws below stay inside these ranges and needn't reach their ends.
There are 2 independent parts, one for each index of `group`. The reference program is written for one: setup_inputs(seed, part) draws one part's arguments, and reference() takes and returns one part's arrays. A program takes and returns all parts, laid end to end along the dimension named above; an argument that names none is the same for every part. Nothing has to cross between parts.
Inputs may be any that keep to these rules, and one draw needn't show every extreme that they name: `expert_ids`: the two experts of a token differ.
All inputs are finite; a program needn't handle non-finite values.
Results may differ from the reference program's by a relative error of at most 0.012.
Values may be sent and summed in bfloat16 or wider, within the bound.
No kernel may reach another device: no remote copies, remote signals or barrier semaphores. Data moves between devices by JAX's collectives and lax.ppermute only.
A program may use at most 64 MiB of HBM per device.

```python
import jax
import jax.numpy as jnp
from jax import lax

D = 3584
FF = 2432
TOK_DEV = 96
EXPERTS = 4
TOKENS = 384
CAP = 96
SLOTS = 384
FF_PART = 608
N_TENSOR = 4


def place_ends(values, stream_key, smallest, largest):
    longest = values.shape.index(max(values.shape))
    spots = []
    for shift in (0, 1):
        where = [jax.random.randint(jax.random.fold_in(stream_key, axis), (), 0, length) for axis, length in enumerate(values.shape)]
        where[longest] = (where[longest] + shift) % values.shape[longest]
        spots.append(tuple(where))
    return values.at[spots[0]].set(smallest).at[spots[1]].set(largest)


def block_scale(stream_key, extent, shards, smallest, largest):
    level = 1.0
    for position, blocks in shards:
        steps = jax.random.uniform(jax.random.fold_in(jax.random.fold_in(stream_key, 6), position), (blocks,), jnp.float32, smallest / len(shards), largest / len(shards))
        level = level * jnp.repeat(jnp.exp(steps), extent[position] // blocks).reshape((-1,) + (1,) * (len(extent) - 1 - position))
    return level


def picks_of(rng, rows, amount, top, lift):
    sequence = jax.random.permutation(jax.random.fold_in(rng, 1), amount)
    pull = sequence
    for power in range(3):
        pull = pull * pull // amount
    pull = pull * lift // amount
    lots = jax.random.randint(jax.random.fold_in(rng, 2), (rows, amount), 0, 4096) + pull
    holders = jax.random.permutation(jax.random.fold_in(rng, 3), rows)[jnp.arange(amount) % rows]
    lots = jnp.where(jnp.arange(rows)[:, None] == holders[None, :], 1 << 14, lots)
    priority = lots * amount + jnp.arange(amount)
    return lax.top_k(priority.astype(jnp.int32), top)[1].astype(jnp.int32)


def normal_values(own_key, dims, deviation, limit, split=(), kind=jnp.bfloat16):
    entries = deviation * jax.random.normal(own_key, dims, jnp.float32)
    if split:
        entries = entries * block_scale(own_key, dims, split, -0.22, 0.18)
    return jnp.clip(entries, -limit, limit).astype(kind)


def setup_inputs(seed: int = 0, part: int = 0) -> dict:
    streams_of = jax.random.split(jax.random.key(seed), 6)
    part_splits = jax.random.split(jax.random.fold_in(streams_of[5], part), 6)
    return {
        "tokens": normal_values(part_splits[0], (TOKENS, D), 1.0, 6.0, ((0, 4), (1, 4))),
        "expert_ids": picks_of(part_splits[1], TOKENS, EXPERTS, 2, 8192),
        "weight_codes": place_ends(jax.random.randint(part_splits[2], (TOKENS, 2), 1, 9), jax.random.fold_in(part_splits[2], 1), 1, 8).astype(jnp.int32),
        "up_weight": normal_values(streams_of[3], (EXPERTS, D, FF), D ** -0.5, 0.09375, ((0, 4), (2, 4))),
        "down_weight": normal_values(streams_of[4], (EXPERTS, FF, D), FF ** -0.5, 0.125, ((0, 4), (1, 4))),
    }


def reference(tokens, expert_ids, weight_codes, up_weight, down_weight):
    blocks = TOKENS // TOK_DEV
    flat_ids = expert_ids.reshape(blocks, TOK_DEV * 2)
    onehot = (flat_ids[:, :, None] == jnp.arange(EXPERTS, dtype=jnp.int32)[None, None, :]).astype(jnp.int32)
    prior = jnp.cumsum(onehot, axis=1) - onehot
    slot = jnp.sum(prior * onehot, axis=2)
    target = jnp.where(slot < CAP, flat_ids * CAP + slot, -1)
    select = (jnp.arange(SLOTS, dtype=jnp.int32)[None, :, None] == target[:, None, :]).astype(jnp.float32)
    repeated = jnp.repeat(tokens.reshape(blocks, TOK_DEV, D), 2, axis=1).astype(jnp.float32)
    dispatched = jnp.einsum("bsa,bad->bsd", select, repeated).astype(jnp.bfloat16)
    per_expert = dispatched.reshape(blocks, EXPERTS, CAP, D).transpose(1, 0, 2, 3).reshape(EXPERTS, blocks * CAP, D)

    def one_expert(index):
        rows = per_expert[index]
        lifted = jnp.dot(rows, up_weight[index], preferred_element_type=jnp.float32)
        hidden = jax.nn.silu(lifted).astype(jnp.bfloat16)
        total = jnp.zeros((rows.shape[0], D), jnp.float32)
        for part in range(N_TENSOR):
            term = jnp.dot(hidden[:, part * FF_PART:(part + 1) * FF_PART],
                           down_weight[index, part * FF_PART:(part + 1) * FF_PART, :],
                           preferred_element_type=jnp.float32).astype(jnp.bfloat16)
            term = lax.optimization_barrier(term)
            total = total + term.astype(jnp.float32)
        return total.astype(jnp.bfloat16)

    expert_out = lax.map(one_expert, jnp.arange(EXPERTS, dtype=jnp.int32))
    back = expert_out.reshape(EXPERTS, blocks, CAP, D).transpose(1, 0, 2, 3).reshape(blocks, SLOTS, D)
    picked = jnp.einsum("bsa,bsd->bad", select, back.astype(jnp.float32)).reshape(blocks, TOK_DEV, 2, D)
    codes = weight_codes.astype(jnp.float32).reshape(blocks, TOK_DEV, 2)
    weight = codes / jnp.sum(codes, axis=2, keepdims=True)
    mixed = jnp.sum(weight[:, :, :, None] * picked, axis=2)
    return mixed.reshape(TOKENS, D).astype(jnp.bfloat16)
```

```python
import jax
import jax.numpy as jnp
from jax import lax
from jax.sharding import PartitionSpec as P


def kept_weights(expert_ids, weight_codes, experts_n, capacity):
    rows = expert_ids.shape[0]
    experts = jnp.arange(experts_n, dtype=jnp.int32)
    chosen = expert_ids[:, :, None] == experts[None, None, :]
    counts = jnp.sum(chosen.astype(jnp.float32), axis=1)
    earlier = (
        jnp.arange(rows, dtype=jnp.int32)[:, None] > jnp.arange(rows, dtype=jnp.int32)[None, :]
    ).astype(jnp.float32)
    before = jnp.dot(earlier, counts, preferred_element_type=jnp.float32)
    codes = weight_codes.astype(jnp.float32)
    weight = codes / jnp.sum(codes, axis=1, keepdims=True)
    first = jnp.where(chosen[:, 0] & (before < capacity), weight[:, 0:1], 0.0)
    slot = before + chosen[:, 0].astype(jnp.float32)
    second = jnp.where(chosen[:, 1] & (slot < capacity), weight[:, 1:2], 0.0)
    return first + second


def whole_blocks(tokens, expert_ids, weight_codes, up_local, down_local, capacity):
    rows = tokens.shape[0]
    experts_n = lax.axis_size("expert")
    weight = kept_weights(expert_ids, weight_codes, experts_n, capacity)
    weight = lax.all_gather(weight, "expert", axis=0, tiled=True)
    column = lax.dynamic_slice_in_dim(weight, lax.axis_index("expert"), 1, 1)
    features = lax.all_gather(tokens, "expert", axis=0, tiled=True)
    features = lax.all_gather(features, "tensor", axis=1, tiled=True)
    lifted = jnp.dot(features, up_local, preferred_element_type=jnp.float32)
    hidden = jax.nn.silu(lifted).astype(jnp.bfloat16)
    partial_out = jnp.dot(hidden, down_local, preferred_element_type=jnp.float32)
    partial_out = (partial_out * column).astype(jnp.bfloat16)
    total = lax.psum_scatter(partial_out, "tensor", scatter_dimension=1, tiled=True)
    return lax.psum_scatter(total, "expert", scatter_dimension=0, tiled=True)


def slotted(tokens, expert_ids, weight_codes, up_local, down_local, capacity):
    rows, share_width = tokens.shape
    experts_n = lax.axis_size("expert")
    slots_n = experts_n * capacity
    flat_ids = expert_ids.reshape(rows * 2)
    onehot = (flat_ids[:, None] == jnp.arange(experts_n, dtype=jnp.int32)[None, :]).astype(
        jnp.int32
    )
    prior = jnp.cumsum(onehot, axis=0) - onehot
    slot = jnp.sum(prior * onehot, axis=1)
    target = jnp.where(slot < capacity, flat_ids * capacity + slot, -1)
    select = (jnp.arange(slots_n, dtype=jnp.int32)[:, None] == target[None, :]).astype(jnp.bfloat16)
    select = select.reshape(slots_n, rows, 2)
    gather_mat = jnp.sum(select, axis=2)
    sending = jnp.dot(gather_mat, tokens, preferred_element_type=jnp.float32).astype(jnp.bfloat16)
    sending = sending.reshape(experts_n, capacity, share_width)
    received = lax.all_to_all(sending, "expert", split_axis=0, concat_axis=0, tiled=True)
    received = received.reshape(slots_n, share_width)
    received = lax.all_gather(received, "tensor", axis=1, tiled=True)
    lifted = jnp.dot(received, up_local, preferred_element_type=jnp.float32)
    hidden = jax.nn.silu(lifted).astype(jnp.bfloat16)
    partial_out = jnp.dot(hidden, down_local, preferred_element_type=jnp.float32)
    total = lax.psum_scatter(
        partial_out.astype(jnp.bfloat16), "tensor", scatter_dimension=1, tiled=True
    )
    total = total.reshape(experts_n, capacity, share_width)
    returned = lax.all_to_all(total, "expert", split_axis=0, concat_axis=0, tiled=True)
    returned = returned.reshape(slots_n, share_width)
    picked = jnp.einsum("srk,sd->krd", select, returned, preferred_element_type=jnp.float32)
    codes = weight_codes.astype(jnp.float32)
    weight = codes / jnp.sum(codes, axis=1, keepdims=True)
    mixed = weight[:, 0:1] * picked[0] + weight[:, 1:2] * picked[1]
    return mixed.astype(jnp.bfloat16)


def body(tokens, expert_ids, weight_codes, up_weight, down_weight):
    rows = tokens.shape[0]
    capacity = 4 * rows // lax.axis_size("expert")
    plan = whole_blocks if capacity >= rows else slotted
    return plan(tokens, expert_ids, weight_codes, up_weight[0], down_weight[0], capacity)


def solution(mesh):
    return jax.shard_map(
        body,
        mesh=mesh,
        in_specs=(
            P(("group", "expert"), "tensor"),
            P(("group", "expert"), None),
            P(("group", "expert"), None),
            P("expert", None, "tensor"),
            P("expert", "tensor", None),
        ),
        out_specs=P(("group", "expert"), "tensor"),
        check_vma=False,
    )
```

```python
import jax
import jax.numpy as jnp
from jax import lax
from jax.sharding import PartitionSpec as P


def kept_weights(expert_ids, weight_codes, experts_n, capacity):
    rows = expert_ids.shape[0]
    experts = jnp.arange(experts_n, dtype=jnp.int32)
    chosen = expert_ids[:, :, None] == experts[None, None, :]
    counts = jnp.sum(chosen.astype(jnp.float32), axis=1)
    earlier = (
        jnp.arange(rows, dtype=jnp.int32)[:, None] > jnp.arange(rows, dtype=jnp.int32)[None, :]
    ).astype(jnp.float32)
    before = jnp.dot(earlier, counts, preferred_element_type=jnp.float32)
    codes = weight_codes.astype(jnp.float32)
    weight = codes / jnp.sum(codes, axis=1, keepdims=True)
    first = jnp.where(chosen[:, 0] & (before < capacity), weight[:, 0:1], 0.0)
    slot = before + chosen[:, 0].astype(jnp.float32)
    second = jnp.where(chosen[:, 1] & (slot < capacity), weight[:, 1:2], 0.0)
    return first + second


def swap(array, bit):
    return lax.ppermute(array, "tensor", [(i, i ^ bit) for i in range(4)])


def whole_blocks(tokens, expert_ids, weight_codes, up_local, down_local, capacity):
    width = tokens.shape[1]
    experts_n = lax.axis_size("expert")
    me = lax.axis_index("expert")
    place = lax.axis_index("tensor")
    weight = kept_weights(expert_ids, weight_codes, experts_n, capacity).T

    def ring(array, by):
        return lax.ppermute(
            array, "expert", [(i, (i + by) % experts_n) for i in range(experts_n)]
        )

    order = (0, 2, 1, 3)
    ups = [lax.dynamic_slice_in_dim(up_local, (place ^ j) * width, width, 0) for j in order]
    downs = [lax.dynamic_slice_in_dim(down_local, (place ^ j) * width, width, 1) for j in order]
    up_mine = jnp.concatenate(ups, axis=0)
    down_mine = jnp.concatenate(downs, axis=1)

    blocks = [tokens]
    scales = [lax.dynamic_index_in_dim(weight, me, 0, keepdims=False)]
    for step in range(1, experts_n):
        blocks.append(ring(blocks[-1], 1))
        to = lax.rem(me + step, experts_n)
        scales.append(ring(lax.dynamic_index_in_dim(weight, to, 0, keepdims=False), step))

    sums = []
    for block, scale in zip(blocks, scales):
        chip = jnp.concatenate([block, swap(block, 2)], axis=1)
        features = jnp.concatenate([chip, swap(chip, 1)], axis=1)
        lifted = jnp.dot(features, up_mine, preferred_element_type=jnp.float32)
        hidden = (jax.nn.silu(lifted) * scale[:, None]).astype(jnp.bfloat16)
        out = jnp.dot(hidden, down_mine, preferred_element_type=jnp.float32)
        got = swap(out[:, 2 * width :].astype(jnp.bfloat16), 1)
        out = out[:, : 2 * width] + got.astype(jnp.float32)
        got = swap(out[:, width:].astype(jnp.bfloat16), 2)
        sums.append(out[:, :width] + got.astype(jnp.float32))

    total = None
    for part in sums[1:]:
        total = part if total is None else total.astype(jnp.float32) + part
        total = ring(total.astype(jnp.bfloat16), 1)
    mixed = sums[0] if total is None else total.astype(jnp.float32) + sums[0]
    return mixed.astype(jnp.bfloat16)


def slotted(tokens, expert_ids, weight_codes, up_local, down_local, capacity):
    rows, share_width = tokens.shape
    experts_n = lax.axis_size("expert")
    slots_n = experts_n * capacity
    flat_ids = expert_ids.reshape(rows * 2)
    onehot = (flat_ids[:, None] == jnp.arange(experts_n, dtype=jnp.int32)[None, :]).astype(
        jnp.int32
    )
    prior = jnp.cumsum(onehot, axis=0) - onehot
    slot = jnp.sum(prior * onehot, axis=1)
    target = jnp.where(slot < capacity, flat_ids * capacity + slot, -1)
    select = (jnp.arange(slots_n, dtype=jnp.int32)[:, None] == target[None, :]).astype(jnp.bfloat16)
    select = select.reshape(slots_n, rows, 2)
    gather_mat = jnp.sum(select, axis=2)
    sending = jnp.dot(gather_mat, tokens, preferred_element_type=jnp.float32).astype(jnp.bfloat16)
    sending = sending.reshape(experts_n, capacity, share_width)
    received = lax.all_to_all(sending, "expert", split_axis=0, concat_axis=0, tiled=True)
    received = received.reshape(slots_n, share_width)
    received = lax.all_gather(received, "tensor", axis=1, tiled=True)
    lifted = jnp.dot(received, up_local, preferred_element_type=jnp.float32)
    hidden = jax.nn.silu(lifted).astype(jnp.bfloat16)
    partial_out = jnp.dot(hidden, down_local, preferred_element_type=jnp.float32)
    total = lax.psum_scatter(
        partial_out.astype(jnp.bfloat16), "tensor", scatter_dimension=1, tiled=True
    )
    total = total.reshape(experts_n, capacity, share_width)
    returned = lax.all_to_all(total, "expert", split_axis=0, concat_axis=0, tiled=True)
    returned = returned.reshape(slots_n, share_width)
    picked = jnp.einsum("srk,sd->krd", select, returned, preferred_element_type=jnp.float32)
    codes = weight_codes.astype(jnp.float32)
    weight = codes / jnp.sum(codes, axis=1, keepdims=True)
    mixed = weight[:, 0:1] * picked[0] + weight[:, 1:2] * picked[1]
    return mixed.astype(jnp.bfloat16)


def body(tokens, expert_ids, weight_codes, up_weight, down_weight):
    rows = tokens.shape[0]
    capacity = 4 * rows // lax.axis_size("expert")
    whole = capacity >= rows and lax.axis_size("tensor") == 4
    plan = whole_blocks if whole else slotted
    return plan(tokens, expert_ids, weight_codes, up_weight[0], down_weight[0], capacity)


def solution(mesh):
    return jax.shard_map(
        body,
        mesh=mesh,
        in_specs=(
            P(("group", "expert"), "tensor"),
            P(("group", "expert"), None),
            P(("group", "expert"), None),
            P("expert", None, "tensor"),
            P("expert", "tensor", None),
        ),
        out_specs=P(("group", "expert"), "tensor"),
        check_vma=False,
    )
```

```python
import functools

import jax
import jax.numpy as jnp
from jax import lax
from jax.experimental import pallas as pl
from jax.experimental.pallas import tpu as pltpu
from jax.sharding import PartitionSpec as P


MIB = 1 << 20
HBM = pl.BlockSpec(memory_space=pl.ANY)
VMEM = pl.BlockSpec(memory_space=pltpu.VMEM)


def kept_weights(ids, codes, experts_n, capacity):
    rows = ids.shape[1]
    experts = lax.broadcasted_iota(jnp.int32, (experts_n, rows), 0)
    first = ids[0:1, :] == experts
    second = ids[1:2, :] == experts
    counts = first.astype(jnp.float32) + second.astype(jnp.float32)
    earlier = lax.broadcasted_iota(jnp.int32, (rows, rows), 0) < lax.broadcasted_iota(
        jnp.int32, (rows, rows), 1
    )
    before = jnp.dot(
        counts.astype(jnp.bfloat16),
        earlier.astype(jnp.float32).astype(jnp.bfloat16),
        preferred_element_type=jnp.float32,
    )
    codes = codes.astype(jnp.float32)
    weight = codes / (codes[0:1, :] + codes[1:2, :])
    keep_first = first & (before < capacity)
    keep_second = second & (before + first.astype(jnp.float32) < capacity)
    return jnp.where(keep_first, weight[0:1, :], 0.0) + jnp.where(
        keep_second, weight[1:2, :], 0.0
    )


def prepare_kernel(capacity, experts_n, ids, codes, up, down, up_out, down_out, *rest):
    scales, (up_sem, down_sem) = rest[:experts_n], rest[experts_n:]
    up_copy = pltpu.make_async_copy(up, up_out, up_sem)
    down_copy = pltpu.make_async_copy(down, down_out, down_sem)
    up_copy.start()
    down_copy.start()
    me = lax.axis_index("expert")
    weight = kept_weights(ids[...], codes[...], experts_n, capacity)
    index = lax.broadcasted_iota(jnp.int32, weight.shape, 0)
    for step, scale in enumerate(scales):
        mine = index == lax.rem(me + step, experts_n)
        scale[...] = jnp.sum(jnp.where(mine, weight, 0.0), axis=0, keepdims=True)
    up_copy.wait()
    down_copy.wait()


def prepare(ids, codes, up_t, down, experts_n, capacity):
    rows = ids.shape[1]
    return pl.pallas_call(
        functools.partial(prepare_kernel, capacity, experts_n),
        out_shape=[pltpu.VMEM(up_t.shape, up_t.dtype), pltpu.VMEM(down.shape, down.dtype)]
        + [jax.ShapeDtypeStruct((1, rows), jnp.float32)] * experts_n,
        in_specs=[VMEM, VMEM, HBM, HBM],
        out_specs=[VMEM] * (2 + experts_n),
        scratch_shapes=[pltpu.SemaphoreType.DMA, pltpu.SemaphoreType.DMA],
        compiler_params=pltpu.CompilerParams(vmem_limit_bytes=20 * MIB),
        cost_estimate=pl.CostEstimate(
            flops=0, bytes_accessed=4 * up_t.size + 4 * down.size, transcendentals=0
        ),
    )(ids, codes, up_t, down)


def expert_kernel(own, other, own_core, other_core, scale, up_t, down, keep, send, features, out):
    rows, width = own.shape
    place = lax.axis_index("tensor")

    def columns(bits):
        return pl.ds(pl.multiple_of((place ^ bits) * width, width), width)

    features[:, columns(0)] = own[...]
    features[:, columns(2)] = other[...]
    features[:, columns(1)] = own_core[...]
    features[:, columns(3)] = other_core[...]
    lifted = lax.dot_general(
        features[...], up_t[...], (((1,), (1,)), ((), ())), preferred_element_type=jnp.float32
    )
    diagonal = lax.broadcasted_iota(jnp.int32, (rows, rows), 0) == lax.broadcasted_iota(
        jnp.int32, (rows, rows), 1
    )
    column = jnp.sum(jnp.where(diagonal, scale[...], 0.0), axis=1, keepdims=True)
    hidden = (lifted / (1.0 + jnp.exp(-lifted)) * column).astype(jnp.bfloat16)
    out[...] = jnp.dot(hidden, down[...], preferred_element_type=jnp.float32)
    keep[:, :width] = out[:, columns(0)]
    keep[:, width:] = out[:, columns(2)]
    send[:, :width] = out[:, columns(1)].astype(jnp.bfloat16)
    send[:, width:] = out[:, columns(3)].astype(jnp.bfloat16)


def expert_block(own, other, own_core, other_core, scale, up_t, down):
    rows, width = own.shape
    hidden_n, model = up_t.shape
    return pl.pallas_call(
        expert_kernel,
        out_shape=[
            jax.ShapeDtypeStruct((rows, 2 * width), jnp.float32),
            jax.ShapeDtypeStruct((rows, 2 * width), jnp.bfloat16),
        ],
        in_specs=[VMEM] * 7,
        out_specs=[VMEM] * 2,
        scratch_shapes=[
            pltpu.VMEM((rows, model), jnp.bfloat16),
            pltpu.VMEM((rows, model), jnp.float32),
        ],
        compiler_params=pltpu.CompilerParams(vmem_limit_bytes=20 * MIB),
        cost_estimate=pl.CostEstimate(
            flops=4 * rows * model * hidden_n,
            bytes_accessed=4 * rows * model,
            transcendentals=rows * hidden_n,
        ),
    )(own, other, own_core, other_core, scale, up_t, down)


def swap(array, bit):
    return lax.ppermute(array, "tensor", [(i, i ^ bit) for i in range(4)])


def whole_blocks(tokens, expert_ids, weight_codes, up_local, down_local, capacity):
    width = tokens.shape[1]
    experts_n = lax.axis_size("expert")

    def shift(array, by):
        if by % experts_n == 0:
            return array
        return lax.ppermute(
            array, "expert", [(i, (i + by) % experts_n) for i in range(experts_n)]
        )

    blocks = [shift(tokens, step) for step in range(experts_n)]
    up_t, down, *scales = prepare(
        expert_ids.T, weight_codes.T, up_local.T, down_local, experts_n, capacity
    )
    scales = [shift(scale, step) for step, scale in enumerate(scales)]

    mixed = None
    for step, (block, scale) in enumerate(zip(blocks, scales)):
        other = swap(block, 2)
        keep, send = expert_block(
            block, other, swap(block, 1), swap(other, 1), scale, up_t, down
        )
        keep = keep + swap(send, 1).astype(jnp.float32)
        part = keep[:, :width] + swap(keep[:, width:].astype(jnp.bfloat16), 2).astype(jnp.float32)
        if step:
            part = shift(part.astype(jnp.bfloat16), -step).astype(jnp.float32)
        mixed = part if mixed is None else mixed + part
    return mixed.astype(jnp.bfloat16)


def slotted(tokens, expert_ids, weight_codes, up_local, down_local, capacity):
    rows, share_width = tokens.shape
    experts_n = lax.axis_size("expert")
    slots_n = experts_n * capacity
    flat_ids = expert_ids.reshape(rows * 2)
    onehot = (flat_ids[:, None] == jnp.arange(experts_n, dtype=jnp.int32)[None, :]).astype(
        jnp.int32
    )
    prior = jnp.cumsum(onehot, axis=0) - onehot
    slot = jnp.sum(prior * onehot, axis=1)
    target = jnp.where(slot < capacity, flat_ids * capacity + slot, -1)
    select = (jnp.arange(slots_n, dtype=jnp.int32)[:, None] == target[None, :]).astype(jnp.bfloat16)
    select = select.reshape(slots_n, rows, 2)
    gather_mat = jnp.sum(select, axis=2)
    sending = jnp.dot(gather_mat, tokens, preferred_element_type=jnp.float32).astype(jnp.bfloat16)
    sending = sending.reshape(experts_n, capacity, share_width)
    received = lax.all_to_all(sending, "expert", split_axis=0, concat_axis=0, tiled=True)
    received = received.reshape(slots_n, share_width)
    received = lax.all_gather(received, "tensor", axis=1, tiled=True)
    lifted = jnp.dot(received, up_local, preferred_element_type=jnp.float32)
    hidden = jax.nn.silu(lifted).astype(jnp.bfloat16)
    partial_out = jnp.dot(hidden, down_local, preferred_element_type=jnp.float32)
    total = lax.psum_scatter(
        partial_out.astype(jnp.bfloat16), "tensor", scatter_dimension=1, tiled=True
    )
    total = total.reshape(experts_n, capacity, share_width)
    returned = lax.all_to_all(total, "expert", split_axis=0, concat_axis=0, tiled=True)
    returned = returned.reshape(slots_n, share_width)
    picked = jnp.einsum("srk,sd->krd", select, returned, preferred_element_type=jnp.float32)
    codes = weight_codes.astype(jnp.float32)
    weight = codes / jnp.sum(codes, axis=1, keepdims=True)
    mixed = weight[:, 0:1] * picked[0] + weight[:, 1:2] * picked[1]
    return mixed.astype(jnp.bfloat16)


def body(tokens, expert_ids, weight_codes, up_weight, down_weight):
    rows = tokens.shape[0]
    capacity = 4 * rows // lax.axis_size("expert")
    whole = capacity >= rows and lax.axis_size("tensor") == 4
    plan = whole_blocks if whole else slotted
    return plan(tokens, expert_ids, weight_codes, up_weight[0], down_weight[0], capacity)


def solution(mesh):
    return jax.shard_map(
        body,
        mesh=mesh,
        in_specs=(
            P(("group", "expert"), "tensor"),
            P(("group", "expert"), None),
            P(("group", "expert"), None),
            P("expert", None, "tensor"),
            P("expert", "tensor", None),
        ),
        out_specs=P(("group", "expert"), "tensor"),
        check_vma=False,
    )
```

```python
import functools

import jax
import jax.numpy as jnp
from jax import lax
from jax.experimental import pallas as pl
from jax.experimental.pallas import tpu as pltpu
from jax.sharding import PartitionSpec as P


MIB = 1 << 20
HBM = pl.BlockSpec(memory_space=pltpu.HBM)
VMEM = pl.BlockSpec(memory_space=pltpu.VMEM)


def kept_weights(ids, codes, experts_n, capacity):
    rows = ids.shape[1]
    experts = lax.broadcasted_iota(jnp.int32, (experts_n, rows), 0)
    first = ids[0:1, :] == experts
    second = ids[1:2, :] == experts
    counts = first.astype(jnp.float32) + second.astype(jnp.float32)
    earlier = lax.broadcasted_iota(jnp.int32, (rows, rows), 0) < lax.broadcasted_iota(
        jnp.int32, (rows, rows), 1
    )
    before = jnp.dot(
        counts.astype(jnp.bfloat16),
        earlier.astype(jnp.float32).astype(jnp.bfloat16),
        preferred_element_type=jnp.float32,
    )
    codes = codes.astype(jnp.float32)
    weight = codes / (codes[0:1, :] + codes[1:2, :])
    keep_first = first & (before < capacity)
    keep_second = second & (before + first.astype(jnp.float32) < capacity)
    return jnp.where(keep_first, weight[0:1, :], 0.0) + jnp.where(
        keep_second, weight[1:2, :], 0.0
    )


def prepare_kernel(capacity, experts_n, ids, codes, up, down, columns, up_out, down_out, sems):
    copies = [
        pltpu.make_async_copy(up, up_out, sems.at[0]),
        pltpu.make_async_copy(down, down_out, sems.at[1]),
    ]
    for copy in copies:
        copy.start()
    me = lax.axis_index("expert")
    weight = kept_weights(ids[...], codes[...], experts_n, capacity)
    rows = weight.shape[1]
    index = lax.broadcasted_iota(jnp.int32, weight.shape, 0)
    diagonal = lax.broadcasted_iota(jnp.int32, (rows, rows), 0) == lax.broadcasted_iota(
        jnp.int32, (rows, rows), 1
    )
    for step in range(experts_n):
        mine = index == lax.rem(me + step, experts_n)
        row = jnp.sum(jnp.where(mine, weight, 0.0), axis=0, keepdims=True)
        column = jnp.sum(jnp.where(diagonal, row, 0.0), axis=1, keepdims=True)
        columns[step] = jnp.broadcast_to(column, columns.shape[1:])
    for copy in copies:
        copy.wait()


def local_call(kernel, out_shape, operands, others=(), in_specs=None, **kwargs):
    count = len(operands)

    def body_of(*refs):
        kernel(*refs[:count], *refs[count + len(others) :])

    return pl.pallas_call(
        body_of,
        out_shape=out_shape,
        in_specs=list(in_specs or [VMEM] * count) + [pl.BlockSpec(memory_space=pl.ANY)] * len(others),
        out_specs=jax.tree.map(lambda _: VMEM, out_shape),
        **kwargs,
    )(*operands, *others)


def prepare(ids, codes, up_t, down, experts_n, capacity):
    rows = ids.shape[1]
    return local_call(
        functools.partial(prepare_kernel, capacity, experts_n),
        [
            jax.ShapeDtypeStruct((experts_n, rows, 128), jnp.float32),
            pltpu.VMEM(up_t.shape, up_t.dtype),
            pltpu.VMEM(down.shape, down.dtype),
        ],
        (ids, codes, up_t, down),
        in_specs=[VMEM, VMEM, HBM, HBM],
        scratch_shapes=[pltpu.SemaphoreType.DMA((2,))],
        compiler_params=pltpu.CompilerParams(vmem_limit_bytes=52 * MIB),
        cost_estimate=pl.CostEstimate(
            flops=0, bytes_accessed=2 * up_t.size + 2 * down.size, transcendentals=0
        ),
    )


def expert_kernel(own, other, own_core, other_core, up_t, down, keep, send, features, out):
    width = own.shape[1]
    place = lax.axis_index("tensor")

    def columns(bits):
        return pl.ds(pl.multiple_of((place ^ bits) * width, width), width)

    features[:, columns(0)] = own[...]
    features[:, columns(2)] = other[...]
    features[:, columns(1)] = own_core[...]
    features[:, columns(3)] = other_core[...]
    lifted = lax.dot_general(
        features[...], up_t[...], (((1,), (1,)), ((), ())), preferred_element_type=jnp.float32
    )
    hidden = (lifted / (1.0 + jnp.exp(-lifted))).astype(jnp.bfloat16)
    out[...] = jnp.dot(hidden, down[...], preferred_element_type=jnp.float32)
    keep[:, :width] = out[:, columns(0)]
    keep[:, width:] = out[:, columns(2)]
    send[:, :width] = out[:, columns(1)].astype(jnp.bfloat16)
    send[:, width:] = out[:, columns(3)].astype(jnp.bfloat16)


def expert_block(block, up_t, down, others):
    rows, width = block[0].shape
    model = up_t.shape[1]
    return local_call(
        expert_kernel,
        [
            jax.ShapeDtypeStruct((rows, 2 * width), jnp.float32),
            jax.ShapeDtypeStruct((rows, 2 * width), jnp.bfloat16),
        ],
        (*block, up_t, down),
        others,
        scratch_shapes=[
            pltpu.VMEM((rows, model), jnp.bfloat16),
            pltpu.VMEM((rows, model), jnp.float32),
        ],
        compiler_params=pltpu.CompilerParams(vmem_limit_bytes=20 * MIB),
        cost_estimate=pl.CostEstimate(flops=1, bytes_accessed=1, transcendentals=0),
    )


def core_sum_kernel(keep, got, own, send):
    width = own.shape[1]
    own[...] = keep[:, :width] + got[:, :width].astype(jnp.float32)
    send[...] = (keep[:, width:] + got[:, width:].astype(jnp.float32)).astype(send.dtype)


def core_sum(keep, got, others):
    rows, width = keep.shape[0], keep.shape[1] // 2
    return local_call(
        core_sum_kernel,
        [
            jax.ShapeDtypeStruct((rows, width), jnp.float32),
            jax.ShapeDtypeStruct((rows, width), jnp.bfloat16),
        ],
        (keep, got),
        others,
    )


def chip_sum_kernel(own, got, part):
    part[...] = (own[...] + got[...].astype(jnp.float32)).astype(part.dtype)


def chip_sum(own, got, others):
    return local_call(
        chip_sum_kernel, jax.ShapeDtypeStruct(own.shape, jnp.bfloat16), (own, got), others
    )


def combine_kernel(columns, own, got, *rest):
    parts, mixed = rest[:-1], rest[-1]
    total = columns[0, :, 0:1] * (own[...] + got[...].astype(jnp.float32))
    for step, part in enumerate(parts, 1):
        total += columns[step, :, 0:1] * part[...].astype(jnp.float32)
    mixed[...] = total.astype(mixed.dtype)


def combine(columns, own, got, parts, others):
    return local_call(
        combine_kernel,
        jax.ShapeDtypeStruct(own.shape, jnp.bfloat16),
        (columns, own, got, *parts),
        others,
    )


def swap(array, bit):
    return lax.ppermute(array, "tensor", [(i, i ^ bit) for i in range(4)])


def whole_blocks(tokens, expert_ids, weight_codes, up_local, down_local, capacity):
    experts_n = lax.axis_size("expert")

    def shift(array, by):
        return lax.ppermute(
            array, "expert", [(i, (i + by) % experts_n) for i in range(experts_n)]
        )

    steps = list(range(1, experts_n))
    steps = steps[:1] + steps[:0:-1]
    blocks = {0: tokens} | {step: shift(tokens, step) for step in steps}
    others = {step: swap(block, 2) for step, block in blocks.items()}
    columns, up_t, down = prepare(
        expert_ids.T, weight_codes.T, up_local.T, down_local, experts_n, capacity
    )

    order = [0] + steps
    kept, sums, parts = {}, {}, {}
    last = [columns]

    def expert(step, *waits):
        block = blocks[step], others[step], swap(blocks[step], 1), swap(others[step], 1)
        kept[step] = expert_block(block, up_t, down, last + list(waits))
        last[:] = kept[step][:1]

    def cores(step):
        keep, send = kept[step]
        own, away = core_sum(keep, swap(send, 1), last)
        sums[step] = own, swap(away, 2)
        last[:] = [own]

    def chips(step):
        part = chip_sum(*sums[step], last)
        parts[step] = shift(part, -step)
        last[:] = [part]

    for place, step in enumerate(order):
        expert(step, *[blocks[following] for following in order[place + 1 : place + 3]])
        if place >= 2:
            cores(order[place - 1])
    if steps:
        cores(order[-1])
    cores(0)
    for step in steps:
        chips(step)
    return combine(columns, *sums[0], [parts[step] for step in range(1, experts_n)], last)


def slotted(tokens, expert_ids, weight_codes, up_local, down_local, capacity):
    rows, share_width = tokens.shape
    experts_n = lax.axis_size("expert")
    slots_n = experts_n * capacity
    flat_ids = expert_ids.reshape(rows * 2)
    onehot = (flat_ids[:, None] == jnp.arange(experts_n, dtype=jnp.int32)[None, :]).astype(
        jnp.int32
    )
    prior = jnp.cumsum(onehot, axis=0) - onehot
    slot = jnp.sum(prior * onehot, axis=1)
    target = jnp.where(slot < capacity, flat_ids * capacity + slot, -1)
    select = (jnp.arange(slots_n, dtype=jnp.int32)[:, None] == target[None, :]).astype(jnp.bfloat16)
    select = select.reshape(slots_n, rows, 2)
    gather_mat = jnp.sum(select, axis=2)
    sending = jnp.dot(gather_mat, tokens, preferred_element_type=jnp.float32).astype(jnp.bfloat16)
    sending = sending.reshape(experts_n, capacity, share_width)
    received = lax.all_to_all(sending, "expert", split_axis=0, concat_axis=0, tiled=True)
    received = received.reshape(slots_n, share_width)
    received = lax.all_gather(received, "tensor", axis=1, tiled=True)
    lifted = jnp.dot(received, up_local, preferred_element_type=jnp.float32)
    hidden = jax.nn.silu(lifted).astype(jnp.bfloat16)
    partial_out = jnp.dot(hidden, down_local, preferred_element_type=jnp.float32)
    total = lax.psum_scatter(
        partial_out.astype(jnp.bfloat16), "tensor", scatter_dimension=1, tiled=True
    )
    total = total.reshape(experts_n, capacity, share_width)
    returned = lax.all_to_all(total, "expert", split_axis=0, concat_axis=0, tiled=True)
    returned = returned.reshape(slots_n, share_width)
    picked = jnp.einsum("srk,sd->krd", select, returned, preferred_element_type=jnp.float32)
    codes = weight_codes.astype(jnp.float32)
    weight = codes / jnp.sum(codes, axis=1, keepdims=True)
    mixed = weight[:, 0:1] * picked[0] + weight[:, 1:2] * picked[1]
    return mixed.astype(jnp.bfloat16)


def body(tokens, expert_ids, weight_codes, up_weight, down_weight):
    rows = tokens.shape[0]
    capacity = 4 * rows // lax.axis_size("expert")
    whole = capacity >= rows and lax.axis_size("tensor") == 4
    plan = whole_blocks if whole else slotted
    return plan(tokens, expert_ids, weight_codes, up_weight[0], down_weight[0], capacity)


def solution(mesh):
    return jax.shard_map(
        body,
        mesh=mesh,
        in_specs=(
            P(("group", "expert"), "tensor"),
            P(("group", "expert"), None),
            P(("group", "expert"), None),
            P("expert", None, "tensor"),
            P("expert", "tensor", None),
        ),
        out_specs=P(("group", "expert"), "tensor"),
        check_vma=False,
    )
```

```python
import functools

import jax
import jax.numpy as jnp
from jax import lax
from jax.experimental import pallas as pl
from jax.experimental.pallas import tpu as pltpu
from jax.sharding import PartitionSpec as P


MIB = 1 << 20
HBM = pl.BlockSpec(memory_space=pltpu.HBM)
VMEM = pl.BlockSpec(memory_space=pltpu.VMEM)


def kept_weights(ids, codes, experts_n, capacity):
    rows = ids.shape[1]
    experts = lax.broadcasted_iota(jnp.int32, (experts_n, rows), 0)
    first = ids[0:1, :] == experts
    second = ids[1:2, :] == experts
    counts = first.astype(jnp.float32) + second.astype(jnp.float32)
    earlier = lax.broadcasted_iota(jnp.int32, (rows, rows), 0) < lax.broadcasted_iota(
        jnp.int32, (rows, rows), 1
    )
    before = jnp.dot(
        counts.astype(jnp.bfloat16),
        earlier.astype(jnp.float32).astype(jnp.bfloat16),
        preferred_element_type=jnp.float32,
    )
    codes = codes.astype(jnp.float32)
    weight = codes / (codes[0:1, :] + codes[1:2, :])
    keep_first = first & (before < capacity)
    keep_second = second & (before + first.astype(jnp.float32) < capacity)
    return jnp.where(keep_first, weight[0:1, :], 0.0) + jnp.where(
        keep_second, weight[1:2, :], 0.0
    )


def prepare_kernel(capacity, experts_n, ids, codes, up, down, columns, up_out, down_out, sems):
    copies = [
        pltpu.make_async_copy(up, up_out, sems.at[0]),
        pltpu.make_async_copy(down, down_out, sems.at[1]),
    ]
    for copy in copies:
        copy.start()
    me = lax.axis_index("expert")
    weight = kept_weights(ids[...], codes[...], experts_n, capacity)
    rows = weight.shape[1]
    index = lax.broadcasted_iota(jnp.int32, weight.shape, 0)
    diagonal = lax.broadcasted_iota(jnp.int32, (rows, rows), 0) == lax.broadcasted_iota(
        jnp.int32, (rows, rows), 1
    )
    for step in range(experts_n):
        mine = index == lax.rem(me + step, experts_n)
        row = jnp.sum(jnp.where(mine, weight, 0.0), axis=0, keepdims=True)
        column = jnp.sum(jnp.where(diagonal, row, 0.0), axis=1, keepdims=True)
        columns[step] = jnp.broadcast_to(column, columns.shape[1:])
    for copy in copies:
        copy.wait()


def local_call(kernel, out_shape, operands, others=(), in_specs=None, limit=4 * MIB, **kwargs):
    count = len(operands)

    name = getattr(kernel, "func", kernel).__name__

    def body_of(*refs):
        kernel(*refs[:count], *refs[count + len(others) :])

    return pl.pallas_call(
        body_of,
        name=name,
        out_shape=out_shape,
        in_specs=list(in_specs or [VMEM] * count) + [pl.BlockSpec(memory_space=pl.ANY)] * len(others),
        out_specs=jax.tree.map(lambda _: VMEM, out_shape),
        compiler_params=pltpu.CompilerParams(vmem_limit_bytes=limit),
        **kwargs,
    )(*operands, *others)


def after(array, other):
    anywhere = pl.BlockSpec(memory_space=pl.ANY)
    return pl.pallas_call(
        lambda *refs: None,
        out_shape=jax.ShapeDtypeStruct(array.shape, array.dtype),
        in_specs=[anywhere, anywhere],
        out_specs=anywhere,
        input_output_aliases={0: 0},
        compiler_params=pltpu.CompilerParams(vmem_limit_bytes=MIB),
    )(array, other)


def prepare(ids, codes, up_t, down, experts_n, capacity):
    rows = ids.shape[1]
    return local_call(
        functools.partial(prepare_kernel, capacity, experts_n),
        [
            pltpu.VMEM((experts_n, rows, 128), jnp.float32),
            pltpu.VMEM(up_t.shape, up_t.dtype),
            pltpu.VMEM(down.shape, down.dtype),
        ],
        (ids, codes, up_t, down),
        in_specs=[VMEM, VMEM, HBM, HBM],
        scratch_shapes=[pltpu.SemaphoreType.DMA((2,))],
        limit=50 * MIB,
        cost_estimate=pl.CostEstimate(
            flops=0, bytes_accessed=4 * up_t.size, transcendentals=0
        ),
    )


def pack_kernel(*refs):
    packed = refs[-1]
    rows, width = refs[0].shape
    for index, ref in enumerate(refs[:-1]):
        at, column = index // 2 * rows, index % 2 * width
        packed[at : at + rows, column : column + width] = ref[...]


def pack(pairs, others):
    rows, width = pairs[0][0].shape
    return local_call(
        pack_kernel,
        jax.ShapeDtypeStruct((len(pairs) * rows, 2 * width), pairs[0][0].dtype),
        [array for pair in pairs for array in pair],
        others,
    )


def expert_kernel(chip, core, up_t, down, keep, send, features, out):
    width = chip.shape[1] // 2
    place = lax.axis_index("tensor")

    def columns(bits):
        return pl.ds(pl.multiple_of((place ^ bits) * width, width), width)

    features[:, columns(0)] = chip[:, :width]
    features[:, columns(2)] = chip[:, width:]
    features[:, columns(1)] = core[:, :width]
    features[:, columns(3)] = core[:, width:]
    lifted = lax.dot_general(
        features[...], up_t[...], (((1,), (1,)), ((), ())), preferred_element_type=jnp.float32
    )
    hidden = (lifted / (1.0 + jnp.exp(-lifted))).astype(jnp.bfloat16)
    out[...] = jnp.dot(hidden, down[...], preferred_element_type=jnp.float32)
    keep[:, :width] = out[:, columns(0)]
    keep[:, width:] = out[:, columns(2)]
    send[:, :width] = out[:, columns(1)].astype(jnp.bfloat16)
    send[:, width:] = out[:, columns(3)].astype(jnp.bfloat16)


def expert_rows(chip, core, up_t, down, others):
    rows, model = chip.shape[0], up_t.shape[1]
    return local_call(
        expert_kernel,
        [
            jax.ShapeDtypeStruct(chip.shape, jnp.float32),
            jax.ShapeDtypeStruct(chip.shape, jnp.bfloat16),
        ],
        (chip, core, up_t, down),
        others,
        limit=10 * MIB,
        scratch_shapes=[
            pltpu.VMEM((rows, model), jnp.bfloat16),
            pltpu.VMEM((rows, model), jnp.float32),
        ],
        cost_estimate=pl.CostEstimate(
            flops=8 * chip.size * up_t.shape[0], bytes_accessed=0, transcendentals=0
        ),
    )


def core_sum_kernel(keep, got, own, *sends):
    width = own.shape[1]
    own[...] = keep[:, :width] + got[:, :width].astype(jnp.float32)
    for index, send in enumerate(sends):
        rows = slice(index * send.shape[0], (index + 1) * send.shape[0])
        send[...] = (keep[rows, width:] + got[rows, width:].astype(jnp.float32)).astype(send.dtype)


def core_sum(keep, got, count, others):
    rows, width = keep.shape[0], keep.shape[1] // 2
    return local_call(
        core_sum_kernel,
        [jax.ShapeDtypeStruct((rows, width), jnp.float32)]
        + [jax.ShapeDtypeStruct((rows // count, width), jnp.bfloat16)] * count,
        (keep, got),
        others,
    )


def chip_sum_kernel(index, own, got, part):
    rows = slice(index * got.shape[0], (index + 1) * got.shape[0])
    part[...] = (own[rows, :] + got[...].astype(jnp.float32)).astype(part.dtype)


def chip_sum(own, got, index, others):
    return local_call(
        functools.partial(chip_sum_kernel, index),
        jax.ShapeDtypeStruct(got.shape, jnp.bfloat16),
        (own, got),
        others,
    )


def combine_kernel(columns, own, got, *rest):
    parts, mixed = rest[:-1], rest[-1]
    total = columns[0, :, 0:1] * (own[...] + got[...].astype(jnp.float32))
    for step, part in enumerate(parts, 1):
        total += columns[step, :, 0:1] * part[...].astype(jnp.float32)
    mixed[...] = total.astype(mixed.dtype)


def combine(columns, own, got, parts, others):
    return local_call(
        combine_kernel,
        jax.ShapeDtypeStruct(own.shape, jnp.bfloat16),
        (columns, own, got, *parts),
        others,
    )


def swap(array, bit):
    return lax.ppermute(array, "tensor", [(i, i ^ bit) for i in range(4)])


def whole_blocks(tokens, expert_ids, weight_codes, up_local, down_local, capacity):
    experts_n = lax.axis_size("expert")

    def shift(array, by):
        return lax.ppermute(
            array, "expert", [(i, (i + by) % experts_n) for i in range(experts_n)]
        )

    steps = (3, 2, 1)
    order = [step for step in steps if step < experts_n] + [0]
    blocks = {0: tokens} | {step: shift(tokens, step) for step in order[:-1]}
    columns, up_t, down = prepare(
        expert_ids.T, weight_codes.T, up_local.T, down_local, experts_n, capacity
    )
    blocks[order[0]] = after(blocks[order[0]], columns)
    others = {step: swap(block, 2) for step, block in blocks.items()}

    chips, sums, parts = {}, {}, {}
    for step in order:
        waits = [] if chips else [others[0]]
        chips[step] = pack([(blocks[step], others[step])], waits)
    for step in order:
        keep, send = expert_rows(chips[step], swap(chips[step], 1), up_t, down, ())
        own, away = core_sum(keep, swap(send, 1), 1, ())
        sums[step] = own, swap(away, 2)
    for step in order[:-1]:
        parts[step] = shift(chip_sum(*sums[step], 0, ()), -step)
    return combine(columns, *sums[0], [parts[step] for step in range(1, experts_n)], ())


def slotted(tokens, expert_ids, weight_codes, up_local, down_local, capacity):
    rows, share_width = tokens.shape
    experts_n = lax.axis_size("expert")
    slots_n = experts_n * capacity
    flat_ids = expert_ids.reshape(rows * 2)
    onehot = (flat_ids[:, None] == jnp.arange(experts_n, dtype=jnp.int32)[None, :]).astype(
        jnp.int32
    )
    prior = jnp.cumsum(onehot, axis=0) - onehot
    slot = jnp.sum(prior * onehot, axis=1)
    target = jnp.where(slot < capacity, flat_ids * capacity + slot, -1)
    select = (jnp.arange(slots_n, dtype=jnp.int32)[:, None] == target[None, :]).astype(jnp.bfloat16)
    select = select.reshape(slots_n, rows, 2)
    gather_mat = jnp.sum(select, axis=2)
    sending = jnp.dot(gather_mat, tokens, preferred_element_type=jnp.float32).astype(jnp.bfloat16)
    sending = sending.reshape(experts_n, capacity, share_width)
    received = lax.all_to_all(sending, "expert", split_axis=0, concat_axis=0, tiled=True)
    received = received.reshape(slots_n, share_width)
    received = lax.all_gather(received, "tensor", axis=1, tiled=True)
    lifted = jnp.dot(received, up_local, preferred_element_type=jnp.float32)
    hidden = jax.nn.silu(lifted).astype(jnp.bfloat16)
    partial_out = jnp.dot(hidden, down_local, preferred_element_type=jnp.float32)
    total = lax.psum_scatter(
        partial_out.astype(jnp.bfloat16), "tensor", scatter_dimension=1, tiled=True
    )
    total = total.reshape(experts_n, capacity, share_width)
    returned = lax.all_to_all(total, "expert", split_axis=0, concat_axis=0, tiled=True)
    returned = returned.reshape(slots_n, share_width)
    picked = jnp.einsum("srk,sd->krd", select, returned, preferred_element_type=jnp.float32)
    codes = weight_codes.astype(jnp.float32)
    weight = codes / jnp.sum(codes, axis=1, keepdims=True)
    mixed = weight[:, 0:1] * picked[0] + weight[:, 1:2] * picked[1]
    return mixed.astype(jnp.bfloat16)


def body(tokens, expert_ids, weight_codes, up_weight, down_weight):
    rows = tokens.shape[0]
    capacity = 4 * rows // lax.axis_size("expert")
    whole = capacity >= rows and lax.axis_size("tensor") == 4
    plan = whole_blocks if whole else slotted
    return plan(tokens, expert_ids, weight_codes, up_weight[0], down_weight[0], capacity)


def solution(mesh):
    return jax.shard_map(
        body,
        mesh=mesh,
        in_specs=(
            P(("group", "expert"), "tensor"),
            P(("group", "expert"), None),
            P(("group", "expert"), None),
            P("expert", None, "tensor"),
            P("expert", "tensor", None),
        ),
        out_specs=P(("group", "expert"), "tensor"),
        check_vma=False,
    )
```

```python
import functools

import jax
import jax.numpy as jnp
from jax import lax
from jax.experimental import pallas as pl
from jax.experimental.pallas import tpu as pltpu
from jax.sharding import PartitionSpec as P


MIB = 1 << 20
HBM = pl.BlockSpec(memory_space=pltpu.HBM)
VMEM = pl.BlockSpec(memory_space=pltpu.VMEM)


def kept_weights(ids, codes, experts_n, capacity):
    rows = ids.shape[1]
    experts = lax.broadcasted_iota(jnp.int32, (experts_n, rows), 0)
    first = ids[0:1, :] == experts
    second = ids[1:2, :] == experts
    counts = first.astype(jnp.float32) + second.astype(jnp.float32)
    earlier = lax.broadcasted_iota(jnp.int32, (rows, rows), 0) < lax.broadcasted_iota(
        jnp.int32, (rows, rows), 1
    )
    before = jnp.dot(
        counts.astype(jnp.bfloat16),
        earlier.astype(jnp.float32).astype(jnp.bfloat16),
        preferred_element_type=jnp.float32,
    )
    codes = codes.astype(jnp.float32)
    weight = codes / (codes[0:1, :] + codes[1:2, :])
    keep_first = first & (before < capacity)
    keep_second = second & (before + first.astype(jnp.float32) < capacity)
    return jnp.where(keep_first, weight[0:1, :], 0.0) + jnp.where(
        keep_second, weight[1:2, :], 0.0
    )


def prepare_kernel(capacity, experts_n, ids, codes, up, down, columns, up_out, down_out, sems):
    copies = [
        pltpu.make_async_copy(up, up_out, sems.at[0]),
        pltpu.make_async_copy(down, down_out, sems.at[1]),
    ]
    for copy in copies:
        copy.start()
    me = lax.axis_index("expert")
    weight = kept_weights(ids[...], codes[...], experts_n, capacity)
    rows = weight.shape[1]
    index = lax.broadcasted_iota(jnp.int32, weight.shape, 0)
    diagonal = lax.broadcasted_iota(jnp.int32, (rows, rows), 0) == lax.broadcasted_iota(
        jnp.int32, (rows, rows), 1
    )
    for step in range(experts_n):
        mine = index == lax.rem(me + step, experts_n)
        row = jnp.sum(jnp.where(mine, weight, 0.0), axis=0, keepdims=True)
        column = jnp.sum(jnp.where(diagonal, row, 0.0), axis=1, keepdims=True)
        columns[step] = jnp.broadcast_to(column, columns.shape[1:])
    for copy in copies:
        copy.wait()


def local_call(kernel, out_shape, operands, others=(), in_specs=None, limit=4 * MIB, **kwargs):
    count = len(operands)

    name = getattr(kernel, "func", kernel).__name__

    def body_of(*refs):
        kernel(*refs[:count], *refs[count + len(others) :])

    return pl.pallas_call(
        body_of,
        name=name,
        out_shape=out_shape,
        in_specs=list(in_specs or [VMEM] * count) + [pl.BlockSpec(memory_space=pl.ANY)] * len(others),
        out_specs=jax.tree.map(lambda _: VMEM, out_shape),
        compiler_params=pltpu.CompilerParams(vmem_limit_bytes=limit),
        **kwargs,
    )(*operands, *others)


def after(array, other):
    anywhere = pl.BlockSpec(memory_space=pl.ANY)
    return pl.pallas_call(
        lambda *refs: None,
        out_shape=jax.ShapeDtypeStruct(array.shape, array.dtype),
        in_specs=[anywhere, anywhere],
        out_specs=anywhere,
        input_output_aliases={0: 0},
        compiler_params=pltpu.CompilerParams(vmem_limit_bytes=MIB),
    )(array, other)


def prepare(ids, codes, up_t, down, experts_n, capacity):
    rows = ids.shape[1]
    return local_call(
        functools.partial(prepare_kernel, capacity, experts_n),
        [
            pltpu.VMEM((experts_n, rows, 128), jnp.float32),
            pltpu.VMEM(up_t.shape, up_t.dtype),
            pltpu.VMEM(down.shape, down.dtype),
        ],
        (ids, codes, up_t, down),
        in_specs=[VMEM, VMEM, HBM, HBM],
        scratch_shapes=[pltpu.SemaphoreType.DMA((2,))],
        limit=50 * MIB,
        cost_estimate=pl.CostEstimate(
            flops=0, bytes_accessed=4 * up_t.size, transcendentals=0
        ),
    )


def pack_kernel(*refs):
    packed = refs[-1]
    rows, width = refs[0].shape
    for index, ref in enumerate(refs[:-1]):
        at, column = index // 2 * rows, index % 2 * width
        packed[at : at + rows, column : column + width] = ref[...]


def pack(pairs, others):
    rows, width = pairs[0][0].shape
    return local_call(
        pack_kernel,
        jax.ShapeDtypeStruct((len(pairs) * rows, 2 * width), pairs[0][0].dtype),
        [array for pair in pairs for array in pair],
        others,
    )


def expert_kernel(chip, core, up_t, down, keep, send, features, out):
    width = chip.shape[1] // 2
    place = lax.axis_index("tensor")

    def columns(bits):
        return pl.ds(pl.multiple_of((place ^ bits) * width, width), width)

    features[:, columns(0)] = chip[:, :width]
    features[:, columns(2)] = chip[:, width:]
    features[:, columns(1)] = core[:, :width]
    features[:, columns(3)] = core[:, width:]
    lifted = lax.dot_general(
        features[...], up_t[...], (((1,), (1,)), ((), ())), preferred_element_type=jnp.float32
    )
    hidden = (lifted / (1.0 + jnp.exp(-lifted))).astype(jnp.bfloat16)
    out[...] = jnp.dot(hidden, down[...], preferred_element_type=jnp.float32)
    keep[:, :width] = out[:, columns(0)]
    keep[:, width:] = out[:, columns(2)]
    send[:, :width] = out[:, columns(1)].astype(jnp.bfloat16)
    send[:, width:] = out[:, columns(3)].astype(jnp.bfloat16)


def expert_rows(chip, core, up_t, down, others):
    rows, model = chip.shape[0], up_t.shape[1]
    return local_call(
        expert_kernel,
        [
            jax.ShapeDtypeStruct(chip.shape, jnp.float32),
            jax.ShapeDtypeStruct(chip.shape, jnp.bfloat16),
        ],
        (chip, core, up_t, down),
        others,
        limit=10 * MIB,
        scratch_shapes=[
            pltpu.VMEM((rows, model), jnp.bfloat16),
            pltpu.VMEM((rows, model), jnp.float32),
        ],
        cost_estimate=pl.CostEstimate(
            flops=8 * chip.size * up_t.shape[0], bytes_accessed=0, transcendentals=0
        ),
    )


def core_sum_kernel(keep, got, own, *sends):
    width = own.shape[1]
    own[...] = keep[:, :width] + got[:, :width].astype(jnp.float32)
    for index, send in enumerate(sends):
        rows = slice(index * send.shape[0], (index + 1) * send.shape[0])
        send[...] = (keep[rows, width:] + got[rows, width:].astype(jnp.float32)).astype(send.dtype)


def core_sum(keep, got, count, others):
    rows, width = keep.shape[0], keep.shape[1] // 2
    return local_call(
        core_sum_kernel,
        [jax.ShapeDtypeStruct((rows, width), jnp.float32)]
        + [jax.ShapeDtypeStruct((rows // count, width), jnp.bfloat16)] * count,
        (keep, got),
        others,
    )


def chip_sum_kernel(index, own, got, part):
    rows = slice(index * got.shape[0], (index + 1) * got.shape[0])
    part[...] = (own[rows, :] + got[...].astype(jnp.float32)).astype(part.dtype)


def chip_sum(own, got, index, others):
    return local_call(
        functools.partial(chip_sum_kernel, index),
        jax.ShapeDtypeStruct(got.shape, jnp.bfloat16),
        (own, got),
        others,
    )


def combine_kernel(columns, own, got, *rest):
    parts, mixed = rest[:-1], rest[-1]
    total = columns[0, :, 0:1] * (own[...] + got[...].astype(jnp.float32))
    for step, part in enumerate(parts, 1):
        total += columns[step, :, 0:1] * part[...].astype(jnp.float32)
    mixed[...] = total.astype(mixed.dtype)


def combine(columns, own, got, parts, others):
    return local_call(
        combine_kernel,
        jax.ShapeDtypeStruct(own.shape, jnp.bfloat16),
        (columns, own, got, *parts),
        others,
    )


def swap(array, bit):
    return lax.ppermute(array, "tensor", [(i, i ^ bit) for i in range(4)])


def whole_blocks(tokens, expert_ids, weight_codes, up_local, down_local, capacity):
    experts_n = lax.axis_size("expert")

    def shift(array, by):
        return lax.ppermute(
            array, "expert", [(i, (i + by) % experts_n) for i in range(experts_n)]
        )

    columns, up_t, down = prepare(
        expert_ids.T, weight_codes.T, up_local.T, down_local, experts_n, capacity
    )
    blocks, others, chips, kept, sums, added, parts = {}, {}, {}, {}, {}, {}, {}

    def arrive(step, waits):
        blocks[step] = shift(blocks[step - 1], 1) if step else tokens
        for wait in waits:
            blocks[step] = after(blocks[step], wait)
        others[step] = swap(blocks[step], 2)

    def lay(step, waits):
        chips[step] = pack([(blocks[step], others[step])], waits)

    def run(step, waits):
        kept[step] = expert_rows(chips[step], swap(chips[step], 1), up_t, down, waits)

    def leave(step, waits):
        keep, send = kept[step]
        own, away = core_sum(keep, swap(send, 1), 1, waits)
        sums[step] = own, swap(away, 2)

    def give(step, waits):
        added[step] = chip_sum(*sums[step], 0, waits)
        parts[step] = shift(added[step], -step)

    arrive(0, [])
    if experts_n > 1:
        arrive(1, [columns])
    lay(0, [blocks[1]] if experts_n > 1 else [])
    run(0, [])
    waits = []
    for step in range(1, experts_n):
        if step + 1 < experts_n:
            arrive(step + 1, [kept[step - 1][0]])
            lay(step, [blocks[step + 1]])
        else:
            lay(step, [kept[step - 1][0]])
            leave(0, [sums[1][0]] if 1 in sums else [])
            waits = [sums[0][0]]
        if step > 1:
            leave(step - 1, waits)
            waits = [sums[step - 1][0]]
        if step > 2:
            waits.append(sums[step - 2][1])
        run(step, waits)
        if step > 2:
            give(step - 2, [kept[step][0]])
    if not sums:
        leave(0, [])
    if experts_n > 1:
        leave(experts_n - 1, list(added.values())[-1:])
    for step in range(1, experts_n):
        if step not in parts:
            give(step, [sums[experts_n - 1][0]])
    return combine(columns, *sums[0], [parts[step] for step in range(1, experts_n)], ())


def slotted(tokens, expert_ids, weight_codes, up_local, down_local, capacity):
    rows, share_width = tokens.shape
    experts_n = lax.axis_size("expert")
    slots_n = experts_n * capacity
    flat_ids = expert_ids.reshape(rows * 2)
    onehot = (flat_ids[:, None] == jnp.arange(experts_n, dtype=jnp.int32)[None, :]).astype(
        jnp.int32
    )
    prior = jnp.cumsum(onehot, axis=0) - onehot
    slot = jnp.sum(prior * onehot, axis=1)
    target = jnp.where(slot < capacity, flat_ids * capacity + slot, -1)
    select = (jnp.arange(slots_n, dtype=jnp.int32)[:, None] == target[None, :]).astype(jnp.bfloat16)
    select = select.reshape(slots_n, rows, 2)
    gather_mat = jnp.sum(select, axis=2)
    sending = jnp.dot(gather_mat, tokens, preferred_element_type=jnp.float32).astype(jnp.bfloat16)
    sending = sending.reshape(experts_n, capacity, share_width)
    received = lax.all_to_all(sending, "expert", split_axis=0, concat_axis=0, tiled=True)
    received = received.reshape(slots_n, share_width)
    received = lax.all_gather(received, "tensor", axis=1, tiled=True)
    lifted = jnp.dot(received, up_local, preferred_element_type=jnp.float32)
    hidden = jax.nn.silu(lifted).astype(jnp.bfloat16)
    partial_out = jnp.dot(hidden, down_local, preferred_element_type=jnp.float32)
    total = lax.psum_scatter(
        partial_out.astype(jnp.bfloat16), "tensor", scatter_dimension=1, tiled=True
    )
    total = total.reshape(experts_n, capacity, share_width)
    returned = lax.all_to_all(total, "expert", split_axis=0, concat_axis=0, tiled=True)
    returned = returned.reshape(slots_n, share_width)
    picked = jnp.einsum("srk,sd->krd", select, returned, preferred_element_type=jnp.float32)
    codes = weight_codes.astype(jnp.float32)
    weight = codes / jnp.sum(codes, axis=1, keepdims=True)
    mixed = weight[:, 0:1] * picked[0] + weight[:, 1:2] * picked[1]
    return mixed.astype(jnp.bfloat16)


def body(tokens, expert_ids, weight_codes, up_weight, down_weight):
    rows = tokens.shape[0]
    capacity = 4 * rows // lax.axis_size("expert")
    whole = capacity >= rows and lax.axis_size("tensor") == 4
    plan = whole_blocks if whole else slotted
    return plan(tokens, expert_ids, weight_codes, up_weight[0], down_weight[0], capacity)


def solution(mesh):
    return jax.shard_map(
        body,
        mesh=mesh,
        in_specs=(
            P(("group", "expert"), "tensor"),
            P(("group", "expert"), None),
            P(("group", "expert"), None),
            P("expert", None, "tensor"),
            P("expert", "tensor", None),
        ),
        out_specs=P(("group", "expert"), "tensor"),
        check_vma=False,
    )
```

```python
import functools

import jax
import jax.numpy as jnp
from jax import lax
from jax.experimental import pallas as pl
from jax.experimental.pallas import tpu as pltpu
from jax.sharding import PartitionSpec as P


MIB = 1 << 20
HBM = pl.BlockSpec(memory_space=pltpu.HBM)
VMEM = pl.BlockSpec(memory_space=pltpu.VMEM)


def kept_weights(ids, codes, experts_n, capacity):
    rows = ids.shape[1]
    experts = lax.broadcasted_iota(jnp.int32, (experts_n, rows), 0)
    first = ids[0:1, :] == experts
    second = ids[1:2, :] == experts
    counts = first.astype(jnp.float32) + second.astype(jnp.float32)
    earlier = lax.broadcasted_iota(jnp.int32, (rows, rows), 0) < lax.broadcasted_iota(
        jnp.int32, (rows, rows), 1
    )
    before = jnp.dot(
        counts.astype(jnp.bfloat16),
        earlier.astype(jnp.float32).astype(jnp.bfloat16),
        preferred_element_type=jnp.float32,
    )
    codes = codes.astype(jnp.float32)
    weight = codes / (codes[0:1, :] + codes[1:2, :])
    keep_first = first & (before < capacity)
    keep_second = second & (before + first.astype(jnp.float32) < capacity)
    return jnp.where(keep_first, weight[0:1, :], 0.0) + jnp.where(
        keep_second, weight[1:2, :], 0.0
    )


def prepare_kernel(capacity, experts_n, ids, codes, up, down, columns, up_out, down_out, sems):
    copies = [
        pltpu.make_async_copy(up, up_out, sems.at[0]),
        pltpu.make_async_copy(down, down_out, sems.at[1]),
    ]
    for copy in copies:
        copy.start()
    me = lax.axis_index("expert")
    weight = kept_weights(ids[...], codes[...], experts_n, capacity)
    rows = weight.shape[1]
    index = lax.broadcasted_iota(jnp.int32, weight.shape, 0)
    diagonal = lax.broadcasted_iota(jnp.int32, (rows, rows), 0) == lax.broadcasted_iota(
        jnp.int32, (rows, rows), 1
    )
    for step in range(experts_n):
        mine = index == lax.rem(me + step, experts_n)
        row = jnp.sum(jnp.where(mine, weight, 0.0), axis=0, keepdims=True)
        column = jnp.sum(jnp.where(diagonal, row, 0.0), axis=1, keepdims=True)
        columns[step] = jnp.broadcast_to(column, columns.shape[1:])
    for copy in copies:
        copy.wait()


def local_call(
    kernel, out_shape, operands, others=(), in_specs=None, limit=4 * MIB, cost=0.5, **kwargs
):
    count = len(operands)

    name = getattr(kernel, "func", kernel).__name__

    def body_of(*refs):
        kernel(*refs[:count], *refs[count + len(others) :])

    return pl.pallas_call(
        body_of,
        name=name,
        out_shape=out_shape,
        in_specs=list(in_specs or [VMEM] * count) + [pl.BlockSpec(memory_space=pl.ANY)] * len(others),
        out_specs=jax.tree.map(lambda _: VMEM, out_shape),
        compiler_params=pltpu.CompilerParams(vmem_limit_bytes=limit),
        cost_estimate=pl.CostEstimate(
            flops=int(cost * 1.15e9), bytes_accessed=0, transcendentals=0
        ),
        **kwargs,
    )(*operands, *others)


def after(array, other):
    anywhere = pl.BlockSpec(memory_space=pl.ANY)
    return pl.pallas_call(
        lambda *refs: None,
        out_shape=jax.ShapeDtypeStruct(array.shape, array.dtype),
        in_specs=[anywhere, anywhere],
        out_specs=anywhere,
        input_output_aliases={0: 0},
        compiler_params=pltpu.CompilerParams(vmem_limit_bytes=MIB),
    )(array, other)


def prepare(ids, codes, up_t, down, experts_n, capacity):
    rows = ids.shape[1]
    return local_call(
        functools.partial(prepare_kernel, capacity, experts_n),
        [
            pltpu.VMEM((experts_n, rows, 128), jnp.float32),
            pltpu.VMEM(up_t.shape, up_t.dtype),
            pltpu.VMEM(down.shape, down.dtype),
        ],
        (ids, codes, up_t, down),
        in_specs=[VMEM, VMEM, HBM, HBM],
        scratch_shapes=[pltpu.SemaphoreType.DMA((2,))],
        limit=50 * MIB,
        cost=4,
    )


def pack_kernel(*refs):
    packed = refs[-1]
    rows, width = refs[0].shape
    for index, ref in enumerate(refs[:-1]):
        at, column = index // 2 * rows, index % 2 * width
        packed[at : at + rows, column : column + width] = ref[...]


def pack(pairs, others):
    rows, width = pairs[0][0].shape
    return local_call(
        pack_kernel,
        jax.ShapeDtypeStruct((len(pairs) * rows, 2 * width), pairs[0][0].dtype),
        [array for pair in pairs for array in pair],
        others,
    )


def expert_kernel(chip, core, up_t, down, keep, send, features, out):
    width = chip.shape[1] // 2
    place = lax.axis_index("tensor")

    def columns(bits):
        return pl.ds(pl.multiple_of((place ^ bits) * width, width), width)

    features[:, columns(0)] = chip[:, :width]
    features[:, columns(2)] = chip[:, width:]
    features[:, columns(1)] = core[:, :width]
    features[:, columns(3)] = core[:, width:]
    lifted = lax.dot_general(
        features[...], up_t[...], (((1,), (1,)), ((), ())), preferred_element_type=jnp.float32
    )
    hidden = (lifted / (1.0 + jnp.exp(-lifted))).astype(jnp.bfloat16)
    out[...] = jnp.dot(hidden, down[...], preferred_element_type=jnp.float32)
    keep[:, :width] = out[:, columns(0)]
    keep[:, width:] = out[:, columns(2)]
    send[:, :width] = out[:, columns(1)].astype(jnp.bfloat16)
    send[:, width:] = out[:, columns(3)].astype(jnp.bfloat16)


def expert_rows(chip, core, up_t, down, others):
    rows, model = chip.shape[0], up_t.shape[1]
    return local_call(
        expert_kernel,
        [
            jax.ShapeDtypeStruct(chip.shape, jnp.float32),
            jax.ShapeDtypeStruct(chip.shape, jnp.bfloat16),
        ],
        (chip, core, up_t, down),
        others,
        limit=10 * MIB,
        scratch_shapes=[
            pltpu.VMEM((rows, model), jnp.bfloat16),
            pltpu.VMEM((rows, model), jnp.float32),
        ],
        cost=2.6,
    )


def core_sum_kernel(keep, got, own, *sends):
    width = own.shape[1]
    own[...] = keep[:, :width] + got[:, :width].astype(jnp.float32)
    for index, send in enumerate(sends):
        rows = slice(index * send.shape[0], (index + 1) * send.shape[0])
        send[...] = (keep[rows, width:] + got[rows, width:].astype(jnp.float32)).astype(send.dtype)


def core_sum(keep, got, count, others):
    rows, width = keep.shape[0], keep.shape[1] // 2
    return local_call(
        core_sum_kernel,
        [jax.ShapeDtypeStruct((rows, width), jnp.float32)]
        + [jax.ShapeDtypeStruct((rows // count, width), jnp.bfloat16)] * count,
        (keep, got),
        others,
        cost=2,
    )


def chip_sum_kernel(index, own, got, part):
    rows = slice(index * got.shape[0], (index + 1) * got.shape[0])
    part[...] = (own[rows, :] + got[...].astype(jnp.float32)).astype(part.dtype)


def chip_sum(own, got, index, others):
    return local_call(
        functools.partial(chip_sum_kernel, index),
        jax.ShapeDtypeStruct(got.shape, jnp.bfloat16),
        (own, got),
        others,
        cost=2,
    )


def combine_kernel(columns, own, got, *rest):
    parts, mixed = rest[:-1], rest[-1]
    total = columns[0, :, 0:1] * (own[...] + got[...].astype(jnp.float32))
    for step, part in enumerate(parts, 1):
        total += columns[step, :, 0:1] * part[...].astype(jnp.float32)
    mixed[...] = total.astype(mixed.dtype)


def combine(columns, own, got, parts, others):
    return local_call(
        combine_kernel,
        jax.ShapeDtypeStruct(own.shape, jnp.bfloat16),
        (columns, own, got, *parts),
        others,
    )


def swap(array, bit):
    return lax.ppermute(array, "tensor", [(i, i ^ bit) for i in range(4)])


def whole_blocks(tokens, expert_ids, weight_codes, up_local, down_local, capacity):
    experts_n = lax.axis_size("expert")

    def shift(array, by):
        return lax.ppermute(
            array, "expert", [(i, (i + by) % experts_n) for i in range(experts_n)]
        )

    columns, up_t, down = prepare(
        expert_ids.T, weight_codes.T, up_local.T, down_local, experts_n, capacity
    )
    blocks, others, chips, kept, sums, added, parts = {}, {}, {}, {}, {}, {}, {}

    def arrive(step, source, by, waits):
        blocks[step] = shift(source, by) if step else tokens
        for wait in waits:
            blocks[step] = after(blocks[step], wait)
        others[step] = swap(blocks[step], 2)

    def lay(step, waits):
        chips[step] = pack([(blocks[step], others[step])], waits)

    def run(step, waits):
        kept[step] = expert_rows(chips[step], swap(chips[step], 1), up_t, down, waits)

    def leave(step, waits):
        keep, send = kept[step]
        own, away = core_sum(keep, swap(send, 1), 1, waits)
        sums[step] = own, swap(away, 2)

    def give(step, waits):
        added[step] = chip_sum(*sums[step], 0, waits)
        parts[step] = shift(added[step], -step)

    arrive(0, tokens, 0, [])
    arrive(1, tokens, 1, [columns])
    arrive(3, tokens, -1, [columns])
    lay(0, [blocks[1], blocks[3]])
    run(0, [])
    arrive(2, blocks[1], 1, [kept[0][0]])
    lay(1, [kept[0][0], blocks[2], others[3]])
    run(1, [])
    lay(3, [chips[1]])
    run(3, [kept[1][0]])
    lay(2, [kept[3][0]])
    leave(1, [])
    run(2, [sums[1][0], chips[2]])
    leave(3, [kept[2][0]])
    give(1, [sums[3][0]])
    leave(2, [added[1]])
    leave(0, [sums[2][0]])
    give(3, [sums[2][0]])
    give(2, [added[3]])
    return combine(columns, *sums[0], [parts[step] for step in range(1, experts_n)], ())


def slotted(tokens, expert_ids, weight_codes, up_local, down_local, capacity):
    rows, share_width = tokens.shape
    experts_n = lax.axis_size("expert")
    slots_n = experts_n * capacity
    flat_ids = expert_ids.reshape(rows * 2)
    onehot = (flat_ids[:, None] == jnp.arange(experts_n, dtype=jnp.int32)[None, :]).astype(
        jnp.int32
    )
    prior = jnp.cumsum(onehot, axis=0) - onehot
    slot = jnp.sum(prior * onehot, axis=1)
    target = jnp.where(slot < capacity, flat_ids * capacity + slot, -1)
    select = (jnp.arange(slots_n, dtype=jnp.int32)[:, None] == target[None, :]).astype(jnp.bfloat16)
    select = select.reshape(slots_n, rows, 2)
    gather_mat = jnp.sum(select, axis=2)
    sending = jnp.dot(gather_mat, tokens, preferred_element_type=jnp.float32).astype(jnp.bfloat16)
    sending = sending.reshape(experts_n, capacity, share_width)
    received = lax.all_to_all(sending, "expert", split_axis=0, concat_axis=0, tiled=True)
    received = received.reshape(slots_n, share_width)
    received = lax.all_gather(received, "tensor", axis=1, tiled=True)
    lifted = jnp.dot(received, up_local, preferred_element_type=jnp.float32)
    hidden = jax.nn.silu(lifted).astype(jnp.bfloat16)
    partial_out = jnp.dot(hidden, down_local, preferred_element_type=jnp.float32)
    total = lax.psum_scatter(
        partial_out.astype(jnp.bfloat16), "tensor", scatter_dimension=1, tiled=True
    )
    total = total.reshape(experts_n, capacity, share_width)
    returned = lax.all_to_all(total, "expert", split_axis=0, concat_axis=0, tiled=True)
    returned = returned.reshape(slots_n, share_width)
    picked = jnp.einsum("srk,sd->krd", select, returned, preferred_element_type=jnp.float32)
    codes = weight_codes.astype(jnp.float32)
    weight = codes / jnp.sum(codes, axis=1, keepdims=True)
    mixed = weight[:, 0:1] * picked[0] + weight[:, 1:2] * picked[1]
    return mixed.astype(jnp.bfloat16)


def body(tokens, expert_ids, weight_codes, up_weight, down_weight):
    rows = tokens.shape[0]
    capacity = 4 * rows // lax.axis_size("expert")
    whole = capacity >= rows and lax.axis_size("expert") == lax.axis_size("tensor") == 4
    plan = whole_blocks if whole else slotted
    return plan(tokens, expert_ids, weight_codes, up_weight[0], down_weight[0], capacity)


def solution(mesh):
    return jax.shard_map(
        body,
        mesh=mesh,
        in_specs=(
            P(("group", "expert"), "tensor"),
            P(("group", "expert"), None),
            P(("group", "expert"), None),
            P("expert", None, "tensor"),
            P("expert", "tensor", None),
        ),
        out_specs=P(("group", "expert"), "tensor"),
        check_vma=False,
    )
```

```python
import functools

import jax
import jax.numpy as jnp
from jax import lax
from jax.experimental import pallas as pl
from jax.experimental.pallas import tpu as pltpu
from jax.sharding import PartitionSpec as P


MIB = 1 << 20
HBM = pl.BlockSpec(memory_space=pltpu.HBM)
VMEM = pl.BlockSpec(memory_space=pltpu.VMEM)


def kept_weights(ids, codes, experts_n, capacity):
    rows = ids.shape[1]
    experts = lax.broadcasted_iota(jnp.int32, (experts_n, rows), 0)
    first = ids[0:1, :] == experts
    second = ids[1:2, :] == experts
    counts = first.astype(jnp.float32) + second.astype(jnp.float32)
    earlier = lax.broadcasted_iota(jnp.int32, (rows, rows), 0) < lax.broadcasted_iota(
        jnp.int32, (rows, rows), 1
    )
    before = jnp.dot(
        counts.astype(jnp.bfloat16),
        earlier.astype(jnp.float32).astype(jnp.bfloat16),
        preferred_element_type=jnp.float32,
    )
    codes = codes.astype(jnp.float32)
    weight = codes / (codes[0:1, :] + codes[1:2, :])
    keep_first = first & (before < capacity)
    keep_second = second & (before + first.astype(jnp.float32) < capacity)
    return jnp.where(keep_first, weight[0:1, :], 0.0) + jnp.where(
        keep_second, weight[1:2, :], 0.0
    )


def prepare_kernel(capacity, experts_n, ids, codes, up, down, columns, up_out, down_out, sems):
    copies = [
        pltpu.make_async_copy(up, up_out, sems.at[0]),
        pltpu.make_async_copy(down, down_out, sems.at[1]),
    ]
    for copy in copies:
        copy.start()
    me = lax.axis_index("expert")
    weight = kept_weights(ids[...], codes[...], experts_n, capacity)
    rows = weight.shape[1]
    index = lax.broadcasted_iota(jnp.int32, weight.shape, 0)
    diagonal = lax.broadcasted_iota(jnp.int32, (rows, rows), 0) == lax.broadcasted_iota(
        jnp.int32, (rows, rows), 1
    )
    for step in range(experts_n):
        mine = index == lax.rem(me + step, experts_n)
        row = jnp.sum(jnp.where(mine, weight, 0.0), axis=0, keepdims=True)
        column = jnp.sum(jnp.where(diagonal, row, 0.0), axis=1, keepdims=True)
        columns[step] = jnp.broadcast_to(column, columns.shape[1:])
    for copy in copies:
        copy.wait()


def local_call(
    kernel, out_shape, operands, others=(), in_specs=None, limit=4 * MIB, cost=0.5, **kwargs
):
    count = len(operands)

    name = getattr(kernel, "func", kernel).__name__

    def body_of(*refs):
        kernel(*refs[:count], *refs[count + len(others) :])

    return pl.pallas_call(
        body_of,
        name=name,
        out_shape=out_shape,
        in_specs=list(in_specs or [VMEM] * count) + [pl.BlockSpec(memory_space=pl.ANY)] * len(others),
        out_specs=jax.tree.map(lambda _: VMEM, out_shape),
        compiler_params=pltpu.CompilerParams(vmem_limit_bytes=limit),
        cost_estimate=pl.CostEstimate(
            flops=int(cost * 1.15e9), bytes_accessed=0, transcendentals=0
        ),
        **kwargs,
    )(*operands, *others)


def after(array, other):
    anywhere = pl.BlockSpec(memory_space=pl.ANY)
    return pl.pallas_call(
        lambda *refs: None,
        out_shape=jax.ShapeDtypeStruct(array.shape, array.dtype),
        in_specs=[anywhere, anywhere],
        out_specs=anywhere,
        input_output_aliases={0: 0},
        compiler_params=pltpu.CompilerParams(vmem_limit_bytes=MIB),
    )(array, other)


def prepare(ids, codes, up_t, down, experts_n, capacity):
    rows = ids.shape[1]
    return local_call(
        functools.partial(prepare_kernel, capacity, experts_n),
        [
            pltpu.VMEM((experts_n, rows, 128), jnp.float32),
            pltpu.VMEM(up_t.shape, up_t.dtype),
            pltpu.VMEM(down.shape, down.dtype),
        ],
        (ids, codes, up_t, down),
        in_specs=[VMEM, VMEM, HBM, HBM],
        scratch_shapes=[pltpu.SemaphoreType.DMA((2,))],
        limit=50 * MIB,
        cost=4,
    )


def pack_kernel(*refs):
    packed = refs[-1]
    rows, width = refs[0].shape
    for index, ref in enumerate(refs[:-1]):
        at, column = index // 2 * rows, index % 2 * width
        packed[at : at + rows, column : column + width] = ref[...]


def pack(pairs, others, cost):
    rows, width = pairs[0][0].shape
    return local_call(
        pack_kernel,
        jax.ShapeDtypeStruct((len(pairs) * rows, 2 * width), pairs[0][0].dtype),
        [array for pair in pairs for array in pair],
        others,
        cost=cost,
    )


def expert_kernel(chip, core, up_t, down, keep, send, features, out):
    width = chip.shape[1] // 2
    place = lax.axis_index("tensor")

    def columns(bits):
        return pl.ds(pl.multiple_of((place ^ bits) * width, width), width)

    features[:, columns(0)] = chip[:, :width]
    features[:, columns(2)] = chip[:, width:]
    features[:, columns(1)] = core[:, :width]
    features[:, columns(3)] = core[:, width:]
    lifted = lax.dot_general(
        features[...], up_t[...], (((1,), (1,)), ((), ())), preferred_element_type=jnp.float32
    )
    hidden = (lifted / (1.0 + jnp.exp(-lifted))).astype(jnp.bfloat16)
    out[...] = jnp.dot(hidden, down[...], preferred_element_type=jnp.float32)
    keep[:, :width] = out[:, columns(0)]
    keep[:, width:] = out[:, columns(2)]
    send[:, :width] = out[:, columns(1)].astype(jnp.bfloat16)
    send[:, width:] = out[:, columns(3)].astype(jnp.bfloat16)


def expert_rows(chip, core, up_t, down, others):
    rows, model = chip.shape[0], up_t.shape[1]
    return local_call(
        expert_kernel,
        [
            jax.ShapeDtypeStruct(chip.shape, jnp.float32),
            jax.ShapeDtypeStruct(chip.shape, jnp.bfloat16),
        ],
        (chip, core, up_t, down),
        others,
        limit=10 * MIB,
        scratch_shapes=[
            pltpu.VMEM((rows, model), jnp.bfloat16),
            pltpu.VMEM((rows, model), jnp.float32),
        ],
        cost=2.6,
    )


def core_sum_kernel(keep, got, own, *sends):
    width = own.shape[1]
    own[...] = keep[:, :width] + got[:, :width].astype(jnp.float32)
    for index, send in enumerate(sends):
        rows = slice(index * send.shape[0], (index + 1) * send.shape[0])
        send[...] = (keep[rows, width:] + got[rows, width:].astype(jnp.float32)).astype(send.dtype)


def core_sum(keep, got, count, others):
    rows, width = keep.shape[0], keep.shape[1] // 2
    return local_call(
        core_sum_kernel,
        [jax.ShapeDtypeStruct((rows, width), jnp.float32)]
        + [jax.ShapeDtypeStruct((rows // count, width), jnp.bfloat16)] * count,
        (keep, got),
        others,
        cost=2,
    )


def chip_sum_kernel(index, own, got, part):
    rows = slice(index * got.shape[0], (index + 1) * got.shape[0])
    part[...] = (own[rows, :] + got[...].astype(jnp.float32)).astype(part.dtype)


def chip_sum(own, got, index, others):
    return local_call(
        functools.partial(chip_sum_kernel, index),
        jax.ShapeDtypeStruct(got.shape, jnp.bfloat16),
        (own, got),
        others,
        cost=2,
    )


def weigh_kernel(steps, columns, own, got, *rest):
    parts, out = rest[:-1], rest[-1]
    for at in range(0, out.shape[1], 128):
        here = slice(at, at + 128)
        total = own[:, here]
        if got is not None:
            total = columns[0] * (total + got[:, here].astype(jnp.float32))
        for step, part in zip(steps, parts):
            total = total + columns[step] * part[:, here].astype(jnp.float32)
        out[:, here] = total.astype(out.dtype)


def weigh(columns, own, got, steps, parts):
    return local_call(
        functools.partial(weigh_kernel, steps),
        jax.ShapeDtypeStruct(own.shape, jnp.float32),
        (columns, own, got, *parts),
    )


def finish_kernel(steps, columns, total, *rest):
    weigh_kernel(steps, columns, total, None, *rest)


def finish(columns, total, steps, parts):
    return local_call(
        functools.partial(finish_kernel, steps),
        jax.ShapeDtypeStruct(total.shape, jnp.bfloat16),
        (columns, total, *parts),
    )


def swap(array, bit):
    return lax.ppermute(array, "tensor", [(i, i ^ bit) for i in range(4)])


def whole_blocks(tokens, expert_ids, weight_codes, up_local, down_local, capacity):
    experts_n = lax.axis_size("expert")

    def shift(array, by):
        return lax.ppermute(
            array, "expert", [(i, (i + by) % experts_n) for i in range(experts_n)]
        )

    columns, up_t, down = prepare(
        expert_ids.T, weight_codes.T, up_local.T, down_local, experts_n, capacity
    )
    blocks, others, chips, kept, sums, added, parts = {}, {}, {}, {}, {}, {}, {}

    def arrive(step, source, by, waits):
        blocks[step] = shift(source, by) if step else tokens
        for wait in waits:
            blocks[step] = after(blocks[step], wait)
        others[step] = swap(blocks[step], 2)

    def lay(steps, waits, cost=0.5):
        chips[steps] = pack([(blocks[step], others[step]) for step in steps], waits, cost)

    def run(steps, waits):
        chip = chips[steps]
        kept[steps] = expert_rows(chip, swap(chip, 1), up_t, down, waits)

    def leave(steps, waits):
        keep, send = kept[steps]
        own, *aways = core_sum(keep, swap(send, 1), len(steps), waits)
        for index, step in enumerate(steps):
            sums[step] = own, swap(aways[index], 2), index

    def give(step, waits):
        added[step] = chip_sum(*sums[step], waits)
        parts[step] = shift(added[step], -step)

    arrive(0, tokens, 0, [])
    arrive(1, tokens, 1, [columns])
    arrive(3, tokens, -1, [columns])
    lay((0,), [blocks[1], blocks[3]])
    run((0,), [])
    arrive(2, blocks[1], 1, [kept[0,][0]])
    lay((1, 3), [kept[0,][0], blocks[2]])
    run((1, 3), [])
    lay((2,), [kept[1, 3][0]], cost=4)
    leave((1, 3), [chips[2,]])
    run((2,), [sums[1][0]])
    give(1, [kept[2,][0]])
    leave((2,), [added[1]])
    leave((0,), [sums[2][0]])
    give(3, [sums[2][0]])
    give(2, [added[3]])
    total = weigh(columns, *sums[0][:2], (1,), [parts[1]])
    return finish(columns, total, (3, 2), [parts[3], parts[2]])


def slotted(tokens, expert_ids, weight_codes, up_local, down_local, capacity):
    rows, share_width = tokens.shape
    experts_n = lax.axis_size("expert")
    slots_n = experts_n * capacity
    flat_ids = expert_ids.reshape(rows * 2)
    onehot = (flat_ids[:, None] == jnp.arange(experts_n, dtype=jnp.int32)[None, :]).astype(
        jnp.int32
    )
    prior = jnp.cumsum(onehot, axis=0) - onehot
    slot = jnp.sum(prior * onehot, axis=1)
    target = jnp.where(slot < capacity, flat_ids * capacity + slot, -1)
    select = (jnp.arange(slots_n, dtype=jnp.int32)[:, None] == target[None, :]).astype(jnp.bfloat16)
    select = select.reshape(slots_n, rows, 2)
    gather_mat = jnp.sum(select, axis=2)
    sending = jnp.dot(gather_mat, tokens, preferred_element_type=jnp.float32).astype(jnp.bfloat16)
    sending = sending.reshape(experts_n, capacity, share_width)
    received = lax.all_to_all(sending, "expert", split_axis=0, concat_axis=0, tiled=True)
    received = received.reshape(slots_n, share_width)
    received = lax.all_gather(received, "tensor", axis=1, tiled=True)
    lifted = jnp.dot(received, up_local, preferred_element_type=jnp.float32)
    hidden = jax.nn.silu(lifted).astype(jnp.bfloat16)
    partial_out = jnp.dot(hidden, down_local, preferred_element_type=jnp.float32)
    total = lax.psum_scatter(
        partial_out.astype(jnp.bfloat16), "tensor", scatter_dimension=1, tiled=True
    )
    total = total.reshape(experts_n, capacity, share_width)
    returned = lax.all_to_all(total, "expert", split_axis=0, concat_axis=0, tiled=True)
    returned = returned.reshape(slots_n, share_width)
    picked = jnp.einsum("srk,sd->krd", select, returned, preferred_element_type=jnp.float32)
    codes = weight_codes.astype(jnp.float32)
    weight = codes / jnp.sum(codes, axis=1, keepdims=True)
    mixed = weight[:, 0:1] * picked[0] + weight[:, 1:2] * picked[1]
    return mixed.astype(jnp.bfloat16)


def body(tokens, expert_ids, weight_codes, up_weight, down_weight):
    rows = tokens.shape[0]
    capacity = 4 * rows // lax.axis_size("expert")
    whole = capacity >= rows and lax.axis_size("expert") == lax.axis_size("tensor") == 4
    plan = whole_blocks if whole else slotted
    return plan(tokens, expert_ids, weight_codes, up_weight[0], down_weight[0], capacity)


def solution(mesh):
    return jax.shard_map(
        body,
        mesh=mesh,
        in_specs=(
            P(("group", "expert"), "tensor"),
            P(("group", "expert"), None),
            P(("group", "expert"), None),
            P("expert", None, "tensor"),
            P("expert", "tensor", None),
        ),
        out_specs=P(("group", "expert"), "tensor"),
        check_vma=False,
    )
```

```python
import functools

import jax
import jax.numpy as jnp
from jax import lax
from jax.experimental import pallas as pl
from jax.experimental.pallas import tpu as pltpu
from jax.sharding import PartitionSpec as P


MIB = 1 << 20
HBM = pl.BlockSpec(memory_space=pltpu.HBM)
VMEM = pl.BlockSpec(memory_space=pltpu.VMEM)


def kept_weights(ids, codes, experts_n, capacity):
    rows = ids.shape[1]
    experts = lax.broadcasted_iota(jnp.int32, (experts_n, rows), 0)
    first = ids[0:1, :] == experts
    second = ids[1:2, :] == experts
    counts = first.astype(jnp.float32) + second.astype(jnp.float32)
    earlier = lax.broadcasted_iota(jnp.int32, (rows, rows), 0) < lax.broadcasted_iota(
        jnp.int32, (rows, rows), 1
    )
    before = jnp.dot(
        counts.astype(jnp.bfloat16),
        earlier.astype(jnp.float32).astype(jnp.bfloat16),
        preferred_element_type=jnp.float32,
    )
    codes = codes.astype(jnp.float32)
    weight = codes / (codes[0:1, :] + codes[1:2, :])
    keep_first = first & (before < capacity)
    keep_second = second & (before + first.astype(jnp.float32) < capacity)
    return jnp.where(keep_first, weight[0:1, :], 0.0) + jnp.where(
        keep_second, weight[1:2, :], 0.0
    )


def prepare_kernel(capacity, experts_n, ids, codes, up, down, columns, up_out, down_out, sems):
    copies = [
        pltpu.make_async_copy(up, up_out, sems.at[0]),
        pltpu.make_async_copy(down, down_out, sems.at[1]),
    ]
    for copy in copies:
        copy.start()
    me = lax.axis_index("expert")
    weight = kept_weights(ids[...], codes[...], experts_n, capacity)
    rows = weight.shape[1]
    index = lax.broadcasted_iota(jnp.int32, weight.shape, 0)
    diagonal = lax.broadcasted_iota(jnp.int32, (rows, rows), 0) == lax.broadcasted_iota(
        jnp.int32, (rows, rows), 1
    )
    for step in range(experts_n):
        mine = index == lax.rem(me + step, experts_n)
        row = jnp.sum(jnp.where(mine, weight, 0.0), axis=0, keepdims=True)
        column = jnp.sum(jnp.where(diagonal, row, 0.0), axis=1, keepdims=True)
        columns[step] = jnp.broadcast_to(column, columns.shape[1:])
    for copy in copies:
        copy.wait()


def local_call(
    kernel, out_shape, operands, others=(), in_specs=None, limit=4 * MIB, cost=0.5, **kwargs
):
    count = len(operands)

    name = getattr(kernel, "func", kernel).__name__

    def body_of(*refs):
        kernel(*refs[:count], *refs[count + len(others) :])

    return pl.pallas_call(
        body_of,
        name=name,
        out_shape=out_shape,
        in_specs=list(in_specs or [VMEM] * count) + [pl.BlockSpec(memory_space=pl.ANY)] * len(others),
        out_specs=jax.tree.map(lambda _: VMEM, out_shape),
        compiler_params=pltpu.CompilerParams(vmem_limit_bytes=limit),
        cost_estimate=pl.CostEstimate(
            flops=int(cost * 1.15e9), bytes_accessed=0, transcendentals=0
        ),
        **kwargs,
    )(*operands, *others)


def after(array, other):
    anywhere = pl.BlockSpec(memory_space=pl.ANY)
    return pl.pallas_call(
        lambda *refs: None,
        out_shape=jax.ShapeDtypeStruct(array.shape, array.dtype),
        in_specs=[anywhere, anywhere],
        out_specs=anywhere,
        input_output_aliases={0: 0},
        compiler_params=pltpu.CompilerParams(vmem_limit_bytes=MIB),
    )(array, other)


def prepare(ids, codes, up_t, down, experts_n, capacity):
    rows = ids.shape[1]
    return local_call(
        functools.partial(prepare_kernel, capacity, experts_n),
        [
            pltpu.VMEM((experts_n, rows, 128), jnp.float32),
            pltpu.VMEM(up_t.shape, up_t.dtype),
            pltpu.VMEM(down.shape, down.dtype),
        ],
        (ids, codes, up_t, down),
        in_specs=[VMEM, VMEM, HBM, HBM],
        scratch_shapes=[pltpu.SemaphoreType.DMA((2,))],
        limit=50 * MIB,
        cost=4,
    )


def pack_kernel(*refs):
    packed = refs[-1]
    rows, width = refs[0].shape
    for index, ref in enumerate(refs[:-1]):
        at, column = index // 2 * rows, index % 2 * width
        packed[at : at + rows, column : column + width] = ref[...]


def pack(pairs, others, cost):
    rows, width = pairs[0][0].shape
    return local_call(
        pack_kernel,
        jax.ShapeDtypeStruct((len(pairs) * rows, 2 * width), pairs[0][0].dtype),
        [array for pair in pairs for array in pair],
        others,
        cost=cost,
    )


def expert_kernel(chip, core, up_t, down, keep, send, features, out):
    width = chip.shape[1] // 2
    place = lax.axis_index("tensor")

    def columns(bits):
        return pl.ds(pl.multiple_of((place ^ bits) * width, width), width)

    features[:, columns(0)] = chip[:, :width]
    features[:, columns(2)] = chip[:, width:]
    features[:, columns(1)] = core[:, :width]
    features[:, columns(3)] = core[:, width:]
    lifted = lax.dot_general(
        features[...], up_t[...], (((1,), (1,)), ((), ())), preferred_element_type=jnp.float32
    )
    hidden = (lifted / (1.0 + jnp.exp(-lifted))).astype(jnp.bfloat16)
    out[...] = jnp.dot(hidden, down[...], preferred_element_type=jnp.float32)
    keep[:, :width] = out[:, columns(0)]
    keep[:, width:] = out[:, columns(2)]
    send[:, :width] = out[:, columns(1)].astype(jnp.bfloat16)
    send[:, width:] = out[:, columns(3)].astype(jnp.bfloat16)


def expert_rows(chip, core, up_t, down, others, cost):
    rows, model = chip.shape[0], up_t.shape[1]
    return local_call(
        expert_kernel,
        [
            jax.ShapeDtypeStruct(chip.shape, jnp.float32),
            jax.ShapeDtypeStruct(chip.shape, jnp.bfloat16),
        ],
        (chip, core, up_t, down),
        others,
        limit=10 * MIB,
        scratch_shapes=[
            pltpu.VMEM((rows, model), jnp.bfloat16),
            pltpu.VMEM((rows, model), jnp.float32),
        ],
        cost=cost,
    )


def core_sum_kernel(keep, got, own, *sends):
    width = own.shape[1]
    own[...] = keep[:, :width] + got[:, :width].astype(jnp.float32)
    for index, send in enumerate(sends):
        rows = slice(index * send.shape[0], (index + 1) * send.shape[0])
        send[...] = (keep[rows, width:] + got[rows, width:].astype(jnp.float32)).astype(send.dtype)


def core_sum(keep, got, count, others, cost):
    rows, width = keep.shape[0], keep.shape[1] // 2
    return local_call(
        core_sum_kernel,
        [jax.ShapeDtypeStruct((rows, width), jnp.float32)]
        + [jax.ShapeDtypeStruct((rows // count, width), jnp.bfloat16)] * count,
        (keep, got),
        others,
        cost=cost,
    )


def chip_sum_kernel(index, own, got, part):
    rows = slice(index * got.shape[0], (index + 1) * got.shape[0])
    part[...] = (own[rows, :] + got[...].astype(jnp.float32)).astype(part.dtype)


def chip_sum(own, got, index, others, cost):
    return local_call(
        functools.partial(chip_sum_kernel, index),
        jax.ShapeDtypeStruct(got.shape, jnp.bfloat16),
        (own, got),
        others,
        cost=cost,
    )


def weigh_kernel(steps, columns, own, got, *rest):
    parts, out = rest[:-1], rest[-1]
    for at in range(0, out.shape[1], 128):
        here = slice(at, at + 128)
        total = own[:, here]
        if got is not None:
            total = columns[0] * (total + got[:, here].astype(jnp.float32))
        for step, part in zip(steps, parts):
            total = total + columns[step] * part[:, here].astype(jnp.float32)
        out[:, here] = total.astype(out.dtype)


def weigh(columns, own, got, steps, parts):
    return local_call(
        functools.partial(weigh_kernel, steps),
        jax.ShapeDtypeStruct(own.shape, jnp.float32),
        (columns, own, got, *parts),
        cost=4,
    )


def finish_kernel(steps, columns, total, *rest):
    weigh_kernel(steps, columns, total, None, *rest)


def finish(columns, total, steps, parts):
    return local_call(
        functools.partial(finish_kernel, steps),
        jax.ShapeDtypeStruct(total.shape, jnp.bfloat16),
        (columns, total, *parts),
    )


def swap(array, bit):
    return lax.ppermute(array, "tensor", [(i, i ^ bit) for i in range(4)])


def whole_blocks(tokens, expert_ids, weight_codes, up_local, down_local, capacity):
    experts_n = lax.axis_size("expert")

    def shift(array, by):
        return lax.ppermute(
            array, "expert", [(i, (i + by) % experts_n) for i in range(experts_n)]
        )

    columns, up_t, down = prepare(
        expert_ids.T, weight_codes.T, up_local.T, down_local, experts_n, capacity
    )
    blocks, others, chips, kept, sums, added, parts = {}, {}, {}, {}, {}, {}, {}

    def arrive(step, source, by, waits):
        blocks[step] = shift(source, by) if step else tokens
        for wait in waits:
            blocks[step] = after(blocks[step], wait)
        others[step] = swap(blocks[step], 2)

    def lay(steps, waits, cost=0.5):
        chips[steps] = pack([(blocks[step], others[step]) for step in steps], waits, cost)

    def run(steps, waits, cost):
        chip = chips[steps]
        kept[steps] = expert_rows(chip, swap(chip, 1), up_t, down, waits, cost)

    def leave(steps, waits, cost=2):
        keep, send = kept[steps]
        own, *aways = core_sum(keep, swap(send, 1), len(steps), waits, cost)
        for index, step in enumerate(steps):
            sums[step] = own, swap(aways[index], 2), index

    def give(step, waits, cost=2):
        added[step] = chip_sum(*sums[step], waits, cost)
        parts[step] = shift(added[step], -step)

    arrive(0, tokens, 0, [])
    arrive(1, tokens, 1, [columns])
    arrive(3, tokens, -1, [columns])
    lay((0,), [blocks[1], blocks[3]])
    run((0,), [], 2.6)
    arrive(2, blocks[1], 1, [kept[0,][0]])
    lay((1,), [kept[0,][0], blocks[2]])
    run((1,), [], 4)
    lay((3,), [kept[1,][0]], .5)
    lay((2,), [chips[3,]], 4)
    leave((1,), [chips[2,]], 2)
    run((3,), [sums[1][0]], 4)
    run((2,), [kept[3,][0]], .05)
    give(1, [kept[2,][0]], 2)
    leave((3,), [added[1]], 4)
    leave((2,), [sums[3][0]], 2)
    leave((0,), [sums[2][0]])
    give(3, [sums[2][0]], 4)
    give(2, [added[3]], 4)
    total = weigh(columns, *sums[0][:2], (1, 3), [parts[1], parts[3]])
    return finish(columns, total, (2,), [parts[2]])


def slotted(tokens, expert_ids, weight_codes, up_local, down_local, capacity):
    rows, share_width = tokens.shape
    experts_n = lax.axis_size("expert")
    slots_n = experts_n * capacity
    flat_ids = expert_ids.reshape(rows * 2)
    onehot = (flat_ids[:, None] == jnp.arange(experts_n, dtype=jnp.int32)[None, :]).astype(
        jnp.int32
    )
    prior = jnp.cumsum(onehot, axis=0) - onehot
    slot = jnp.sum(prior * onehot, axis=1)
    target = jnp.where(slot < capacity, flat_ids * capacity + slot, -1)
    select = (jnp.arange(slots_n, dtype=jnp.int32)[:, None] == target[None, :]).astype(jnp.bfloat16)
    select = select.reshape(slots_n, rows, 2)
    gather_mat = jnp.sum(select, axis=2)
    sending = jnp.dot(gather_mat, tokens, preferred_element_type=jnp.float32).astype(jnp.bfloat16)
    sending = sending.reshape(experts_n, capacity, share_width)
    received = lax.all_to_all(sending, "expert", split_axis=0, concat_axis=0, tiled=True)
    received = received.reshape(slots_n, share_width)
    received = lax.all_gather(received, "tensor", axis=1, tiled=True)
    lifted = jnp.dot(received, up_local, preferred_element_type=jnp.float32)
    hidden = jax.nn.silu(lifted).astype(jnp.bfloat16)
    partial_out = jnp.dot(hidden, down_local, preferred_element_type=jnp.float32)
    total = lax.psum_scatter(
        partial_out.astype(jnp.bfloat16), "tensor", scatter_dimension=1, tiled=True
    )
    total = total.reshape(experts_n, capacity, share_width)
    returned = lax.all_to_all(total, "expert", split_axis=0, concat_axis=0, tiled=True)
    returned = returned.reshape(slots_n, share_width)
    picked = jnp.einsum("srk,sd->krd", select, returned, preferred_element_type=jnp.float32)
    codes = weight_codes.astype(jnp.float32)
    weight = codes / jnp.sum(codes, axis=1, keepdims=True)
    mixed = weight[:, 0:1] * picked[0] + weight[:, 1:2] * picked[1]
    return mixed.astype(jnp.bfloat16)


def body(tokens, expert_ids, weight_codes, up_weight, down_weight):
    rows = tokens.shape[0]
    capacity = 4 * rows // lax.axis_size("expert")
    whole = capacity >= rows and lax.axis_size("expert") == lax.axis_size("tensor") == 4
    plan = whole_blocks if whole else slotted
    return plan(tokens, expert_ids, weight_codes, up_weight[0], down_weight[0], capacity)


def solution(mesh):
    return jax.shard_map(
        body,
        mesh=mesh,
        in_specs=(
            P(("group", "expert"), "tensor"),
            P(("group", "expert"), None),
            P(("group", "expert"), None),
            P("expert", None, "tensor"),
            P("expert", "tensor", None),
        ),
        out_specs=P(("group", "expert"), "tensor"),
        check_vma=False,
    )
```

```python
import functools

import jax
import jax.numpy as jnp
from jax import lax
from jax.experimental import pallas as pl
from jax.experimental.pallas import tpu as pltpu
from jax.sharding import PartitionSpec as P


MIB = 1 << 20
HBM = pl.BlockSpec(memory_space=pltpu.HBM)
VMEM = pl.BlockSpec(memory_space=pltpu.VMEM)


def kept_weights(ids, codes, experts_n, capacity):
    rows = ids.shape[1]
    experts = lax.broadcasted_iota(jnp.int32, (experts_n, rows), 0)
    first = ids[0:1, :] == experts
    second = ids[1:2, :] == experts
    counts = first.astype(jnp.float32) + second.astype(jnp.float32)
    earlier = lax.broadcasted_iota(jnp.int32, (rows, rows), 0) < lax.broadcasted_iota(
        jnp.int32, (rows, rows), 1
    )
    before = jnp.dot(
        counts.astype(jnp.bfloat16),
        earlier.astype(jnp.float32).astype(jnp.bfloat16),
        preferred_element_type=jnp.float32,
    )
    codes = codes.astype(jnp.float32)
    weight = codes / (codes[0:1, :] + codes[1:2, :])
    keep_first = first & (before < capacity)
    keep_second = second & (before + first.astype(jnp.float32) < capacity)
    return jnp.where(keep_first, weight[0:1, :], 0.0) + jnp.where(
        keep_second, weight[1:2, :], 0.0
    )


def prepare_kernel(capacity, experts_n, ids, codes, up, down, columns, up_out, down_out, sems):
    copies = [
        pltpu.make_async_copy(up, up_out, sems.at[0]),
        pltpu.make_async_copy(down, down_out, sems.at[1]),
    ]
    for copy in copies:
        copy.start()
    me = lax.axis_index("expert")
    weight = kept_weights(ids[...], codes[...], experts_n, capacity)
    rows = weight.shape[1]
    index = lax.broadcasted_iota(jnp.int32, weight.shape, 0)
    diagonal = lax.broadcasted_iota(jnp.int32, (rows, rows), 0) == lax.broadcasted_iota(
        jnp.int32, (rows, rows), 1
    )
    for step in range(experts_n):
        mine = index == lax.rem(me + step, experts_n)
        row = jnp.sum(jnp.where(mine, weight, 0.0), axis=0, keepdims=True)
        column = jnp.sum(jnp.where(diagonal, row, 0.0), axis=1, keepdims=True)
        columns[step] = jnp.broadcast_to(column, columns.shape[1:])
    for copy in copies:
        copy.wait()


def local_call(
    kernel, out_shape, operands, others=(), in_specs=None, limit=4 * MIB, cost=0.5, **kwargs
):
    count = len(operands)

    name = getattr(kernel, "func", kernel).__name__

    def body_of(*refs):
        kernel(*refs[:count], *refs[count + len(others) :])

    return pl.pallas_call(
        body_of,
        name=name,
        out_shape=out_shape,
        in_specs=list(in_specs or [VMEM] * count) + [pl.BlockSpec(memory_space=pl.ANY)] * len(others),
        out_specs=jax.tree.map(lambda _: VMEM, out_shape),
        compiler_params=pltpu.CompilerParams(vmem_limit_bytes=limit),
        cost_estimate=pl.CostEstimate(
            flops=int(cost * 1.15e9), bytes_accessed=0, transcendentals=0
        ),
        **kwargs,
    )(*operands, *others)


def after(array, other):
    anywhere = pl.BlockSpec(memory_space=pl.ANY)
    return pl.pallas_call(
        lambda *refs: None,
        out_shape=jax.ShapeDtypeStruct(array.shape, array.dtype),
        in_specs=[anywhere, anywhere],
        out_specs=anywhere,
        input_output_aliases={0: 0},
        compiler_params=pltpu.CompilerParams(vmem_limit_bytes=MIB),
    )(array, other)


def prepare(ids, codes, up_t, down, experts_n, capacity):
    rows = ids.shape[1]
    return local_call(
        functools.partial(prepare_kernel, capacity, experts_n),
        [
            pltpu.VMEM((experts_n, rows, 128), jnp.float32),
            pltpu.VMEM(up_t.shape, up_t.dtype),
            pltpu.VMEM(down.shape, down.dtype),
        ],
        (ids, codes, up_t, down),
        in_specs=[VMEM, VMEM, HBM, HBM],
        scratch_shapes=[pltpu.SemaphoreType.DMA((2,))],
        limit=50 * MIB,
        cost=4,
    )


def pack_kernel(*refs):
    packed = refs[-1]
    rows, width = refs[0].shape
    for index, ref in enumerate(refs[:-1]):
        at, column = index // 2 * rows, index % 2 * width
        packed[at : at + rows, column : column + width] = ref[...]


def pack(pairs, others, cost):
    rows, width = pairs[0][0].shape
    return local_call(
        pack_kernel,
        jax.ShapeDtypeStruct((len(pairs) * rows, 2 * width), pairs[0][0].dtype),
        [array for pair in pairs for array in pair],
        others,
        cost=cost,
    )


def expert_kernel(chip, core, up_t, down, keep, near, away, features, out):
    width = chip.shape[1] // 2
    place = lax.axis_index("tensor")

    def columns(bits):
        return pl.ds(pl.multiple_of((place ^ bits) * width, width), width)

    features[:, columns(0)] = chip[:, :width]
    features[:, columns(2)] = chip[:, width:]
    features[:, columns(1)] = core[:, :width]
    features[:, columns(3)] = core[:, width:]
    lifted = lax.dot_general(
        features[...], up_t[...], (((1,), (1,)), ((), ())), preferred_element_type=jnp.float32
    )
    hidden = (lifted / (1.0 + jnp.exp(-lifted))).astype(jnp.bfloat16)
    out[...] = jnp.dot(hidden, down[...], preferred_element_type=jnp.float32)
    keep[:, :width] = out[:, columns(0)]
    keep[:, width:] = out[:, columns(2)]
    near[...] = out[:, columns(1)].astype(jnp.bfloat16)
    away[...] = out[:, columns(3)].astype(jnp.bfloat16)


def expert_rows(chip, core, up_t, down, others, cost):
    rows, width, model = chip.shape[0], chip.shape[1] // 2, up_t.shape[1]
    return local_call(
        expert_kernel,
        [
            jax.ShapeDtypeStruct(chip.shape, jnp.float32),
            jax.ShapeDtypeStruct((rows, width), jnp.bfloat16),
            jax.ShapeDtypeStruct((rows, width), jnp.bfloat16),
        ],
        (chip, core, up_t, down),
        others,
        limit=10 * MIB,
        scratch_shapes=[
            pltpu.VMEM((rows, model), jnp.bfloat16),
            pltpu.VMEM((rows, model), jnp.float32),
        ],
        cost=cost,
    )


def core_sum_kernel(keep, got, away):
    width = away.shape[1]
    away[...] = (keep[:, width:] + got[...].astype(jnp.float32)).astype(away.dtype)


def core_sum(keep, got, others, cost):
    return local_call(
        core_sum_kernel, jax.ShapeDtypeStruct(got.shape, jnp.bfloat16), (keep, got), others, cost=cost
    )


def chip_sum_kernel(keep, near, far, *parts):
    rows, width = parts[0].shape
    for index, part in enumerate(parts):
        here = slice(index * rows, (index + 1) * rows)
        total = keep[here, :width] + near[here, :].astype(jnp.float32)
        part[...] = (total + far[here, :].astype(jnp.float32)).astype(part.dtype)


def chip_sum(keep, near, far, count, others, cost):
    shape = near.shape[0] // count, near.shape[1]
    return local_call(
        chip_sum_kernel,
        [jax.ShapeDtypeStruct(shape, jnp.bfloat16)] * count,
        (keep, near, far),
        others,
        cost=cost,
    )


def weigh_kernel(steps, counts, columns, *refs):
    refs, out = list(refs[:-1]), refs[-1]
    for at in range(0, out.shape[1], 128):
        here = slice(at, at + 128)
        left = list(refs)
        total = left.pop(0)[:, here] if len(left) > sum(counts) else None
        for step, count in zip(steps, counts):
            rows = sum(left.pop(0)[:, here].astype(jnp.float32) for _ in range(count))
            rows = columns[step] * rows
            total = rows if total is None else total + rows
        out[:, here] = total.astype(out.dtype)


def weigh(columns, totals, steps, terms, dtype, cost):
    arrays = [*totals, *[array for term in terms for array in term]]
    return local_call(
        functools.partial(weigh_kernel, steps, [len(term) for term in terms]),
        jax.ShapeDtypeStruct(arrays[-1].shape, dtype),
        (columns, *arrays),
        cost=cost,
    )


def swap(array, bit):
    return lax.ppermute(array, "tensor", [(i, i ^ bit) for i in range(4)])


def whole_blocks(tokens, expert_ids, weight_codes, up_local, down_local, capacity):
    experts_n = lax.axis_size("expert")

    def shift(array, by):
        return lax.ppermute(
            array, "expert", [(i, (i + by) % experts_n) for i in range(experts_n)]
        )

    columns, up_t, down = prepare(
        expert_ids.T, weight_codes.T, up_local.T, down_local, experts_n, capacity
    )
    blocks, others, chips, kept, left, sums, added, parts = {}, {}, {}, {}, {}, {}, {}, {}

    def arrive(step, source, by, waits):
        blocks[step] = shift(source, by) if step else tokens
        for wait in waits:
            blocks[step] = after(blocks[step], wait)
        others[step] = swap(blocks[step], 2)

    def lay(steps, waits, cost=0.5):
        chips[steps] = pack([(blocks[step], others[step]) for step in steps], waits, cost)

    def run(steps, waits, cost):
        chip = chips[steps]
        kept[steps] = expert_rows(chip, swap(chip, 1), up_t, down, waits, cost)

    def leave(steps, waits, cost):
        keep, near, away = kept[steps]
        left[steps] = core_sum(keep, swap(away, 1), waits, cost)
        sums[steps] = keep, swap(near, 1), swap(left[steps], 2)

    def give(steps, waits, cost):
        added[steps] = chip_sum(*sums[steps], len(steps), waits, cost)
        for step, part in zip(steps, added[steps]):
            parts[step] = shift(part, -step)

    arrive(0, tokens, 0, [])
    arrive(1, tokens, 1, [columns])
    arrive(3, tokens, -1, [columns])
    lay((0,), [blocks[1], blocks[3]])
    run((0,), [], 2.6)
    arrive(2, blocks[1], 1, [kept[0,][0]])
    lay((1, 3), [kept[0,][0], blocks[2]])
    run((1, 3), [], 2.6)
    lay((2,), [kept[1, 3][0]], cost=4)
    leave((1, 3), [chips[2,]], 2)
    run((2,), [left[1, 3]], .05)
    leave((2,), [kept[2,][0]], .05)
    give((1, 3), [left[2,]], 2)
    if False:
        leave((0,), [added[1, 3][0]], 2)
        give((2,), [left[0,]], 2)
    else:
        give((2,), [added[1, 3][0]], 2)
        leave((0,), [added[2,][0]], 2)
    total = weigh(columns, [], (1, 3), [[parts[1]], [parts[3]]], jnp.float32, 4)
    total = weigh(columns, [total], (0,), [sums[0,]], jnp.float32, 4)
    return weigh(columns, [total], (2,), [[parts[2]]], jnp.bfloat16, 0.5)


def slotted(tokens, expert_ids, weight_codes, up_local, down_local, capacity):
    rows, share_width = tokens.shape
    experts_n = lax.axis_size("expert")
    slots_n = experts_n * capacity
    flat_ids = expert_ids.reshape(rows * 2)
    onehot = (flat_ids[:, None] == jnp.arange(experts_n, dtype=jnp.int32)[None, :]).astype(
        jnp.int32
    )
    prior = jnp.cumsum(onehot, axis=0) - onehot
    slot = jnp.sum(prior * onehot, axis=1)
    target = jnp.where(slot < capacity, flat_ids * capacity + slot, -1)
    select = (jnp.arange(slots_n, dtype=jnp.int32)[:, None] == target[None, :]).astype(jnp.bfloat16)
    select = select.reshape(slots_n, rows, 2)
    gather_mat = jnp.sum(select, axis=2)
    sending = jnp.dot(gather_mat, tokens, preferred_element_type=jnp.float32).astype(jnp.bfloat16)
    sending = sending.reshape(experts_n, capacity, share_width)
    received = lax.all_to_all(sending, "expert", split_axis=0, concat_axis=0, tiled=True)
    received = received.reshape(slots_n, share_width)
    received = lax.all_gather(received, "tensor", axis=1, tiled=True)
    lifted = jnp.dot(received, up_local, preferred_element_type=jnp.float32)
    hidden = jax.nn.silu(lifted).astype(jnp.bfloat16)
    partial_out = jnp.dot(hidden, down_local, preferred_element_type=jnp.float32)
    total = lax.psum_scatter(
        partial_out.astype(jnp.bfloat16), "tensor", scatter_dimension=1, tiled=True
    )
    total = total.reshape(experts_n, capacity, share_width)
    returned = lax.all_to_all(total, "expert", split_axis=0, concat_axis=0, tiled=True)
    returned = returned.reshape(slots_n, share_width)
    picked = jnp.einsum("srk,sd->krd", select, returned, preferred_element_type=jnp.float32)
    codes = weight_codes.astype(jnp.float32)
    weight = codes / jnp.sum(codes, axis=1, keepdims=True)
    mixed = weight[:, 0:1] * picked[0] + weight[:, 1:2] * picked[1]
    return mixed.astype(jnp.bfloat16)


def body(tokens, expert_ids, weight_codes, up_weight, down_weight):
    rows = tokens.shape[0]
    capacity = 4 * rows // lax.axis_size("expert")
    whole = capacity >= rows and lax.axis_size("expert") == lax.axis_size("tensor") == 4
    plan = whole_blocks if whole else slotted
    return plan(tokens, expert_ids, weight_codes, up_weight[0], down_weight[0], capacity)


def solution(mesh):
    return jax.shard_map(
        body,
        mesh=mesh,
        in_specs=(
            P(("group", "expert"), "tensor"),
            P(("group", "expert"), None),
            P(("group", "expert"), None),
            P("expert", None, "tensor"),
            P("expert", "tensor", None),
        ),
        out_specs=P(("group", "expert"), "tensor"),
        check_vma=False,
    )
```

```python
import functools

import jax
import jax.numpy as jnp
from jax import lax
from jax.experimental import pallas as pl
from jax.experimental.pallas import tpu as pltpu
from jax.sharding import PartitionSpec as P


MIB = 1 << 20
HBM = pl.BlockSpec(memory_space=pltpu.HBM)
VMEM = pl.BlockSpec(memory_space=pltpu.VMEM)


def kept_weights(ids, codes, experts_n, capacity):
    rows = ids.shape[1]
    experts = lax.broadcasted_iota(jnp.int32, (experts_n, rows), 0)
    first = ids[0:1, :] == experts
    second = ids[1:2, :] == experts
    counts = first.astype(jnp.float32) + second.astype(jnp.float32)
    earlier = lax.broadcasted_iota(jnp.int32, (rows, rows), 0) < lax.broadcasted_iota(
        jnp.int32, (rows, rows), 1
    )
    before = jnp.dot(
        counts.astype(jnp.bfloat16),
        earlier.astype(jnp.float32).astype(jnp.bfloat16),
        preferred_element_type=jnp.float32,
    )
    codes = codes.astype(jnp.float32)
    weight = codes / (codes[0:1, :] + codes[1:2, :])
    keep_first = first & (before < capacity)
    keep_second = second & (before + first.astype(jnp.float32) < capacity)
    return jnp.where(keep_first, weight[0:1, :], 0.0) + jnp.where(
        keep_second, weight[1:2, :], 0.0
    )


def prepare_kernel(
    capacity, experts_n, ids, codes, tokens, up, down, columns, copy_out, up_out, down_out, sems
):
    copies = [
        pltpu.make_async_copy(up, up_out, sems.at[0]),
        pltpu.make_async_copy(down, down_out, sems.at[1]),
    ]
    for copy in copies:
        copy.start()
    copy_out[...] = tokens[...]
    me = lax.axis_index("expert")
    weight = kept_weights(ids[...], codes[...], experts_n, capacity)
    rows = weight.shape[1]
    index = lax.broadcasted_iota(jnp.int32, weight.shape, 0)
    diagonal = lax.broadcasted_iota(jnp.int32, (rows, rows), 0) == lax.broadcasted_iota(
        jnp.int32, (rows, rows), 1
    )
    for step in range(experts_n):
        mine = index == lax.rem(me + step, experts_n)
        row = jnp.sum(jnp.where(mine, weight, 0.0), axis=0, keepdims=True)
        column = jnp.sum(jnp.where(diagonal, row, 0.0), axis=1, keepdims=True)
        columns[step] = jnp.broadcast_to(column, columns.shape[1:])
    for copy in copies:
        copy.wait()


def local_call(
    kernel, out_shape, operands, others=(), in_specs=None, limit=4 * MIB, cost=0.5, **kwargs
):
    count = len(operands)

    name = getattr(kernel, "func", kernel).__name__

    def body_of(*refs):
        kernel(*refs[:count], *refs[count + len(others) :])

    return pl.pallas_call(
        body_of,
        name=name,
        out_shape=out_shape,
        in_specs=list(in_specs or [VMEM] * count) + [pl.BlockSpec(memory_space=pl.ANY)] * len(others),
        out_specs=jax.tree.map(lambda _: VMEM, out_shape),
        compiler_params=pltpu.CompilerParams(vmem_limit_bytes=limit),
        cost_estimate=pl.CostEstimate(
            flops=int(cost * 1.15e9), bytes_accessed=0, transcendentals=0
        ),
        **kwargs,
    )(*operands, *others)


def after(array, other):
    anywhere = pl.BlockSpec(memory_space=pl.ANY)
    return pl.pallas_call(
        lambda *refs: None,
        out_shape=jax.ShapeDtypeStruct(array.shape, array.dtype),
        in_specs=[anywhere, anywhere],
        out_specs=anywhere,
        input_output_aliases={0: 0},
        compiler_params=pltpu.CompilerParams(vmem_limit_bytes=MIB),
    )(array, other)


def prepare(ids, codes, tokens, up_t, down, experts_n, capacity):
    rows = ids.shape[1]
    return local_call(
        functools.partial(prepare_kernel, capacity, experts_n),
        [
            pltpu.VMEM((experts_n, rows, 128), jnp.float32),
            pltpu.VMEM(tokens.shape, tokens.dtype),
            pltpu.VMEM(up_t.shape, up_t.dtype),
            pltpu.VMEM(down.shape, down.dtype),
        ],
        (ids, codes, tokens, up_t, down),
        in_specs=[VMEM, VMEM, VMEM, HBM, HBM],
        scratch_shapes=[pltpu.SemaphoreType.DMA((2,))],
        limit=50 * MIB,
        cost=4,
    )


def pack_kernel(*refs):
    packed = refs[-1]
    rows, width = refs[0].shape
    for index, ref in enumerate(refs[:-1]):
        at, column = index // 2 * rows, index % 2 * width
        packed[at : at + rows, column : column + width] = ref[...]


def pack(pairs, others, cost):
    rows, width = pairs[0][0].shape
    return local_call(
        pack_kernel,
        jax.ShapeDtypeStruct((len(pairs) * rows, 2 * width), pairs[0][0].dtype),
        [array for pair in pairs for array in pair],
        others,
        cost=cost,
    )


def expert_kernel(chip, core, up_t, down, keep, send, features, out):
    width = chip.shape[1] // 2
    place = lax.axis_index("tensor")

    def columns(bits):
        return pl.ds(pl.multiple_of((place ^ bits) * width, width), width)

    features[:, columns(0)] = chip[:, :width]
    features[:, columns(2)] = chip[:, width:]
    features[:, columns(1)] = core[:, :width]
    features[:, columns(3)] = core[:, width:]
    lifted = lax.dot_general(
        features[...], up_t[...], (((1,), (1,)), ((), ())), preferred_element_type=jnp.float32
    )
    hidden = (lifted / (1.0 + jnp.exp(-lifted))).astype(jnp.bfloat16)
    out[...] = jnp.dot(hidden, down[...], preferred_element_type=jnp.float32)
    keep[:, :width] = out[:, columns(0)]
    keep[:, width:] = out[:, columns(2)]
    send[:, :width] = out[:, columns(1)].astype(jnp.bfloat16)
    send[:, width:] = out[:, columns(3)].astype(jnp.bfloat16)


def expert_rows(chip, core, up_t, down, others, cost):
    rows, model = chip.shape[0], up_t.shape[1]
    return local_call(
        expert_kernel,
        [
            jax.ShapeDtypeStruct(chip.shape, jnp.float32),
            jax.ShapeDtypeStruct(chip.shape, jnp.bfloat16),
        ],
        (chip, core, up_t, down),
        others,
        limit=10 * MIB,
        scratch_shapes=[
            pltpu.VMEM((rows, model), jnp.bfloat16),
            pltpu.VMEM((rows, model), jnp.float32),
        ],
        cost=cost,
    )


def core_sum_kernel(keep, got, own, *sends):
    width = own.shape[1]
    own[...] = keep[:, :width] + got[:, :width].astype(jnp.float32)
    for index, send in enumerate(sends):
        rows = slice(index * send.shape[0], (index + 1) * send.shape[0])
        send[...] = (keep[rows, width:] + got[rows, width:].astype(jnp.float32)).astype(send.dtype)


def core_sum(keep, got, count, others, cost):
    rows, width = keep.shape[0], keep.shape[1] // 2
    return local_call(
        core_sum_kernel,
        [jax.ShapeDtypeStruct((rows, width), jnp.float32)]
        + [jax.ShapeDtypeStruct((rows // count, width), jnp.bfloat16)] * count,
        (keep, got),
        others,
        cost=cost,
    )


def chip_sum_kernel(index, own, got, part):
    rows = slice(index * got.shape[0], (index + 1) * got.shape[0])
    part[...] = (own[rows, :] + got[...].astype(jnp.float32)).astype(part.dtype)


def chip_sum(own, got, index, others, cost):
    return local_call(
        functools.partial(chip_sum_kernel, index),
        jax.ShapeDtypeStruct(got.shape, jnp.bfloat16),
        (own, got),
        others,
        cost=cost,
    )


def weigh_kernel(steps, columns, own, got, *rest):
    parts, out = rest[:-1], rest[-1]
    for at in range(0, out.shape[1], 128):
        here = slice(at, at + 128)
        total = own[:, here]
        if got is not None:
            total = columns[0] * (total + got[:, here].astype(jnp.float32))
        for step, part in zip(steps, parts):
            total = total + columns[step] * part[:, here].astype(jnp.float32)
        out[:, here] = total.astype(out.dtype)


def weigh(columns, own, got, steps, parts):
    return local_call(
        functools.partial(weigh_kernel, steps),
        jax.ShapeDtypeStruct(own.shape, jnp.float32),
        (columns, own, got, *parts),
        cost=4,
    )


def finish_kernel(steps, columns, total, *rest):
    weigh_kernel(steps, columns, total, None, *rest)


def finish(columns, total, steps, parts):
    return local_call(
        functools.partial(finish_kernel, steps),
        jax.ShapeDtypeStruct(total.shape, jnp.bfloat16),
        (columns, total, *parts),
    )


def swap(array, bit):
    return lax.ppermute(array, "tensor", [(i, i ^ bit) for i in range(4)])


def whole_blocks(tokens, expert_ids, weight_codes, up_local, down_local, capacity):
    experts_n = lax.axis_size("expert")

    def shift(array, by):
        return lax.ppermute(
            array, "expert", [(i, (i + by) % experts_n) for i in range(experts_n)]
        )

    columns, copied, up_t, down = prepare(
        expert_ids.T, weight_codes.T, tokens, up_local.T, down_local, experts_n, capacity
    )
    blocks, others, chips, kept, sums, added, parts = {}, {}, {}, {}, {}, {}, {}

    def arrive(step, source, by, waits):
        blocks[step] = shift(source, by) if step else tokens
        for wait in waits:
            blocks[step] = after(blocks[step], wait)
        others[step] = swap(blocks[step], 2)

    def lay(steps, waits, cost=0.5):
        chips[steps] = pack([(blocks[step], others[step]) for step in steps], waits, cost)

    def run(steps, waits, cost):
        chip = chips[steps]
        kept[steps] = expert_rows(chip, swap(chip, 1), up_t, down, waits, cost)

    def leave(steps, waits, cost=2):
        keep, send = kept[steps]
        own, *aways = core_sum(keep, swap(send, 1), len(steps), waits, cost)
        for index, step in enumerate(steps):
            sums[step] = own, swap(aways[index], 2), index

    def give(step, waits, cost=2):
        added[step] = chip_sum(*sums[step], waits, cost)
        parts[step] = shift(added[step], -step)

    arrive(0, tokens, 0, [])
    arrive(1, tokens, 1, [columns])
    lay((0,), [blocks[1]])
    run((0,), [], 2.6)
    arrive(2, blocks[1], 1, [kept[0,][0]])
    arrive(3, after(copied, chips[0,]), -1, [kept[0,][0]])
    lay((1,), [blocks[2], blocks[3]], .5)
    run((1,), [], 4)
    lay((2,), [kept[1,][0]], 4)
    leave((1,), [chips[2,]], 2)
    run((2,), [sums[1][0]], 4)
    lay((3,), [kept[2,][0]], 4)
    leave((2,), [chips[3,]], 4)
    run((3,), [sums[2][0]], 4)
    give(1, [kept[3,][0]], 4)
    leave((3,), [added[1]], 4)
    give(2, [sums[3][0]], 2)
    give(3, [added[2]], 2)
    leave((0,), [added[3]], 2)
    total = weigh(columns, *sums[0][:2], (1, 2), [parts[1], parts[2]])
    return finish(columns, total, (3,), [parts[3]])


def slotted(tokens, expert_ids, weight_codes, up_local, down_local, capacity):
    rows, share_width = tokens.shape
    experts_n = lax.axis_size("expert")
    slots_n = experts_n * capacity
    flat_ids = expert_ids.reshape(rows * 2)
    onehot = (flat_ids[:, None] == jnp.arange(experts_n, dtype=jnp.int32)[None, :]).astype(
        jnp.int32
    )
    prior = jnp.cumsum(onehot, axis=0) - onehot
    slot = jnp.sum(prior * onehot, axis=1)
    target = jnp.where(slot < capacity, flat_ids * capacity + slot, -1)
    select = (jnp.arange(slots_n, dtype=jnp.int32)[:, None] == target[None, :]).astype(jnp.bfloat16)
    select = select.reshape(slots_n, rows, 2)
    gather_mat = jnp.sum(select, axis=2)
    sending = jnp.dot(gather_mat, tokens, preferred_element_type=jnp.float32).astype(jnp.bfloat16)
    sending = sending.reshape(experts_n, capacity, share_width)
    received = lax.all_to_all(sending, "expert", split_axis=0, concat_axis=0, tiled=True)
    received = received.reshape(slots_n, share_width)
    received = lax.all_gather(received, "tensor", axis=1, tiled=True)
    lifted = jnp.dot(received, up_local, preferred_element_type=jnp.float32)
    hidden = jax.nn.silu(lifted).astype(jnp.bfloat16)
    partial_out = jnp.dot(hidden, down_local, preferred_element_type=jnp.float32)
    total = lax.psum_scatter(
        partial_out.astype(jnp.bfloat16), "tensor", scatter_dimension=1, tiled=True
    )
    total = total.reshape(experts_n, capacity, share_width)
    returned = lax.all_to_all(total, "expert", split_axis=0, concat_axis=0, tiled=True)
    returned = returned.reshape(slots_n, share_width)
    picked = jnp.einsum("srk,sd->krd", select, returned, preferred_element_type=jnp.float32)
    codes = weight_codes.astype(jnp.float32)
    weight = codes / jnp.sum(codes, axis=1, keepdims=True)
    mixed = weight[:, 0:1] * picked[0] + weight[:, 1:2] * picked[1]
    return mixed.astype(jnp.bfloat16)


def body(tokens, expert_ids, weight_codes, up_weight, down_weight):
    rows = tokens.shape[0]
    capacity = 4 * rows // lax.axis_size("expert")
    whole = capacity >= rows and lax.axis_size("expert") == lax.axis_size("tensor") == 4
    plan = whole_blocks if whole else slotted
    return plan(tokens, expert_ids, weight_codes, up_weight[0], down_weight[0], capacity)


def solution(mesh):
    return jax.shard_map(
        body,
        mesh=mesh,
        in_specs=(
            P(("group", "expert"), "tensor"),
            P(("group", "expert"), None),
            P(("group", "expert"), None),
            P("expert", None, "tensor"),
            P("expert", "tensor", None),
        ),
        out_specs=P(("group", "expert"), "tensor"),
        check_vma=False,
    )
```

```python
import functools

import jax
import jax.numpy as jnp
from jax import lax
from jax.experimental import pallas as pl
from jax.experimental.pallas import tpu as pltpu
from jax.sharding import PartitionSpec as P


MIB = 1 << 20
HBM = pl.BlockSpec(memory_space=pltpu.HBM)
VMEM = pl.BlockSpec(memory_space=pltpu.VMEM)


def kept_weights(ids, codes, experts_n, capacity):
    rows = ids.shape[1]
    experts = lax.broadcasted_iota(jnp.int32, (experts_n, rows), 0)
    first = ids[0:1, :] == experts
    second = ids[1:2, :] == experts
    counts = first.astype(jnp.float32) + second.astype(jnp.float32)
    earlier = lax.broadcasted_iota(jnp.int32, (rows, rows), 0) < lax.broadcasted_iota(
        jnp.int32, (rows, rows), 1
    )
    before = jnp.dot(
        counts.astype(jnp.bfloat16),
        earlier.astype(jnp.float32).astype(jnp.bfloat16),
        preferred_element_type=jnp.float32,
    )
    codes = codes.astype(jnp.float32)
    weight = codes / (codes[0:1, :] + codes[1:2, :])
    keep_first = first & (before < capacity)
    keep_second = second & (before + first.astype(jnp.float32) < capacity)
    return jnp.where(keep_first, weight[0:1, :], 0.0) + jnp.where(
        keep_second, weight[1:2, :], 0.0
    )


def prepare_kernel(capacity, experts_n, ids, codes, up, down, columns, up_out, down_out, sems):
    copies = [
        pltpu.make_async_copy(up, up_out, sems.at[0]),
        pltpu.make_async_copy(down, down_out, sems.at[1]),
    ]
    for copy in copies:
        copy.start()
    me = lax.axis_index("expert")
    weight = kept_weights(ids[...], codes[...], experts_n, capacity)
    rows = weight.shape[1]
    index = lax.broadcasted_iota(jnp.int32, weight.shape, 0)
    diagonal = lax.broadcasted_iota(jnp.int32, (rows, rows), 0) == lax.broadcasted_iota(
        jnp.int32, (rows, rows), 1
    )
    for step in range(experts_n):
        mine = index == lax.rem(me + step, experts_n)
        row = jnp.sum(jnp.where(mine, weight, 0.0), axis=0, keepdims=True)
        column = jnp.sum(jnp.where(diagonal, row, 0.0), axis=1, keepdims=True)
        columns[step] = jnp.broadcast_to(column, columns.shape[1:])
    for copy in copies:
        copy.wait()


def local_call(
    kernel, out_shape, operands, others=(), in_specs=None, limit=4 * MIB, cost=0.5, **kwargs
):
    count = len(operands)

    name = getattr(kernel, "func", kernel).__name__

    def body_of(*refs):
        kernel(*refs[:count], *refs[count + len(others) :])

    return pl.pallas_call(
        body_of,
        name=name,
        out_shape=out_shape,
        in_specs=list(in_specs or [VMEM] * count) + [pl.BlockSpec(memory_space=pl.ANY)] * len(others),
        out_specs=jax.tree.map(lambda _: VMEM, out_shape),
        compiler_params=pltpu.CompilerParams(vmem_limit_bytes=limit),
        cost_estimate=pl.CostEstimate(
            flops=int(cost * 1.15e9), bytes_accessed=0, transcendentals=0
        ),
        **kwargs,
    )(*operands, *others)


def after(array, other):
    anywhere = pl.BlockSpec(memory_space=pl.ANY)
    return pl.pallas_call(
        lambda *refs: None,
        out_shape=jax.ShapeDtypeStruct(array.shape, array.dtype),
        in_specs=[anywhere, anywhere],
        out_specs=anywhere,
        input_output_aliases={0: 0},
        compiler_params=pltpu.CompilerParams(vmem_limit_bytes=MIB),
    )(array, other)


def prepare(ids, codes, up_t, down, experts_n, capacity):
    rows = ids.shape[1]
    return local_call(
        functools.partial(prepare_kernel, capacity, experts_n),
        [
            pltpu.VMEM((experts_n, rows, 128), jnp.float32),
            pltpu.VMEM(up_t.shape, up_t.dtype),
            pltpu.VMEM(down.shape, down.dtype),
        ],
        (ids, codes, up_t, down),
        in_specs=[VMEM, VMEM, HBM, HBM],
        scratch_shapes=[pltpu.SemaphoreType.DMA((2,))],
        limit=50 * MIB,
        cost=4,
    )


def pack_kernel(*refs):
    packed = refs[-1]
    rows, width = refs[0].shape
    for index, ref in enumerate(refs[:-1]):
        at, column = index // 2 * rows, index % 2 * width
        packed[at : at + rows, column : column + width] = ref[...]


def pack(pairs, others, cost):
    rows, width = pairs[0][0].shape
    return local_call(
        pack_kernel,
        jax.ShapeDtypeStruct((len(pairs) * rows, 2 * width), pairs[0][0].dtype),
        [array for pair in pairs for array in pair],
        others,
        cost=cost,
    )


def expert_kernel(chip, core, up_t, down, keep, send, features, out):
    width = chip.shape[1] // 2
    place = lax.axis_index("tensor")

    def columns(bits):
        return pl.ds(pl.multiple_of((place ^ bits) * width, width), width)

    features[:, columns(0)] = chip[:, :width]
    features[:, columns(2)] = chip[:, width:]
    features[:, columns(1)] = core[:, :width]
    features[:, columns(3)] = core[:, width:]
    lifted = lax.dot_general(
        features[...], up_t[...], (((1,), (1,)), ((), ())), preferred_element_type=jnp.float32
    )
    hidden = (lifted / (1.0 + jnp.exp(-lifted))).astype(jnp.bfloat16)
    out[...] = jnp.dot(hidden, down[...], preferred_element_type=jnp.float32)
    keep[:, :width] = out[:, columns(0)]
    keep[:, width:] = out[:, columns(2)]
    send[:, :width] = out[:, columns(1)].astype(jnp.bfloat16)
    send[:, width:] = out[:, columns(3)].astype(jnp.bfloat16)


def expert_rows(chip, core, up_t, down, others, cost):
    rows, model = chip.shape[0], up_t.shape[1]
    return local_call(
        expert_kernel,
        [
            jax.ShapeDtypeStruct(chip.shape, jnp.float32),
            jax.ShapeDtypeStruct(chip.shape, jnp.bfloat16),
        ],
        (chip, core, up_t, down),
        others,
        limit=10 * MIB,
        scratch_shapes=[
            pltpu.VMEM((rows, model), jnp.bfloat16),
            pltpu.VMEM((rows, model), jnp.float32),
        ],
        cost=cost,
    )


def core_sum_kernel(keep, got, own, *sends):
    width = own.shape[1]
    own[...] = keep[:, :width] + got[:, :width].astype(jnp.float32)
    for index, send in enumerate(sends):
        rows = slice(index * send.shape[0], (index + 1) * send.shape[0])
        send[...] = (keep[rows, width:] + got[rows, width:].astype(jnp.float32)).astype(send.dtype)


def core_sum(keep, got, count, others, cost):
    rows, width = keep.shape[0], keep.shape[1] // 2
    return local_call(
        core_sum_kernel,
        [jax.ShapeDtypeStruct((rows, width), jnp.float32)]
        + [jax.ShapeDtypeStruct((rows // count, width), jnp.bfloat16)] * count,
        (keep, got),
        others,
        cost=cost,
    )


def chip_sum_kernel(index, own, got, part):
    rows = slice(index * got.shape[0], (index + 1) * got.shape[0])
    part[...] = (own[rows, :] + got[...].astype(jnp.float32)).astype(part.dtype)


def chip_sum(own, got, index, others, cost):
    return local_call(
        functools.partial(chip_sum_kernel, index),
        jax.ShapeDtypeStruct(got.shape, jnp.bfloat16),
        (own, got),
        others,
        cost=cost,
    )


def weigh_kernel(steps, columns, own, got, *rest):
    parts, out = rest[:-1], rest[-1]
    for at in range(0, out.shape[1], 128):
        here = slice(at, at + 128)
        total = own[:, here]
        if got is not None:
            total = columns[0] * (total + got[:, here].astype(jnp.float32))
        for step, part in zip(steps, parts):
            total = total + columns[step] * part[:, here].astype(jnp.float32)
        out[:, here] = total.astype(out.dtype)


def weigh(columns, own, got, steps, parts):
    return local_call(
        functools.partial(weigh_kernel, steps),
        jax.ShapeDtypeStruct(own.shape, jnp.float32),
        (columns, own, got, *parts),
        cost=4,
    )


def finish_kernel(steps, columns, total, *rest):
    weigh_kernel(steps, columns, total, None, *rest)


def finish(columns, total, steps, parts):
    return local_call(
        functools.partial(finish_kernel, steps),
        jax.ShapeDtypeStruct(total.shape, jnp.bfloat16),
        (columns, total, *parts),
    )


def swap(array, bit):
    return lax.ppermute(array, "tensor", [(i, i ^ bit) for i in range(4)])


def whole_blocks(tokens, expert_ids, weight_codes, up_local, down_local, capacity):
    experts_n = lax.axis_size("expert")

    def shift(array, by):
        return lax.ppermute(
            array, "expert", [(i, (i + by) % experts_n) for i in range(experts_n)]
        )

    columns, up_t, down = prepare(
        expert_ids.T, weight_codes.T, up_local.T, down_local, experts_n, capacity
    )
    blocks, others, chips, kept, sums, added, parts = {}, {}, {}, {}, {}, {}, {}

    def arrive(step, source, by, waits):
        blocks[step] = shift(source, by) if step else tokens
        for wait in waits:
            blocks[step] = after(blocks[step], wait)
        others[step] = swap(blocks[step], 2)

    def lay(steps, waits, cost=0.5):
        chips[steps] = pack([(blocks[step], others[step]) for step in steps], waits, cost)

    def run(steps, waits, cost):
        chip = chips[steps]
        kept[steps] = expert_rows(chip, swap(chip, 1), up_t, down, waits, cost)

    def leave(steps, waits, cost=2):
        keep, send = kept[steps]
        own, *aways = core_sum(keep, swap(send, 1), len(steps), waits, cost)
        for index, step in enumerate(steps):
            sums[step] = own, swap(aways[index], 2), index

    def give(step, waits, cost=2):
        added[step] = chip_sum(*sums[step], waits, cost)
        parts[step] = shift(added[step], -step)

    arrive(0, tokens, 0, [])
    arrive(1, tokens, 1, [columns])
    lay((0,), [blocks[1]])
    chips[3,] = shift(chips[0,], -1)
    run((0,), [], 2.6)
    arrive(2, blocks[1], 1, [kept[0,][0]])
    lay((1,), [blocks[2]], .5)
    run((1,), [], 8)
    run((3,), [kept[1,][0]], 8)
    lay((2,), [kept[3,][0]], 8)
    leave((1,), [chips[2,]], 2)
    run((2,), [sums[1][0]], 2.6)
    leave((3,), [kept[2,][0]], 2)
    give(1, [sums[3][0]], 2)
    leave((2,), [added[1]], 2)
    leave((0,), [sums[2][0]], 2)
    give(3, [sums[2][0]], 2)
    give(2, [added[3]], 2)
    total = weigh(columns, *sums[0][:2], (1, 3), [parts[1], parts[3]])
    return finish(columns, total, (2,), [parts[2]])


def slotted(tokens, expert_ids, weight_codes, up_local, down_local, capacity):
    rows, share_width = tokens.shape
    experts_n = lax.axis_size("expert")
    slots_n = experts_n * capacity
    flat_ids = expert_ids.reshape(rows * 2)
    onehot = (flat_ids[:, None] == jnp.arange(experts_n, dtype=jnp.int32)[None, :]).astype(
        jnp.int32
    )
    prior = jnp.cumsum(onehot, axis=0) - onehot
    slot = jnp.sum(prior * onehot, axis=1)
    target = jnp.where(slot < capacity, flat_ids * capacity + slot, -1)
    select = (jnp.arange(slots_n, dtype=jnp.int32)[:, None] == target[None, :]).astype(jnp.bfloat16)
    select = select.reshape(slots_n, rows, 2)
    gather_mat = jnp.sum(select, axis=2)
    sending = jnp.dot(gather_mat, tokens, preferred_element_type=jnp.float32).astype(jnp.bfloat16)
    sending = sending.reshape(experts_n, capacity, share_width)
    received = lax.all_to_all(sending, "expert", split_axis=0, concat_axis=0, tiled=True)
    received = received.reshape(slots_n, share_width)
    received = lax.all_gather(received, "tensor", axis=1, tiled=True)
    lifted = jnp.dot(received, up_local, preferred_element_type=jnp.float32)
    hidden = jax.nn.silu(lifted).astype(jnp.bfloat16)
    partial_out = jnp.dot(hidden, down_local, preferred_element_type=jnp.float32)
    total = lax.psum_scatter(
        partial_out.astype(jnp.bfloat16), "tensor", scatter_dimension=1, tiled=True
    )
    total = total.reshape(experts_n, capacity, share_width)
    returned = lax.all_to_all(total, "expert", split_axis=0, concat_axis=0, tiled=True)
    returned = returned.reshape(slots_n, share_width)
    picked = jnp.einsum("srk,sd->krd", select, returned, preferred_element_type=jnp.float32)
    codes = weight_codes.astype(jnp.float32)
    weight = codes / jnp.sum(codes, axis=1, keepdims=True)
    mixed = weight[:, 0:1] * picked[0] + weight[:, 1:2] * picked[1]
    return mixed.astype(jnp.bfloat16)


def body(tokens, expert_ids, weight_codes, up_weight, down_weight):
    rows = tokens.shape[0]
    capacity = 4 * rows // lax.axis_size("expert")
    whole = capacity >= rows and lax.axis_size("expert") == lax.axis_size("tensor") == 4
    plan = whole_blocks if whole else slotted
    return plan(tokens, expert_ids, weight_codes, up_weight[0], down_weight[0], capacity)


def solution(mesh):
    return jax.shard_map(
        body,
        mesh=mesh,
        in_specs=(
            P(("group", "expert"), "tensor"),
            P(("group", "expert"), None),
            P(("group", "expert"), None),
            P("expert", None, "tensor"),
            P("expert", "tensor", None),
        ),
        out_specs=P(("group", "expert"), "tensor"),
        check_vma=False,
    )
```

```python
import functools

import jax
import jax.numpy as jnp
from jax import lax
from jax.experimental import pallas as pl
from jax.experimental.pallas import tpu as pltpu
from jax.sharding import PartitionSpec as P


MIB = 1 << 20
HBM = pl.BlockSpec(memory_space=pltpu.HBM)
VMEM = pl.BlockSpec(memory_space=pltpu.VMEM)


def kept_weights(ids, codes, experts_n, capacity):
    rows = ids.shape[1]
    experts = lax.broadcasted_iota(jnp.int32, (experts_n, rows), 0)
    first = ids[0:1, :] == experts
    second = ids[1:2, :] == experts
    counts = first.astype(jnp.float32) + second.astype(jnp.float32)
    earlier = lax.broadcasted_iota(jnp.int32, (rows, rows), 0) < lax.broadcasted_iota(
        jnp.int32, (rows, rows), 1
    )
    before = jnp.dot(
        counts.astype(jnp.bfloat16),
        earlier.astype(jnp.float32).astype(jnp.bfloat16),
        preferred_element_type=jnp.float32,
    )
    codes = codes.astype(jnp.float32)
    weight = codes / (codes[0:1, :] + codes[1:2, :])
    keep_first = first & (before < capacity)
    keep_second = second & (before + first.astype(jnp.float32) < capacity)
    return jnp.where(keep_first, weight[0:1, :], 0.0) + jnp.where(
        keep_second, weight[1:2, :], 0.0
    )


def prepare_kernel(capacity, experts_n, ids, codes, up, down, columns, up_out, down_out, sems):
    copies = [
        pltpu.make_async_copy(up, up_out, sems.at[0]),
        pltpu.make_async_copy(down, down_out, sems.at[1]),
    ]
    for copy in copies:
        copy.start()
    me = lax.axis_index("expert")
    weight = kept_weights(ids[...], codes[...], experts_n, capacity)
    rows = weight.shape[1]
    index = lax.broadcasted_iota(jnp.int32, weight.shape, 0)
    diagonal = lax.broadcasted_iota(jnp.int32, (rows, rows), 0) == lax.broadcasted_iota(
        jnp.int32, (rows, rows), 1
    )
    for step in range(experts_n):
        mine = index == lax.rem(me + step, experts_n)
        row = jnp.sum(jnp.where(mine, weight, 0.0), axis=0, keepdims=True)
        column = jnp.sum(jnp.where(diagonal, row, 0.0), axis=1, keepdims=True)
        columns[step] = jnp.broadcast_to(column, columns.shape[1:])
    for copy in copies:
        copy.wait()


def local_call(
    kernel, out_shape, operands, others=(), in_specs=None, limit=4 * MIB, cost=0.5, **kwargs
):
    count = len(operands)

    name = getattr(kernel, "func", kernel).__name__

    def body_of(*refs):
        kernel(*refs[:count], *refs[count + len(others) :])

    return pl.pallas_call(
        body_of,
        name=name,
        out_shape=out_shape,
        in_specs=list(in_specs or [VMEM] * count) + [pl.BlockSpec(memory_space=pl.ANY)] * len(others),
        out_specs=jax.tree.map(lambda _: VMEM, out_shape),
        compiler_params=pltpu.CompilerParams(vmem_limit_bytes=limit),
        cost_estimate=pl.CostEstimate(
            flops=int(cost * 1.15e9), bytes_accessed=0, transcendentals=0
        ),
        **kwargs,
    )(*operands, *others)


def after(array, other):
    anywhere = pl.BlockSpec(memory_space=pl.ANY)
    return pl.pallas_call(
        lambda *refs: None,
        out_shape=jax.ShapeDtypeStruct(array.shape, array.dtype),
        in_specs=[anywhere, anywhere],
        out_specs=anywhere,
        input_output_aliases={0: 0},
        compiler_params=pltpu.CompilerParams(vmem_limit_bytes=MIB),
    )(array, other)


def prepare(ids, codes, up_t, down, experts_n, capacity):
    rows = ids.shape[1]
    return local_call(
        functools.partial(prepare_kernel, capacity, experts_n),
        [
            pltpu.VMEM((experts_n, rows, 128), jnp.float32),
            pltpu.VMEM(up_t.shape, up_t.dtype),
            pltpu.VMEM(down.shape, down.dtype),
        ],
        (ids, codes, up_t, down),
        in_specs=[VMEM, VMEM, HBM, HBM],
        scratch_shapes=[pltpu.SemaphoreType.DMA((2,))],
        limit=50 * MIB,
        cost=4,
    )


def pack_kernel(*refs):
    packed = refs[-1]
    rows, width = refs[0].shape
    for index, ref in enumerate(refs[:-1]):
        at, column = index // 2 * rows, index % 2 * width
        packed[at : at + rows, column : column + width] = ref[...]


def pack(pairs, others, cost):
    rows, width = pairs[0][0].shape
    return local_call(
        pack_kernel,
        jax.ShapeDtypeStruct((len(pairs) * rows, 2 * width), pairs[0][0].dtype),
        [array for pair in pairs for array in pair],
        others,
        cost=cost,
    )


def expert_kernel(count, *refs):
    pieces, (up_t, down, keep, send, features, out) = refs[:count], refs[count:]
    width = send.shape[1] // 2
    place = lax.axis_index("tensor")

    def columns(bits):
        return pl.ds(pl.multiple_of((place ^ bits) * width, width), width)

    order = [0, 2, 1, 3]
    for piece in pieces:
        for at in range(0, piece.shape[1], width):
            features[:, columns(order.pop(0))] = piece[:, at : at + width]
    lifted = lax.dot_general(
        features[...], up_t[...], (((1,), (1,)), ((), ())), preferred_element_type=jnp.float32
    )
    hidden = (lifted / (1.0 + jnp.exp(-lifted))).astype(jnp.bfloat16)
    out[...] = jnp.dot(hidden, down[...], preferred_element_type=jnp.float32)
    keep[:, :width] = out[:, columns(0)]
    keep[:, width:] = out[:, columns(2)]
    send[:, :width] = out[:, columns(1)].astype(jnp.bfloat16)
    send[:, width:] = out[:, columns(3)].astype(jnp.bfloat16)


def expert_rows(pieces, up_t, down, others, cost):
    rows, model = pieces[0].shape[0], up_t.shape[1]
    return local_call(
        functools.partial(expert_kernel, len(pieces)),
        [
            jax.ShapeDtypeStruct((rows, model // 2), jnp.float32),
            jax.ShapeDtypeStruct((rows, model // 2), jnp.bfloat16),
        ],
        (*pieces, up_t, down),
        others,
        limit=10 * MIB,
        scratch_shapes=[
            pltpu.VMEM((rows, model), jnp.bfloat16),
            pltpu.VMEM((rows, model), jnp.float32),
        ],
        cost=cost,
    )


def core_sum_kernel(keep, got, own, *sends):
    width = own.shape[1]
    own[...] = keep[:, :width] + got[:, :width].astype(jnp.float32)
    for index, send in enumerate(sends):
        rows = slice(index * send.shape[0], (index + 1) * send.shape[0])
        send[...] = (keep[rows, width:] + got[rows, width:].astype(jnp.float32)).astype(send.dtype)


def core_sum(keep, got, count, others, cost):
    rows, width = keep.shape[0], keep.shape[1] // 2
    return local_call(
        core_sum_kernel,
        [jax.ShapeDtypeStruct((rows, width), jnp.float32)]
        + [jax.ShapeDtypeStruct((rows // count, width), jnp.bfloat16)] * count,
        (keep, got),
        others,
        cost=cost,
    )


def chip_sum_kernel(index, own, got, part):
    rows = slice(index * got.shape[0], (index + 1) * got.shape[0])
    part[...] = (own[rows, :] + got[...].astype(jnp.float32)).astype(part.dtype)


def chip_sum(own, got, index, others, cost):
    return local_call(
        functools.partial(chip_sum_kernel, index),
        jax.ShapeDtypeStruct(got.shape, jnp.bfloat16),
        (own, got),
        others,
        cost=cost,
    )


def weigh_kernel(steps, columns, own, got, *rest):
    parts, out = rest[:-1], rest[-1]
    for at in range(0, out.shape[1], 128):
        here = slice(at, at + 128)
        total = own[:, here]
        if got is not None:
            total = columns[0] * (total + got[:, here].astype(jnp.float32))
        for step, part in zip(steps, parts):
            total = total + columns[step] * part[:, here].astype(jnp.float32)
        out[:, here] = total.astype(out.dtype)


def weigh(columns, own, got, steps, parts):
    return local_call(
        functools.partial(weigh_kernel, steps),
        jax.ShapeDtypeStruct(own.shape, jnp.float32),
        (columns, own, got, *parts),
        cost=4,
    )


def finish_kernel(steps, columns, total, *rest):
    weigh_kernel(steps, columns, total, None, *rest)


def finish(columns, total, steps, parts):
    return local_call(
        functools.partial(finish_kernel, steps),
        jax.ShapeDtypeStruct(total.shape, jnp.bfloat16),
        (columns, total, *parts),
    )


def swap(array, bit):
    return lax.ppermute(array, "tensor", [(i, i ^ bit) for i in range(4)])


def whole_blocks(tokens, expert_ids, weight_codes, up_local, down_local, capacity):
    experts_n = lax.axis_size("expert")

    def shift(array, by):
        return lax.ppermute(
            array, "expert", [(i, (i + by) % experts_n) for i in range(experts_n)]
        )

    columns, up_t, down = prepare(
        expert_ids.T, weight_codes.T, up_local.T, down_local, experts_n, capacity
    )
    blocks, others, chips, kept, sums, added, parts = {}, {}, {}, {}, {}, {}, {}

    def arrive(step, source, by, waits):
        blocks[step] = shift(source, by) if step else tokens
        for wait in waits:
            blocks[step] = after(blocks[step], wait)
        others[step] = swap(blocks[step], 2)

    def lay(steps, waits, cost=0.5):
        chips[steps] = pack([(blocks[step], others[step]) for step in steps], waits, cost)

    def run(steps, waits, cost):
        mine = [chips[steps]] if steps in chips else [blocks[steps[0]], others[steps[0]]]
        pieces = mine + [swap(piece, 1) for piece in mine]
        kept[steps] = expert_rows(pieces, up_t, down, waits, cost)

    def leave(steps, waits, cost=2):
        keep, send = kept[steps]
        own, *aways = core_sum(keep, swap(send, 1), len(steps), waits, cost)
        for index, step in enumerate(steps):
            sums[step] = own, swap(aways[index], 2), index

    def give(step, waits, cost=2):
        added[step] = chip_sum(*sums[step], waits, cost)
        parts[step] = shift(added[step], -step)

    arrive(0, tokens, 0, [])
    arrive(1, tokens, 1, [columns])
    lay((0,), [blocks[1]])
    chips[3,] = shift(chips[0,], -1)
    run((0,), [], 8)
    arrive(2, blocks[1], 1, [kept[0,][0]])
    run((1,), [blocks[2]], .05)
    chips[3,] = after(chips[3,], kept[1,][0])
    lay((2,), [chips[3,]], 8)
    leave((1,), [chips[2,]], 2)
    run((3,), [sums[1][0]], 4)
    run((2,), [kept[3,][0]], .05)
    give(1, [kept[2,][0]], 2)
    leave((3,), [added[1]], 4)
    leave((2,), [sums[3][0]], 2)
    give(3, [sums[2][0]], 4)
    give(2, [added[3]], 4)
    leave((0,), [added[2]], 2)
    total = weigh(columns, *sums[0][:2], (1, 3), [parts[1], parts[3]])
    return finish(columns, total, (2,), [parts[2]])


def slotted(tokens, expert_ids, weight_codes, up_local, down_local, capacity):
    rows, share_width = tokens.shape
    experts_n = lax.axis_size("expert")
    slots_n = experts_n * capacity
    flat_ids = expert_ids.reshape(rows * 2)
    onehot = (flat_ids[:, None] == jnp.arange(experts_n, dtype=jnp.int32)[None, :]).astype(
        jnp.int32
    )
    prior = jnp.cumsum(onehot, axis=0) - onehot
    slot = jnp.sum(prior * onehot, axis=1)
    target = jnp.where(slot < capacity, flat_ids * capacity + slot, -1)
    select = (jnp.arange(slots_n, dtype=jnp.int32)[:, None] == target[None, :]).astype(jnp.bfloat16)
    select = select.reshape(slots_n, rows, 2)
    gather_mat = jnp.sum(select, axis=2)
    sending = jnp.dot(gather_mat, tokens, preferred_element_type=jnp.float32).astype(jnp.bfloat16)
    sending = sending.reshape(experts_n, capacity, share_width)
    received = lax.all_to_all(sending, "expert", split_axis=0, concat_axis=0, tiled=True)
    received = received.reshape(slots_n, share_width)
    received = lax.all_gather(received, "tensor", axis=1, tiled=True)
    lifted = jnp.dot(received, up_local, preferred_element_type=jnp.float32)
    hidden = jax.nn.silu(lifted).astype(jnp.bfloat16)
    partial_out = jnp.dot(hidden, down_local, preferred_element_type=jnp.float32)
    total = lax.psum_scatter(
        partial_out.astype(jnp.bfloat16), "tensor", scatter_dimension=1, tiled=True
    )
    total = total.reshape(experts_n, capacity, share_width)
    returned = lax.all_to_all(total, "expert", split_axis=0, concat_axis=0, tiled=True)
    returned = returned.reshape(slots_n, share_width)
    picked = jnp.einsum("srk,sd->krd", select, returned, preferred_element_type=jnp.float32)
    codes = weight_codes.astype(jnp.float32)
    weight = codes / jnp.sum(codes, axis=1, keepdims=True)
    mixed = weight[:, 0:1] * picked[0] + weight[:, 1:2] * picked[1]
    return mixed.astype(jnp.bfloat16)


def body(tokens, expert_ids, weight_codes, up_weight, down_weight):
    rows = tokens.shape[0]
    capacity = 4 * rows // lax.axis_size("expert")
    whole = capacity >= rows and lax.axis_size("expert") == lax.axis_size("tensor") == 4
    plan = whole_blocks if whole else slotted
    return plan(tokens, expert_ids, weight_codes, up_weight[0], down_weight[0], capacity)


def solution(mesh):
    return jax.shard_map(
        body,
        mesh=mesh,
        in_specs=(
            P(("group", "expert"), "tensor"),
            P(("group", "expert"), None),
            P(("group", "expert"), None),
            P("expert", None, "tensor"),
            P("expert", "tensor", None),
        ),
        out_specs=P(("group", "expert"), "tensor"),
        check_vma=False,
    )
```

```python
import functools

import jax
import jax.numpy as jnp
from jax import lax
from jax.experimental import pallas as pl
from jax.experimental.pallas import tpu as pltpu
from jax.sharding import PartitionSpec as P


MIB = 1 << 20
HBM = pl.BlockSpec(memory_space=pltpu.HBM)
VMEM = pl.BlockSpec(memory_space=pltpu.VMEM)


def kept_weights(ids, codes, experts_n, capacity):
    rows = ids.shape[1]
    experts = lax.broadcasted_iota(jnp.int32, (experts_n, rows), 0)
    first = ids[0:1, :] == experts
    second = ids[1:2, :] == experts
    counts = first.astype(jnp.float32) + second.astype(jnp.float32)
    earlier = lax.broadcasted_iota(jnp.int32, (rows, rows), 0) < lax.broadcasted_iota(
        jnp.int32, (rows, rows), 1
    )
    before = jnp.dot(
        counts.astype(jnp.bfloat16),
        earlier.astype(jnp.float32).astype(jnp.bfloat16),
        preferred_element_type=jnp.float32,
    )
    codes = codes.astype(jnp.float32)
    weight = codes / (codes[0:1, :] + codes[1:2, :])
    keep_first = first & (before < capacity)
    keep_second = second & (before + first.astype(jnp.float32) < capacity)
    return jnp.where(keep_first, weight[0:1, :], 0.0) + jnp.where(
        keep_second, weight[1:2, :], 0.0
    )


def prepare_kernel(capacity, experts_n, ids, codes, up, down, columns, up_out, down_out, sems):
    copies = [
        pltpu.make_async_copy(up, up_out, sems.at[0]),
        pltpu.make_async_copy(down, down_out, sems.at[1]),
    ]
    for copy in copies:
        copy.start()
    me = lax.axis_index("expert")
    weight = kept_weights(ids[...], codes[...], experts_n, capacity)
    rows = weight.shape[1]
    index = lax.broadcasted_iota(jnp.int32, weight.shape, 0)
    diagonal = lax.broadcasted_iota(jnp.int32, (rows, rows), 0) == lax.broadcasted_iota(
        jnp.int32, (rows, rows), 1
    )
    for step in range(experts_n):
        mine = index == lax.rem(me + step, experts_n)
        row = jnp.sum(jnp.where(mine, weight, 0.0), axis=0, keepdims=True)
        column = jnp.sum(jnp.where(diagonal, row, 0.0), axis=1, keepdims=True)
        columns[step] = jnp.broadcast_to(column, columns.shape[1:])
    for copy in copies:
        copy.wait()


def local_call(
    kernel, out_shape, operands, others=(), in_specs=None, limit=4 * MIB, cost=0.5, **kwargs
):
    count = len(operands)

    name = getattr(kernel, "func", kernel).__name__

    def body_of(*refs):
        kernel(*refs[:count], *refs[count + len(others) :])

    return pl.pallas_call(
        body_of,
        name=name,
        out_shape=out_shape,
        in_specs=list(in_specs or [VMEM] * count) + [pl.BlockSpec(memory_space=pl.ANY)] * len(others),
        out_specs=jax.tree.map(lambda _: VMEM, out_shape),
        compiler_params=pltpu.CompilerParams(vmem_limit_bytes=limit),
        cost_estimate=pl.CostEstimate(
            flops=int(cost * 1.15e9), bytes_accessed=0, transcendentals=0
        ),
        **kwargs,
    )(*operands, *others)


def after(array, other):
    anywhere = pl.BlockSpec(memory_space=pl.ANY)
    return pl.pallas_call(
        lambda *refs: None,
        out_shape=jax.ShapeDtypeStruct(array.shape, array.dtype),
        in_specs=[anywhere, anywhere],
        out_specs=anywhere,
        input_output_aliases={0: 0},
        compiler_params=pltpu.CompilerParams(vmem_limit_bytes=MIB),
    )(array, other)


def prepare(ids, codes, up_t, down, experts_n, capacity):
    rows = ids.shape[1]
    return local_call(
        functools.partial(prepare_kernel, capacity, experts_n),
        [
            pltpu.VMEM((experts_n, rows, 128), jnp.float32),
            pltpu.VMEM(up_t.shape, up_t.dtype),
            pltpu.VMEM(down.shape, down.dtype),
        ],
        (ids, codes, up_t, down),
        in_specs=[VMEM, VMEM, HBM, HBM],
        scratch_shapes=[pltpu.SemaphoreType.DMA((2,))],
        limit=50 * MIB,
        cost=4,
    )


def pack_kernel(*refs):
    packed = refs[-1]
    rows, width = refs[0].shape
    for index, ref in enumerate(refs[:-1]):
        at, column = index // 2 * rows, index % 2 * width
        packed[at : at + rows, column : column + width] = ref[...]


def pack(pairs, others, cost):
    rows, width = pairs[0][0].shape
    return local_call(
        pack_kernel,
        jax.ShapeDtypeStruct((len(pairs) * rows, 2 * width), pairs[0][0].dtype),
        [array for pair in pairs for array in pair],
        others,
        cost=cost,
    )


def expert_kernel(count, *refs):
    pieces, (up_t, down, keep, send, features, out) = refs[:count], refs[count:]
    width = send.shape[1] // 2
    place = lax.axis_index("tensor")

    def columns(bits):
        return pl.ds(pl.multiple_of((place ^ bits) * width, width), width)

    order = [0, 2, 1, 3]
    for piece in pieces:
        for at in range(0, piece.shape[1], width):
            features[:, columns(order.pop(0))] = piece[:, at : at + width]
    lifted = lax.dot_general(
        features[...], up_t[...], (((1,), (1,)), ((), ())), preferred_element_type=jnp.float32
    )
    hidden = (lifted / (1.0 + jnp.exp(-lifted))).astype(jnp.bfloat16)
    out[...] = jnp.dot(hidden, down[...], preferred_element_type=jnp.float32)
    keep[:, :width] = out[:, columns(0)]
    keep[:, width:] = out[:, columns(2)]
    send[:, :width] = out[:, columns(1)].astype(jnp.bfloat16)
    send[:, width:] = out[:, columns(3)].astype(jnp.bfloat16)


def expert_rows(pieces, up_t, down, others, cost):
    rows, model = pieces[0].shape[0], up_t.shape[1]
    return local_call(
        functools.partial(expert_kernel, len(pieces)),
        [
            jax.ShapeDtypeStruct((rows, model // 2), jnp.float32),
            jax.ShapeDtypeStruct((rows, model // 2), jnp.bfloat16),
        ],
        (*pieces, up_t, down),
        others,
        limit=10 * MIB,
        scratch_shapes=[
            pltpu.VMEM((rows, model), jnp.bfloat16),
            pltpu.VMEM((rows, model), jnp.float32),
        ],
        cost=cost,
    )


def core_sum_kernel(keep, got, own, *sends):
    width = own.shape[1]
    own[...] = keep[:, :width] + got[:, :width].astype(jnp.float32)
    for index, send in enumerate(sends):
        rows = slice(index * send.shape[0], (index + 1) * send.shape[0])
        send[...] = (keep[rows, width:] + got[rows, width:].astype(jnp.float32)).astype(send.dtype)


def core_sum(keep, got, count, others, cost):
    rows, width = keep.shape[0], keep.shape[1] // 2
    return local_call(
        core_sum_kernel,
        [jax.ShapeDtypeStruct((rows, width), jnp.float32)]
        + [jax.ShapeDtypeStruct((rows // count, width), jnp.bfloat16)] * count,
        (keep, got),
        others,
        cost=cost,
    )


def chip_sum_kernel(index, own, got, part):
    rows = slice(index * got.shape[0], (index + 1) * got.shape[0])
    part[...] = (own[rows, :] + got[...].astype(jnp.float32)).astype(part.dtype)


def chip_sum(own, got, index, others, cost):
    return local_call(
        functools.partial(chip_sum_kernel, index),
        jax.ShapeDtypeStruct(got.shape, jnp.bfloat16),
        (own, got),
        others,
        cost=cost,
    )


def weigh_kernel(steps, columns, own, got, *rest):
    parts, out = rest[:-1], rest[-1]
    for at in range(0, out.shape[1], 128):
        here = slice(at, at + 128)
        total = own[:, here]
        if got is not None:
            total = columns[0] * (total + got[:, here].astype(jnp.float32))
        for step, part in zip(steps, parts):
            total = total + columns[step] * part[:, here].astype(jnp.float32)
        out[:, here] = total.astype(out.dtype)


def weigh(columns, own, got, steps, parts):
    return local_call(
        functools.partial(weigh_kernel, steps),
        jax.ShapeDtypeStruct(own.shape, jnp.float32),
        (columns, own, got, *parts),
        cost=4,
    )


def finish_kernel(steps, columns, total, *rest):
    weigh_kernel(steps, columns, total, None, *rest)


def finish(columns, total, steps, parts):
    return local_call(
        functools.partial(finish_kernel, steps),
        jax.ShapeDtypeStruct(total.shape, jnp.bfloat16),
        (columns, total, *parts),
    )


def swap(array, bit):
    return lax.ppermute(array, "tensor", [(i, i ^ bit) for i in range(4)])


def whole_blocks(tokens, expert_ids, weight_codes, up_local, down_local, capacity):
    experts_n = lax.axis_size("expert")

    def shift(array, by):
        return lax.ppermute(
            array, "expert", [(i, (i + by) % experts_n) for i in range(experts_n)]
        )

    columns, up_t, down = prepare(
        expert_ids.T, weight_codes.T, up_local.T, down_local, experts_n, capacity
    )
    blocks, others, chips, kept, sums, added, parts = {}, {}, {}, {}, {}, {}, {}

    def arrive(step, source, by, waits):
        blocks[step] = shift(source, by) if step else tokens
        for wait in waits:
            blocks[step] = after(blocks[step], wait)
        others[step] = swap(blocks[step], 2)

    def lay(steps, waits, cost=0.5):
        chips[steps] = pack([(blocks[step], others[step]) for step in steps], waits, cost)

    def run(steps, waits, cost):
        mine = [chips[steps]] if steps in chips else [blocks[steps[0]], others[steps[0]]]
        pieces = mine + [swap(piece, 1) for piece in mine]
        kept[steps] = expert_rows(pieces, up_t, down, waits, cost)

    def leave(steps, waits, cost=2):
        keep, send = kept[steps]
        own, *aways = core_sum(keep, swap(send, 1), len(steps), waits, cost)
        for index, step in enumerate(steps):
            sums[step] = own, swap(aways[index], 2), index

    def give(step, waits, cost=2):
        added[step] = chip_sum(*sums[step], waits, cost)
        parts[step] = shift(added[step], -step)

    arrive(0, tokens, 0, [])
    arrive(1, tokens, 1, [columns])
    lay((0,), [blocks[1]])
    chips[3,] = shift(chips[0,], -1)
    run((0,), [], 8)
    arrive(2, blocks[1], 1, [kept[0,][0]])
    run((1,), [blocks[2]], .05)
    run((2,), [kept[1,][0]], .05)
    chips[3,] = after(chips[3,], kept[2,][0])
    leave((1,), [kept[2,][0]], 2)
    leave((2,), [sums[1][0]], 2)
    run((3,), [sums[2][0]], 4)
    give(1, [kept[3,][0]], 4)
    leave((3,), [added[1]], 2)
    give(2, [sums[3][0]], 4)
    give(3, [added[2]], 4)
    leave((0,), [added[3]], 2)
    total = weigh(columns, *sums[0][:2], (1, 2), [parts[1], parts[2]])
    return finish(columns, total, (3,), [parts[3]])


def slotted(tokens, expert_ids, weight_codes, up_local, down_local, capacity):
    rows, share_width = tokens.shape
    experts_n = lax.axis_size("expert")
    slots_n = experts_n * capacity
    flat_ids = expert_ids.reshape(rows * 2)
    onehot = (flat_ids[:, None] == jnp.arange(experts_n, dtype=jnp.int32)[None, :]).astype(
        jnp.int32
    )
    prior = jnp.cumsum(onehot, axis=0) - onehot
    slot = jnp.sum(prior * onehot, axis=1)
    target = jnp.where(slot < capacity, flat_ids * capacity + slot, -1)
    select = (jnp.arange(slots_n, dtype=jnp.int32)[:, None] == target[None, :]).astype(jnp.bfloat16)
    select = select.reshape(slots_n, rows, 2)
    gather_mat = jnp.sum(select, axis=2)
    sending = jnp.dot(gather_mat, tokens, preferred_element_type=jnp.float32).astype(jnp.bfloat16)
    sending = sending.reshape(experts_n, capacity, share_width)
    received = lax.all_to_all(sending, "expert", split_axis=0, concat_axis=0, tiled=True)
    received = received.reshape(slots_n, share_width)
    received = lax.all_gather(received, "tensor", axis=1, tiled=True)
    lifted = jnp.dot(received, up_local, preferred_element_type=jnp.float32)
    hidden = jax.nn.silu(lifted).astype(jnp.bfloat16)
    partial_out = jnp.dot(hidden, down_local, preferred_element_type=jnp.float32)
    total = lax.psum_scatter(
        partial_out.astype(jnp.bfloat16), "tensor", scatter_dimension=1, tiled=True
    )
    total = total.reshape(experts_n, capacity, share_width)
    returned = lax.all_to_all(total, "expert", split_axis=0, concat_axis=0, tiled=True)
    returned = returned.reshape(slots_n, share_width)
    picked = jnp.einsum("srk,sd->krd", select, returned, preferred_element_type=jnp.float32)
    codes = weight_codes.astype(jnp.float32)
    weight = codes / jnp.sum(codes, axis=1, keepdims=True)
    mixed = weight[:, 0:1] * picked[0] + weight[:, 1:2] * picked[1]
    return mixed.astype(jnp.bfloat16)


def body(tokens, expert_ids, weight_codes, up_weight, down_weight):
    rows = tokens.shape[0]
    capacity = 4 * rows // lax.axis_size("expert")
    whole = capacity >= rows and lax.axis_size("expert") == lax.axis_size("tensor") == 4
    plan = whole_blocks if whole else slotted
    return plan(tokens, expert_ids, weight_codes, up_weight[0], down_weight[0], capacity)


def solution(mesh):
    return jax.shard_map(
        body,
        mesh=mesh,
        in_specs=(
            P(("group", "expert"), "tensor"),
            P(("group", "expert"), None),
            P(("group", "expert"), None),
            P("expert", None, "tensor"),
            P("expert", "tensor", None),
        ),
        out_specs=P(("group", "expert"), "tensor"),
        check_vma=False,
    )
```

```python
import functools

import jax
import jax.numpy as jnp
from jax import lax
from jax.experimental import pallas as pl
from jax.experimental.pallas import tpu as pltpu
from jax.sharding import PartitionSpec as P


MIB = 1 << 20
HBM = pl.BlockSpec(memory_space=pltpu.HBM)
VMEM = pl.BlockSpec(memory_space=pltpu.VMEM)


def kept_weights(ids, codes, experts_n, capacity):
    rows = ids.shape[1]
    experts = lax.broadcasted_iota(jnp.int32, (experts_n, rows), 0)
    first = ids[0:1, :] == experts
    second = ids[1:2, :] == experts
    counts = first.astype(jnp.float32) + second.astype(jnp.float32)
    earlier = lax.broadcasted_iota(jnp.int32, (rows, rows), 0) < lax.broadcasted_iota(
        jnp.int32, (rows, rows), 1
    )
    before = jnp.dot(
        counts.astype(jnp.bfloat16),
        earlier.astype(jnp.float32).astype(jnp.bfloat16),
        preferred_element_type=jnp.float32,
    )
    codes = codes.astype(jnp.float32)
    weight = codes / (codes[0:1, :] + codes[1:2, :])
    keep_first = first & (before < capacity)
    keep_second = second & (before + first.astype(jnp.float32) < capacity)
    return jnp.where(keep_first, weight[0:1, :], 0.0) + jnp.where(
        keep_second, weight[1:2, :], 0.0
    )


def prepare_kernel(capacity, experts_n, ids, codes, up, down, columns, up_out, down_out, sems):
    copies = [
        pltpu.make_async_copy(up, up_out, sems.at[0]),
        pltpu.make_async_copy(down, down_out, sems.at[1]),
    ]
    for copy in copies:
        copy.start()
    me = lax.axis_index("expert")
    weight = kept_weights(ids[...], codes[...], experts_n, capacity)
    rows = weight.shape[1]
    index = lax.broadcasted_iota(jnp.int32, weight.shape, 0)
    diagonal = lax.broadcasted_iota(jnp.int32, (rows, rows), 0) == lax.broadcasted_iota(
        jnp.int32, (rows, rows), 1
    )
    for step in range(experts_n):
        mine = index == lax.rem(me + step, experts_n)
        row = jnp.sum(jnp.where(mine, weight, 0.0), axis=0, keepdims=True)
        column = jnp.sum(jnp.where(diagonal, row, 0.0), axis=1, keepdims=True)
        columns[step] = jnp.broadcast_to(column, columns.shape[1:])
    for copy in copies:
        copy.wait()


def local_call(
    kernel, out_shape, operands, others=(), in_specs=None, limit=4 * MIB, cost=0.5, **kwargs
):
    count = len(operands)

    name = getattr(kernel, "func", kernel).__name__

    def body_of(*refs):
        kernel(*refs[:count], *refs[count + len(others) :])

    return pl.pallas_call(
        body_of,
        name=name,
        out_shape=out_shape,
        in_specs=list(in_specs or [VMEM] * count) + [pl.BlockSpec(memory_space=pl.ANY)] * len(others),
        out_specs=jax.tree.map(lambda _: VMEM, out_shape),
        compiler_params=pltpu.CompilerParams(vmem_limit_bytes=limit),
        cost_estimate=pl.CostEstimate(
            flops=int(cost * 1.15e9), bytes_accessed=0, transcendentals=0
        ),
        **kwargs,
    )(*operands, *others)


def after(array, other):
    anywhere = pl.BlockSpec(memory_space=pl.ANY)
    return pl.pallas_call(
        lambda *refs: None,
        out_shape=jax.ShapeDtypeStruct(array.shape, array.dtype),
        in_specs=[anywhere, anywhere],
        out_specs=anywhere,
        input_output_aliases={0: 0},
        compiler_params=pltpu.CompilerParams(vmem_limit_bytes=MIB),
    )(array, other)


def prepare(ids, codes, up_t, down, experts_n, capacity):
    rows = ids.shape[1]
    return local_call(
        functools.partial(prepare_kernel, capacity, experts_n),
        [
            pltpu.VMEM((experts_n, rows, 128), jnp.float32),
            pltpu.VMEM(up_t.shape, up_t.dtype),
            pltpu.VMEM(down.shape, down.dtype),
        ],
        (ids, codes, up_t, down),
        in_specs=[VMEM, VMEM, HBM, HBM],
        scratch_shapes=[pltpu.SemaphoreType.DMA((2,))],
        limit=50 * MIB,
        cost=4,
    )


def pack_kernel(*refs):
    packed = refs[-1]
    rows, width = refs[0].shape
    for index, ref in enumerate(refs[:-1]):
        at, column = index // 2 * rows, index % 2 * width
        packed[at : at + rows, column : column + width] = ref[...]


def pack(pairs, others, cost):
    rows, width = pairs[0][0].shape
    return local_call(
        pack_kernel,
        jax.ShapeDtypeStruct((len(pairs) * rows, 2 * width), pairs[0][0].dtype),
        [array for pair in pairs for array in pair],
        others,
        cost=cost,
    )


def expert_kernel(count, *refs):
    pieces, (up_t, down, keep, send, features, out) = refs[:count], refs[count:]
    width = send.shape[1] // 2
    place = lax.axis_index("tensor")

    def columns(bits):
        return pl.ds(pl.multiple_of((place ^ bits) * width, width), width)

    order = [0, 2, 1, 3]
    for piece in pieces:
        for at in range(0, piece.shape[1], width):
            features[:, columns(order.pop(0))] = piece[:, at : at + width]
    lifted = lax.dot_general(
        features[...], up_t[...], (((1,), (1,)), ((), ())), preferred_element_type=jnp.float32
    )
    hidden = (lifted / (1.0 + jnp.exp(-lifted))).astype(jnp.bfloat16)
    out[...] = jnp.dot(hidden, down[...], preferred_element_type=jnp.float32)
    keep[:, :width] = out[:, columns(0)]
    keep[:, width:] = out[:, columns(2)]
    send[:, :width] = out[:, columns(1)].astype(jnp.bfloat16)
    send[:, width:] = out[:, columns(3)].astype(jnp.bfloat16)


def expert_rows(pieces, up_t, down, others, cost):
    rows, model = pieces[0].shape[0], up_t.shape[1]
    return local_call(
        functools.partial(expert_kernel, len(pieces)),
        [
            jax.ShapeDtypeStruct((rows, model // 2), jnp.float32),
            jax.ShapeDtypeStruct((rows, model // 2), jnp.bfloat16),
        ],
        (*pieces, up_t, down),
        others,
        limit=10 * MIB,
        scratch_shapes=[
            pltpu.VMEM((rows, model), jnp.bfloat16),
            pltpu.VMEM((rows, model), jnp.float32),
        ],
        cost=cost,
    )


def core_sum_kernel(keep, got, own, *sends):
    width = own.shape[1]
    own[...] = keep[:, :width] + got[:, :width].astype(jnp.float32)
    for index, send in enumerate(sends):
        rows = slice(index * send.shape[0], (index + 1) * send.shape[0])
        send[...] = (keep[rows, width:] + got[rows, width:].astype(jnp.float32)).astype(send.dtype)


def core_sum(keep, got, count, others, cost):
    rows, width = keep.shape[0], keep.shape[1] // 2
    return local_call(
        core_sum_kernel,
        [jax.ShapeDtypeStruct((rows, width), jnp.float32)]
        + [jax.ShapeDtypeStruct((rows // count, width), jnp.bfloat16)] * count,
        (keep, got),
        others,
        cost=cost,
    )


def chip_sum_kernel(index, own, got, part):
    rows = slice(index * got.shape[0], (index + 1) * got.shape[0])
    part[...] = (own[rows, :] + got[...].astype(jnp.float32)).astype(part.dtype)


def chip_sum(own, got, index, others, cost):
    return local_call(
        functools.partial(chip_sum_kernel, index),
        jax.ShapeDtypeStruct(got.shape, jnp.bfloat16),
        (own, got),
        others,
        cost=cost,
    )


def weigh_kernel(steps, counts, columns, *refs):
    refs, out = list(refs[:-1]), refs[-1]
    for at in range(0, out.shape[1], 128):
        here = slice(at, at + 128)
        left = list(refs)
        total = left.pop(0)[:, here] if len(left) > sum(counts) else None
        for step, count in zip(steps, counts):
            rows = sum(left.pop(0)[:, here].astype(jnp.float32) for _ in range(count))
            rows = columns[step] * rows
            total = rows if total is None else total + rows
        out[:, here] = total.astype(out.dtype)


def weigh(columns, totals, steps, terms, dtype, cost):
    arrays = [*totals, *[array for term in terms for array in term]]
    return local_call(
        functools.partial(weigh_kernel, steps, [len(term) for term in terms]),
        jax.ShapeDtypeStruct(arrays[-1].shape, dtype),
        (columns, *arrays),
        cost=cost,
    )


def swap(array, bit):
    return lax.ppermute(array, "tensor", [(i, i ^ bit) for i in range(4)])


def whole_blocks(tokens, expert_ids, weight_codes, up_local, down_local, capacity):
    experts_n = lax.axis_size("expert")

    def shift(array, by):
        return lax.ppermute(
            array, "expert", [(i, (i + by) % experts_n) for i in range(experts_n)]
        )

    columns, up_t, down = prepare(
        expert_ids.T, weight_codes.T, up_local.T, down_local, experts_n, capacity
    )
    blocks, others, chips, kept, sums, added, parts = {}, {}, {}, {}, {}, {}, {}

    def arrive(step, source, by, waits):
        blocks[step] = shift(source, by) if step else tokens
        for wait in waits:
            blocks[step] = after(blocks[step], wait)
        others[step] = swap(blocks[step], 2)

    def lay(steps, waits, cost=0.5):
        chips[steps] = pack([(blocks[step], others[step]) for step in steps], waits, cost)

    def run(steps, waits, cost):
        mine = [chips[steps]] if steps in chips else [blocks[steps[0]], others[steps[0]]]
        pieces = mine + [swap(piece, 1) for piece in mine]
        kept[steps] = expert_rows(pieces, up_t, down, waits, cost)

    def leave(steps, waits, cost=2):
        keep, send = kept[steps]
        own, *aways = core_sum(keep, swap(send, 1), len(steps), waits, cost)
        for index, step in enumerate(steps):
            sums[step] = own, swap(aways[index], 2), index

    def give(step, waits, cost=2):
        added[step] = chip_sum(*sums[step], waits, cost)
        parts[step] = shift(added[step], -step)

    arrive(0, tokens, 0, [])
    arrive(1, tokens, 1, [columns])
    lay((0,), [blocks[1]])
    chips[3,] = shift(chips[0,], -1)
    run((0,), [], 8)
    arrive(2, blocks[1], 1, [kept[0,][0]])
    others[1] = after(others[1], kept[0,][0])
    run((1,), [blocks[2]], .05)
    run((2,), [kept[1,][0]], .05)
    chips[3,] = after(chips[3,], kept[2,][0])
    leave((1,), [kept[2,][0]], 2)
    leave((2,), [sums[1][0]], 2)
    run((3,), [sums[2][0]], 4)
    give(1, [kept[3,][0]], 4)
    leave((3,), [added[1]], .05)
    give(2, [sums[3][0]], 4)
    give(3, [added[2]], 4)
    leave((0,), [added[3]], 2)
    total = weigh(columns, [], (1, 2), [[parts[1]], [parts[2]]], jnp.float32, 4)
    total = weigh(columns, [total], (0,), [sums[0][:2]], jnp.float32, 4)
    return weigh(columns, [total], (3,), [[parts[3]]], jnp.bfloat16, 0.5)


def slotted(tokens, expert_ids, weight_codes, up_local, down_local, capacity):
    rows, share_width = tokens.shape
    experts_n = lax.axis_size("expert")
    slots_n = experts_n * capacity
    flat_ids = expert_ids.reshape(rows * 2)
    onehot = (flat_ids[:, None] == jnp.arange(experts_n, dtype=jnp.int32)[None, :]).astype(
        jnp.int32
    )
    prior = jnp.cumsum(onehot, axis=0) - onehot
    slot = jnp.sum(prior * onehot, axis=1)
    target = jnp.where(slot < capacity, flat_ids * capacity + slot, -1)
    select = (jnp.arange(slots_n, dtype=jnp.int32)[:, None] == target[None, :]).astype(jnp.bfloat16)
    select = select.reshape(slots_n, rows, 2)
    gather_mat = jnp.sum(select, axis=2)
    sending = jnp.dot(gather_mat, tokens, preferred_element_type=jnp.float32).astype(jnp.bfloat16)
    sending = sending.reshape(experts_n, capacity, share_width)
    received = lax.all_to_all(sending, "expert", split_axis=0, concat_axis=0, tiled=True)
    received = received.reshape(slots_n, share_width)
    received = lax.all_gather(received, "tensor", axis=1, tiled=True)
    lifted = jnp.dot(received, up_local, preferred_element_type=jnp.float32)
    hidden = jax.nn.silu(lifted).astype(jnp.bfloat16)
    partial_out = jnp.dot(hidden, down_local, preferred_element_type=jnp.float32)
    total = lax.psum_scatter(
        partial_out.astype(jnp.bfloat16), "tensor", scatter_dimension=1, tiled=True
    )
    total = total.reshape(experts_n, capacity, share_width)
    returned = lax.all_to_all(total, "expert", split_axis=0, concat_axis=0, tiled=True)
    returned = returned.reshape(slots_n, share_width)
    picked = jnp.einsum("srk,sd->krd", select, returned, preferred_element_type=jnp.float32)
    codes = weight_codes.astype(jnp.float32)
    weight = codes / jnp.sum(codes, axis=1, keepdims=True)
    mixed = weight[:, 0:1] * picked[0] + weight[:, 1:2] * picked[1]
    return mixed.astype(jnp.bfloat16)


def body(tokens, expert_ids, weight_codes, up_weight, down_weight):
    rows = tokens.shape[0]
    capacity = 4 * rows // lax.axis_size("expert")
    whole = capacity >= rows and lax.axis_size("expert") == lax.axis_size("tensor") == 4
    plan = whole_blocks if whole else slotted
    return plan(tokens, expert_ids, weight_codes, up_weight[0], down_weight[0], capacity)


def solution(mesh):
    return jax.shard_map(
        body,
        mesh=mesh,
        in_specs=(
            P(("group", "expert"), "tensor"),
            P(("group", "expert"), None),
            P(("group", "expert"), None),
            P("expert", None, "tensor"),
            P("expert", "tensor", None),
        ),
        out_specs=P(("group", "expert"), "tensor"),
        check_vma=False,
    )
```

```python
import functools

import jax
import jax.numpy as jnp
from jax import lax
from jax.experimental import pallas as pl
from jax.experimental.pallas import tpu as pltpu
from jax.sharding import PartitionSpec as P


MIB = 1 << 20
HBM = pl.BlockSpec(memory_space=pltpu.HBM)
VMEM = pl.BlockSpec(memory_space=pltpu.VMEM)


def kept_weights(ids, codes, experts_n, capacity):
    rows = ids.shape[1]
    experts = lax.broadcasted_iota(jnp.int32, (experts_n, rows), 0)
    first = ids[0:1, :] == experts
    second = ids[1:2, :] == experts
    counts = first.astype(jnp.float32) + second.astype(jnp.float32)
    earlier = lax.broadcasted_iota(jnp.int32, (rows, rows), 0) < lax.broadcasted_iota(
        jnp.int32, (rows, rows), 1
    )
    before = jnp.dot(
        counts.astype(jnp.bfloat16),
        earlier.astype(jnp.float32).astype(jnp.bfloat16),
        preferred_element_type=jnp.float32,
    )
    codes = codes.astype(jnp.float32)
    weight = codes / (codes[0:1, :] + codes[1:2, :])
    keep_first = first & (before < capacity)
    keep_second = second & (before + first.astype(jnp.float32) < capacity)
    return jnp.where(keep_first, weight[0:1, :], 0.0) + jnp.where(
        keep_second, weight[1:2, :], 0.0
    )


def prepare_kernel(capacity, experts_n, ids, codes, up, down, columns, up_out, down_out, sems):
    copies = [
        pltpu.make_async_copy(up, up_out, sems.at[0]),
        pltpu.make_async_copy(down, down_out, sems.at[1]),
    ]
    for copy in copies:
        copy.start()
    me = lax.axis_index("expert")
    weight = kept_weights(ids[...], codes[...], experts_n, capacity)
    rows = weight.shape[1]
    index = lax.broadcasted_iota(jnp.int32, weight.shape, 0)
    diagonal = lax.broadcasted_iota(jnp.int32, (rows, rows), 0) == lax.broadcasted_iota(
        jnp.int32, (rows, rows), 1
    )
    for step in range(experts_n):
        mine = index == lax.rem(me + step, experts_n)
        row = jnp.sum(jnp.where(mine, weight, 0.0), axis=0, keepdims=True)
        column = jnp.sum(jnp.where(diagonal, row, 0.0), axis=1, keepdims=True)
        columns[step] = jnp.broadcast_to(column, columns.shape[1:])
    for copy in copies:
        copy.wait()


def local_call(
    kernel, out_shape, operands, others=(), in_specs=None, limit=4 * MIB, cost=0.5, **kwargs
):
    count = len(operands)

    name = getattr(kernel, "func", kernel).__name__

    def body_of(*refs):
        kernel(*refs[:count], *refs[count + len(others) :])

    return pl.pallas_call(
        body_of,
        name=name,
        out_shape=out_shape,
        in_specs=list(in_specs or [VMEM] * count) + [pl.BlockSpec(memory_space=pl.ANY)] * len(others),
        out_specs=jax.tree.map(lambda _: VMEM, out_shape),
        compiler_params=pltpu.CompilerParams(vmem_limit_bytes=limit),
        cost_estimate=pl.CostEstimate(
            flops=int(cost * 1.15e9), bytes_accessed=0, transcendentals=0
        ),
        **kwargs,
    )(*operands, *others)


def after(array, other):
    anywhere = pl.BlockSpec(memory_space=pl.ANY)
    return pl.pallas_call(
        lambda *refs: None,
        out_shape=jax.ShapeDtypeStruct(array.shape, array.dtype),
        in_specs=[anywhere, anywhere],
        out_specs=anywhere,
        input_output_aliases={0: 0},
        compiler_params=pltpu.CompilerParams(vmem_limit_bytes=MIB),
    )(array, other)


def prepare(ids, codes, up_t, down, experts_n, capacity):
    rows = ids.shape[1]
    return local_call(
        functools.partial(prepare_kernel, capacity, experts_n),
        [
            pltpu.VMEM((experts_n, rows, 128), jnp.float32),
            pltpu.VMEM(up_t.shape, up_t.dtype),
            pltpu.VMEM(down.shape, down.dtype),
        ],
        (ids, codes, up_t, down),
        in_specs=[VMEM, VMEM, HBM, HBM],
        scratch_shapes=[pltpu.SemaphoreType.DMA((2,))],
        limit=50 * MIB,
        cost=4,
    )


def pack_kernel(*refs):
    packed = refs[-1]
    rows, width = refs[0].shape
    for index, ref in enumerate(refs[:-1]):
        at, column = index // 2 * rows, index % 2 * width
        packed[at : at + rows, column : column + width] = ref[...]


def pack(pairs, others, cost):
    rows, width = pairs[0][0].shape
    return local_call(
        pack_kernel,
        jax.ShapeDtypeStruct((len(pairs) * rows, 2 * width), pairs[0][0].dtype),
        [array for pair in pairs for array in pair],
        others,
        cost=cost,
    )


def expert_kernel(count, *refs):
    pieces, (up_t, down, keep, send, features, out) = refs[:count], refs[count:]
    width = send.shape[1] // 2
    place = lax.axis_index("tensor")

    def columns(bits):
        return pl.ds(pl.multiple_of((place ^ bits) * width, width), width)

    order = [0, 2, 1, 3]
    for piece in pieces:
        for at in range(0, piece.shape[1], width):
            features[:, columns(order.pop(0))] = piece[:, at : at + width]
    lifted = lax.dot_general(
        features[...], up_t[...], (((1,), (1,)), ((), ())), preferred_element_type=jnp.float32
    )
    hidden = (lifted / (1.0 + jnp.exp(-lifted))).astype(jnp.bfloat16)
    out[...] = jnp.dot(hidden, down[...], preferred_element_type=jnp.float32)
    keep[:, :width] = out[:, columns(0)]
    keep[:, width:] = out[:, columns(2)]
    send[:, :width] = out[:, columns(1)].astype(jnp.bfloat16)
    send[:, width:] = out[:, columns(3)].astype(jnp.bfloat16)


def expert_rows(pieces, up_t, down, others, cost):
    rows, model = pieces[0].shape[0], up_t.shape[1]
    return local_call(
        functools.partial(expert_kernel, len(pieces)),
        [
            jax.ShapeDtypeStruct((rows, model // 2), jnp.float32),
            jax.ShapeDtypeStruct((rows, model // 2), jnp.bfloat16),
        ],
        (*pieces, up_t, down),
        others,
        limit=10 * MIB,
        scratch_shapes=[
            pltpu.VMEM((rows, model), jnp.bfloat16),
            pltpu.VMEM((rows, model), jnp.float32),
        ],
        cost=cost,
    )


def core_sum_kernel(keep, got, own, *sends):
    width = own.shape[1]
    own[...] = keep[:, :width] + got[:, :width].astype(jnp.float32)
    for index, send in enumerate(sends):
        rows = slice(index * send.shape[0], (index + 1) * send.shape[0])
        send[...] = (keep[rows, width:] + got[rows, width:].astype(jnp.float32)).astype(send.dtype)


def core_sum(keep, got, count, others, cost):
    rows, width = keep.shape[0], keep.shape[1] // 2
    return local_call(
        core_sum_kernel,
        [jax.ShapeDtypeStruct((rows, width), jnp.float32)]
        + [jax.ShapeDtypeStruct((rows // count, width), jnp.bfloat16)] * count,
        (keep, got),
        others,
        cost=cost,
    )


def chip_sum_kernel(index, own, got, part):
    rows = slice(index * got.shape[0], (index + 1) * got.shape[0])
    part[...] = (own[rows, :] + got[...].astype(jnp.float32)).astype(part.dtype)


def chip_sum(own, got, index, others, cost):
    return local_call(
        functools.partial(chip_sum_kernel, index),
        jax.ShapeDtypeStruct(got.shape, jnp.bfloat16),
        (own, got),
        others,
        cost=cost,
    )


def weigh_kernel(steps, counts, columns, *refs):
    refs, out = list(refs[:-1]), refs[-1]
    for at in range(0, out.shape[1], 128):
        here = slice(at, at + 128)
        left = list(refs)
        total = left.pop(0)[:, here] if len(left) > sum(counts) else None
        for step, count in zip(steps, counts):
            rows = sum(left.pop(0)[:, here].astype(jnp.float32) for _ in range(count))
            rows = columns[step] * rows
            total = rows if total is None else total + rows
        out[:, here] = total.astype(out.dtype)


def weigh(columns, totals, steps, terms, dtype, cost):
    arrays = [*totals, *[array for term in terms for array in term]]
    return local_call(
        functools.partial(weigh_kernel, steps, [len(term) for term in terms]),
        jax.ShapeDtypeStruct(arrays[-1].shape, dtype),
        (columns, *arrays),
        cost=cost,
    )


def swap(array, bit):
    return lax.ppermute(array, "tensor", [(i, i ^ bit) for i in range(4)])


def whole_blocks(tokens, expert_ids, weight_codes, up_local, down_local, capacity):
    experts_n = lax.axis_size("expert")

    def shift(array, by):
        return lax.ppermute(
            array, "expert", [(i, (i + by) % experts_n) for i in range(experts_n)]
        )

    columns, up_t, down = prepare(
        expert_ids.T, weight_codes.T, up_local.T, down_local, experts_n, capacity
    )
    blocks, others, chips, kept, sums, added, parts = {}, {}, {}, {}, {}, {}, {}

    def arrive(step, source, by, waits):
        blocks[step] = shift(source, by) if step else tokens
        for wait in waits:
            blocks[step] = after(blocks[step], wait)
        others[step] = swap(blocks[step], 2)

    def lay(steps, waits, cost=0.5):
        chips[steps] = pack([(blocks[step], others[step]) for step in steps], waits, cost)

    def run(steps, waits, cost):
        mine = [chips[steps]] if steps in chips else [blocks[steps[0]], others[steps[0]]]
        pieces = mine + [swap(piece, 1) for piece in mine]
        kept[steps] = expert_rows(pieces, up_t, down, waits, cost)

    def leave(steps, waits, cost=2):
        keep, send = kept[steps]
        own, *aways = core_sum(keep, swap(send, 1), len(steps), waits, cost)
        for index, step in enumerate(steps):
            sums[step] = own, swap(aways[index], 2), index

    def give(step, waits, cost=2):
        added[step] = chip_sum(*sums[step], waits, cost)
        parts[step] = shift(added[step], -step)

    arrive(0, tokens, 0, [])
    arrive(1, tokens, 1, [columns])
    lay((0,), [blocks[1]])
    chips[3,] = shift(chips[0,], -1)
    run((0,), [], 8)
    arrive(2, blocks[1], 1, [kept[0,][0]])
    others[1] = after(others[1], kept[0,][0])
    run((1,), [blocks[2]], .05)
    run((2,), [kept[1,][0]], .05)
    chips[3,] = after(chips[3,], kept[2,][0])
    leave((1,), [kept[2,][0]], 2)
    leave((2,), [sums[1][0]], 2)
    run((3,), [sums[2][0]], 4)
    give(1, [kept[3,][0]], 4)
    leave((3,), [added[1]], 2)
    give(2, [sums[3][0]], 4)
    give(3, [added[2]], 4)
    leave((0,), [added[3]], 2)
    total = weigh(columns, [], (1, 2), [[parts[1]], [parts[2]]], jnp.float32, 4)
    total = weigh(columns, [total], (0,), [sums[0][:2]], jnp.float32, 4)
    return weigh(columns, [total], (3,), [[parts[3]]], jnp.bfloat16, 0.5)


def slotted(tokens, expert_ids, weight_codes, up_local, down_local, capacity):
    rows, share_width = tokens.shape
    experts_n = lax.axis_size("expert")
    slots_n = experts_n * capacity
    flat_ids = expert_ids.reshape(rows * 2)
    onehot = (flat_ids[:, None] == jnp.arange(experts_n, dtype=jnp.int32)[None, :]).astype(
        jnp.int32
    )
    prior = jnp.cumsum(onehot, axis=0) - onehot
    slot = jnp.sum(prior * onehot, axis=1)
    target = jnp.where(slot < capacity, flat_ids * capacity + slot, -1)
    select = (jnp.arange(slots_n, dtype=jnp.int32)[:, None] == target[None, :]).astype(jnp.bfloat16)
    select = select.reshape(slots_n, rows, 2)
    gather_mat = jnp.sum(select, axis=2)
    sending = jnp.dot(gather_mat, tokens, preferred_element_type=jnp.float32).astype(jnp.bfloat16)
    sending = sending.reshape(experts_n, capacity, share_width)
    received = lax.all_to_all(sending, "expert", split_axis=0, concat_axis=0, tiled=True)
    received = received.reshape(slots_n, share_width)
    received = lax.all_gather(received, "tensor", axis=1, tiled=True)
    lifted = jnp.dot(received, up_local, preferred_element_type=jnp.float32)
    hidden = jax.nn.silu(lifted).astype(jnp.bfloat16)
    partial_out = jnp.dot(hidden, down_local, preferred_element_type=jnp.float32)
    total = lax.psum_scatter(
        partial_out.astype(jnp.bfloat16), "tensor", scatter_dimension=1, tiled=True
    )
    total = total.reshape(experts_n, capacity, share_width)
    returned = lax.all_to_all(total, "expert", split_axis=0, concat_axis=0, tiled=True)
    returned = returned.reshape(slots_n, share_width)
    picked = jnp.einsum("srk,sd->krd", select, returned, preferred_element_type=jnp.float32)
    codes = weight_codes.astype(jnp.float32)
    weight = codes / jnp.sum(codes, axis=1, keepdims=True)
    mixed = weight[:, 0:1] * picked[0] + weight[:, 1:2] * picked[1]
    return mixed.astype(jnp.bfloat16)


def body(tokens, expert_ids, weight_codes, up_weight, down_weight):
    rows = tokens.shape[0]
    capacity = 4 * rows // lax.axis_size("expert")
    whole = capacity >= rows and lax.axis_size("expert") == lax.axis_size("tensor") == 4
    plan = whole_blocks if whole else slotted
    return plan(tokens, expert_ids, weight_codes, up_weight[0], down_weight[0], capacity)


def solution(mesh):
    return jax.shard_map(
        body,
        mesh=mesh,
        in_specs=(
            P(("group", "expert"), "tensor"),
            P(("group", "expert"), None),
            P(("group", "expert"), None),
            P("expert", None, "tensor"),
            P("expert", "tensor", None),
        ),
        out_specs=P(("group", "expert"), "tensor"),
        check_vma=False,
    )
```

```python
import functools

import jax
import jax.numpy as jnp
from jax import lax
from jax.experimental import pallas as pl
from jax.experimental.pallas import tpu as pltpu
from jax.sharding import PartitionSpec as P


MIB = 1 << 20
HBM = pl.BlockSpec(memory_space=pltpu.HBM)
VMEM = pl.BlockSpec(memory_space=pltpu.VMEM)


def kept_weights(ids, codes, experts_n, capacity):
    rows = ids.shape[1]
    experts = lax.broadcasted_iota(jnp.int32, (experts_n, rows), 0)
    first = ids[0:1, :] == experts
    second = ids[1:2, :] == experts
    counts = first.astype(jnp.float32) + second.astype(jnp.float32)
    earlier = lax.broadcasted_iota(jnp.int32, (rows, rows), 0) < lax.broadcasted_iota(
        jnp.int32, (rows, rows), 1
    )
    before = jnp.dot(
        counts.astype(jnp.bfloat16),
        earlier.astype(jnp.float32).astype(jnp.bfloat16),
        preferred_element_type=jnp.float32,
    )
    codes = codes.astype(jnp.float32)
    weight = codes / (codes[0:1, :] + codes[1:2, :])
    keep_first = first & (before < capacity)
    keep_second = second & (before + first.astype(jnp.float32) < capacity)
    return jnp.where(keep_first, weight[0:1, :], 0.0) + jnp.where(
        keep_second, weight[1:2, :], 0.0
    )


def prepare_kernel(capacity, experts_n, ids, codes, up, down, columns, up_out, down_out, sems):
    copies = [
        pltpu.make_async_copy(up, up_out, sems.at[0]),
        pltpu.make_async_copy(down, down_out, sems.at[1]),
    ]
    for copy in copies:
        copy.start()
    me = lax.axis_index("expert")
    weight = kept_weights(ids[...], codes[...], experts_n, capacity)
    rows = weight.shape[1]
    index = lax.broadcasted_iota(jnp.int32, weight.shape, 0)
    diagonal = lax.broadcasted_iota(jnp.int32, (rows, rows), 0) == lax.broadcasted_iota(
        jnp.int32, (rows, rows), 1
    )
    for step in range(experts_n):
        mine = index == lax.rem(me + step, experts_n)
        row = jnp.sum(jnp.where(mine, weight, 0.0), axis=0, keepdims=True)
        column = jnp.sum(jnp.where(diagonal, row, 0.0), axis=1, keepdims=True)
        columns[step] = jnp.broadcast_to(column, columns.shape[1:])
    for copy in copies:
        copy.wait()


def local_call(
    kernel, out_shape, operands, others=(), in_specs=None, limit=4 * MIB, cost=0.5, **kwargs
):
    count = len(operands)

    name = getattr(kernel, "func", kernel).__name__

    def body_of(*refs):
        kernel(*refs[:count], *refs[count + len(others) :])

    return pl.pallas_call(
        body_of,
        name=name,
        out_shape=out_shape,
        in_specs=list(in_specs or [VMEM] * count) + [pl.BlockSpec(memory_space=pl.ANY)] * len(others),
        out_specs=jax.tree.map(lambda _: VMEM, out_shape),
        compiler_params=pltpu.CompilerParams(vmem_limit_bytes=limit),
        cost_estimate=pl.CostEstimate(
            flops=int(cost * 1.15e9), bytes_accessed=0, transcendentals=0
        ),
        **kwargs,
    )(*operands, *others)


def after(array, other):
    anywhere = pl.BlockSpec(memory_space=pl.ANY)
    return pl.pallas_call(
        lambda *refs: None,
        out_shape=jax.ShapeDtypeStruct(array.shape, array.dtype),
        in_specs=[anywhere, anywhere],
        out_specs=anywhere,
        input_output_aliases={0: 0},
        compiler_params=pltpu.CompilerParams(vmem_limit_bytes=MIB),
    )(array, other)


def prepare(ids, codes, up_t, down, experts_n, capacity):
    rows = ids.shape[1]
    return local_call(
        functools.partial(prepare_kernel, capacity, experts_n),
        [
            pltpu.VMEM((experts_n, rows, 128), jnp.float32),
            pltpu.VMEM(up_t.shape, up_t.dtype),
            pltpu.VMEM(down.shape, down.dtype),
        ],
        (ids, codes, up_t, down),
        in_specs=[VMEM, VMEM, HBM, HBM],
        scratch_shapes=[pltpu.SemaphoreType.DMA((2,))],
        limit=50 * MIB,
        cost=4,
    )


def pack_kernel(*refs):
    packed = refs[-1]
    rows, width = refs[0].shape
    for index, ref in enumerate(refs[:-1]):
        at, column = index // 2 * rows, index % 2 * width
        packed[at : at + rows, column : column + width] = ref[...]


def pack(pairs, others, cost):
    rows, width = pairs[0][0].shape
    return local_call(
        pack_kernel,
        jax.ShapeDtypeStruct((len(pairs) * rows, 2 * width), pairs[0][0].dtype),
        [array for pair in pairs for array in pair],
        others,
        cost=cost,
    )


def expert_kernel(count, *refs):
    pieces, (up_t, down, keep, send, features, out) = refs[:count], refs[count:]
    width = send.shape[1] // 2
    place = lax.axis_index("tensor")

    def columns(bits):
        return pl.ds(pl.multiple_of((place ^ bits) * width, width), width)

    order = [0, 2, 1, 3]
    for piece in pieces:
        for at in range(0, piece.shape[1], width):
            features[:, columns(order.pop(0))] = piece[:, at : at + width]
    lifted = lax.dot_general(
        features[...], up_t[...], (((1,), (1,)), ((), ())), preferred_element_type=jnp.float32
    )
    hidden = (lifted / (1.0 + jnp.exp(-lifted))).astype(jnp.bfloat16)
    out[...] = jnp.dot(hidden, down[...], preferred_element_type=jnp.float32)
    keep[:, :width] = out[:, columns(0)]
    keep[:, width:] = out[:, columns(2)]
    send[:, :width] = out[:, columns(1)].astype(jnp.bfloat16)
    send[:, width:] = out[:, columns(3)].astype(jnp.bfloat16)


def expert_rows(pieces, up_t, down, others, cost):
    rows, model = pieces[0].shape[0], up_t.shape[1]
    return local_call(
        functools.partial(expert_kernel, len(pieces)),
        [
            jax.ShapeDtypeStruct((rows, model // 2), jnp.float32),
            jax.ShapeDtypeStruct((rows, model // 2), jnp.bfloat16),
        ],
        (*pieces, up_t, down),
        others,
        limit=10 * MIB,
        scratch_shapes=[
            pltpu.VMEM((rows, model), jnp.bfloat16),
            pltpu.VMEM((rows, model), jnp.float32),
        ],
        cost=cost,
    )


def core_sum_kernel(keep, got, own, *sends):
    width = own.shape[1]
    own[...] = keep[:, :width] + got[:, :width].astype(jnp.float32)
    for index, send in enumerate(sends):
        rows = slice(index * send.shape[0], (index + 1) * send.shape[0])
        send[...] = (keep[rows, width:] + got[rows, width:].astype(jnp.float32)).astype(send.dtype)


def core_sum(keep, got, count, others, cost):
    rows, width = keep.shape[0], keep.shape[1] // 2
    return local_call(
        core_sum_kernel,
        [jax.ShapeDtypeStruct((rows, width), jnp.float32)]
        + [jax.ShapeDtypeStruct((rows // count, width), jnp.bfloat16)] * count,
        (keep, got),
        others,
        cost=cost,
    )


def chip_sum_kernel(index, own, got, part):
    rows = slice(index * got.shape[0], (index + 1) * got.shape[0])
    part[...] = (own[rows, :] + got[...].astype(jnp.float32)).astype(part.dtype)


def chip_sum(own, got, index, others, cost):
    return local_call(
        functools.partial(chip_sum_kernel, index),
        jax.ShapeDtypeStruct(got.shape, jnp.bfloat16),
        (own, got),
        others,
        cost=cost,
    )


def weigh_kernel(steps, counts, columns, *refs):
    refs, out = list(refs[:-1]), refs[-1]
    for at in range(0, out.shape[1], 128):
        here = slice(at, at + 128)
        left = list(refs)
        total = left.pop(0)[:, here] if len(left) > sum(counts) else None
        for step, count in zip(steps, counts):
            rows = sum(left.pop(0)[:, here].astype(jnp.float32) for _ in range(count))
            rows = columns[step] * rows
            total = rows if total is None else total + rows
        out[:, here] = total.astype(out.dtype)


def weigh(columns, totals, steps, terms, dtype, cost):
    arrays = [*totals, *[array for term in terms for array in term]]
    return local_call(
        functools.partial(weigh_kernel, steps, [len(term) for term in terms]),
        jax.ShapeDtypeStruct(arrays[-1].shape, dtype),
        (columns, *arrays),
        cost=cost,
    )


def swap(array, bit):
    return lax.ppermute(array, "tensor", [(i, i ^ bit) for i in range(4)])


def whole_blocks(tokens, expert_ids, weight_codes, up_local, down_local, capacity):
    experts_n = lax.axis_size("expert")

    def shift(array, by):
        return lax.ppermute(
            array, "expert", [(i, (i + by) % experts_n) for i in range(experts_n)]
        )

    columns, up_t, down = prepare(
        expert_ids.T, weight_codes.T, up_local.T, down_local, experts_n, capacity
    )
    blocks, others, chips, kept, sums, added, parts = {}, {}, {}, {}, {}, {}, {}

    def arrive(step, source, by, waits):
        blocks[step] = shift(source, by) if step else tokens
        for wait in waits:
            blocks[step] = after(blocks[step], wait)
        others[step] = swap(blocks[step], 2)

    def lay(steps, waits, cost=0.5):
        chips[steps] = pack([(blocks[step], others[step]) for step in steps], waits, cost)

    def run(steps, waits, cost):
        mine = [chips[steps]] if steps in chips else [blocks[steps[0]], others[steps[0]]]
        pieces = mine + [swap(piece, 1) for piece in mine]
        kept[steps] = expert_rows(pieces, up_t, down, waits, cost)

    def leave(steps, waits, cost=2):
        keep, send = kept[steps]
        own, *aways = core_sum(keep, swap(send, 1), len(steps), waits, cost)
        for index, step in enumerate(steps):
            sums[step] = own, swap(aways[index], 2), index

    def give(step, waits, cost=2):
        added[step] = chip_sum(*sums[step], waits, cost)
        parts[step] = shift(added[step], -step)

    arrive(0, tokens, 0, [])
    arrive(1, tokens, 1, [columns])
    lay((0,), [blocks[1]])
    chips[3,] = shift(chips[0,], -1)
    run((0,), [], .05)
    arrive(2, blocks[1], 1, [kept[0,][0]])
    others[1] = after(others[1], kept[0,][0])
    run((1,), [blocks[2]], .05)
    run((2,), [kept[1,][0]], .05)
    chips[3,] = after(chips[3,], kept[2,][0])
    leave((1,), [kept[2,][0]], 2)
    leave((2,), [sums[1][0]], 2)
    run((3,), [sums[2][0]], 4)
    give(1, [kept[3,][0]], 4)
    leave((3,), [added[1]], .05)
    give(2, [sums[3][0]], 4)
    give(3, [added[2]], 4)
    leave((0,), [added[3]], 2)
    total = weigh(columns, [], (1, 2), [[parts[1]], [parts[2]]], jnp.float32, 4)
    total = weigh(columns, [total], (0,), [sums[0][:2]], jnp.float32, 4)
    return weigh(columns, [total], (3,), [[parts[3]]], jnp.bfloat16, 0.5)


def slotted(tokens, expert_ids, weight_codes, up_local, down_local, capacity):
    rows, share_width = tokens.shape
    experts_n = lax.axis_size("expert")
    slots_n = experts_n * capacity
    flat_ids = expert_ids.reshape(rows * 2)
    onehot = (flat_ids[:, None] == jnp.arange(experts_n, dtype=jnp.int32)[None, :]).astype(
        jnp.int32
    )
    prior = jnp.cumsum(onehot, axis=0) - onehot
    slot = jnp.sum(prior * onehot, axis=1)
    target = jnp.where(slot < capacity, flat_ids * capacity + slot, -1)
    select = (jnp.arange(slots_n, dtype=jnp.int32)[:, None] == target[None, :]).astype(jnp.bfloat16)
    select = select.reshape(slots_n, rows, 2)
    gather_mat = jnp.sum(select, axis=2)
    sending = jnp.dot(gather_mat, tokens, preferred_element_type=jnp.float32).astype(jnp.bfloat16)
    sending = sending.reshape(experts_n, capacity, share_width)
    received = lax.all_to_all(sending, "expert", split_axis=0, concat_axis=0, tiled=True)
    received = received.reshape(slots_n, share_width)
    received = lax.all_gather(received, "tensor", axis=1, tiled=True)
    lifted = jnp.dot(received, up_local, preferred_element_type=jnp.float32)
    hidden = jax.nn.silu(lifted).astype(jnp.bfloat16)
    partial_out = jnp.dot(hidden, down_local, preferred_element_type=jnp.float32)
    total = lax.psum_scatter(
        partial_out.astype(jnp.bfloat16), "tensor", scatter_dimension=1, tiled=True
    )
    total = total.reshape(experts_n, capacity, share_width)
    returned = lax.all_to_all(total, "expert", split_axis=0, concat_axis=0, tiled=True)
    returned = returned.reshape(slots_n, share_width)
    picked = jnp.einsum("srk,sd->krd", select, returned, preferred_element_type=jnp.float32)
    codes = weight_codes.astype(jnp.float32)
    weight = codes / jnp.sum(codes, axis=1, keepdims=True)
    mixed = weight[:, 0:1] * picked[0] + weight[:, 1:2] * picked[1]
    return mixed.astype(jnp.bfloat16)


def body(tokens, expert_ids, weight_codes, up_weight, down_weight):
    rows = tokens.shape[0]
    capacity = 4 * rows // lax.axis_size("expert")
    whole = capacity >= rows and lax.axis_size("expert") == lax.axis_size("tensor") == 4
    plan = whole_blocks if whole else slotted
    return plan(tokens, expert_ids, weight_codes, up_weight[0], down_weight[0], capacity)


def solution(mesh):
    return jax.shard_map(
        body,
        mesh=mesh,
        in_specs=(
            P(("group", "expert"), "tensor"),
            P(("group", "expert"), None),
            P(("group", "expert"), None),
            P("expert", None, "tensor"),
            P("expert", "tensor", None),
        ),
        out_specs=P(("group", "expert"), "tensor"),
        check_vma=False,
    )
```
